128 devices in a mesh: tok: 4 (over x_lo, core), voc: 32 (over x_hi, z, y).
Axes of the slice: x: 4 (x_hi: 2, x_lo: 2; x = x_hi * 2 + x_lo), y: 4, z: 4, core: 2. Of those that a mesh axis runs over, the one named last changes fastest.
Arguments:
- hidden: bfloat16 [32768, 5120], P('tok', 'voc'), may hold values from -240 to 240
- head_weight: bfloat16 [98304, 5120], P(('tok', 'voc')), may hold values from -0.25 to 0.25
- tile_owners: int32 [8192, 2], P(('tok', 'voc')), may hold values from 0 to 127, all different within a row; in each aligned block of 64 rows (0 to 63, 64 to 127, ...) at most 2 rows name the same one
- cand_pos: int32 [32768, 64], P(('tok', 'voc')), may hold values from 0 to 1535, as said below
- teacher_logp: float32 [32768, 64], P(('tok', 'voc')), may hold values from -16 to -2
Outputs:
- token_loss: float32 [32768], P(('tok', 'voc'))
- grad_hidden: bfloat16 [32768, 5120], P(('tok', 'voc'))
- grad_head: bfloat16 [98304, 5120], P(('tok', 'voc'))
The draws below stay inside these ranges and needn't reach their ends.
Inputs may be any that keep to these rules, and one draw needn't show every extreme that they name: `tile_owners`: the 2 panels of a tile are distinct. Among the tiles of one device no panel is named more than 2 times, a bound that some block reaches. `cand_pos`: the 64 entries of a row are distinct.
All inputs are finite; a program needn't handle non-finite values.
Results may differ from the reference program's by a relative error of at most 0.013.
Values may be sent and summed in bfloat16 or wider, within the bound.
No kernel may reach another device: no remote copies, remote signals or barrier semaphores. Data moves between devices by JAX's collectives and lax.ppermute only.
A program may use at most 192 MiB of HBM per device.

```python
import math
import jax
import jax.numpy as jnp
import numpy as np
from jax import lax

D = 5120
VOC_DEV = 768
TOK = 256
TILE = 4
NG = 2
K = 64
VOCAB = 98304
TOKENS = 32768
TILES = 8192
CAP = 2
N_TOK = 4
N_VOC = 32


def draw_hidden(key, part):
    key = jax.random.fold_in(key, 11)
    values = jnp.clip(jax.random.normal(key, (TOKENS, D), jnp.float32), -6.0, 6.0)
    return values.astype(jnp.bfloat16)


def draw_cand_pos(key, part):
    key = jax.random.fold_in(key, 23)
    span_size = NG * VOC_DEV
    scores = jax.random.randint(key, (TOKENS, span_size), 0, 1 << 20, jnp.int32) * span_size
    scores = scores + jnp.arange(span_size, dtype=jnp.int32)[None, :]
    chosen_values, chosen = lax.top_k(scores, K)
    return chosen.astype(jnp.int32)


def block_levels(rng, dims, cuts, least, largest):
    loudness = 1.0
    for axis_at, blocks in cuts:
        draws = jax.random.uniform(jax.random.fold_in(jax.random.fold_in(rng, 6), axis_at), (blocks,), jnp.float32, least / len(cuts), largest / len(cuts))
        loudness = loudness * jnp.repeat(jnp.exp(draws), dims[axis_at] // blocks).reshape((-1,) + (1,) * (len(dims) - 1 - axis_at))
    return loudness


def deal_out(own_key, own, number, rows, number_of, top, limit, skew):
    order = jax.random.permutation(own_key, number_of)
    crowded, ordinary = load_shares(number_of, rows * top, limit, skew, True), load_shares(number_of, rows * top, limit, skew, False)
    places = jnp.arange(number_of)

    def named(sizes, offset_by):
        used = int((sizes > 0).sum())
        fixed = max(1, used // 4)
        shifted = fixed + (places - fixed + offset_by * (used - fixed)) % max(1, number_of - fixed)
        return jnp.zeros((number_of,), jnp.int32).at[order[jnp.where(places < fixed, places, shifted)]].set(jnp.asarray(sizes, jnp.int32))

    sizes = jnp.where(number % 4 == 0, named(crowded, number // 4), named(ordinary, number - number // 4 - 1))
    mixed = jax.random.permutation(jax.random.fold_in(own, 3), number_of)
    giver, receiver = mixed[0:number_of // 2 * 2:2], mixed[1:number_of // 2 * 2:2]
    slack = jnp.minimum(sizes[giver] - 1, limit - sizes[receiver]) // 2
    slack = jnp.where((giver == order[0]) | (receiver == order[0]) | (sizes[receiver] == 0), 0, jnp.maximum(slack, 0))
    shifted = jax.random.randint(jax.random.fold_in(own, 4), (number_of // 2,), 0, 1 << 20) % (slack + 1)
    sizes = sizes.at[giver].add(-shifted).at[receiver].add(shifted)
    labels = jnp.searchsorted(jnp.cumsum(sizes), jnp.arange(rows * top), side="right").astype(jnp.int32)
    table = labels.reshape(top, rows).T
    table = table[jax.random.permutation(jax.random.fold_in(own, 1), rows)]
    offset_by = jax.random.randint(jax.random.fold_in(own, 2), (rows, 1), 0, top)
    return jnp.take_along_axis(table, (jnp.arange(top)[None, :] + offset_by) % top, axis=1)


def load_shares(amount, total, bound, skew, full):
    portions = [(1 << 20) // math.isqrt(standing ** skew) + 1 for standing in range(1, amount + 1)]
    largest = bound if full else min(bound, max(-(-total // amount), total * portions[0] // sum(portions)))
    least = 1 if total - largest >= amount - 1 else 0
    holding, surplus = [largest] + [least] * (amount - 1), total - largest - least * (amount - 1)
    while surplus > 0:
        candidates = [i for i in range(1, amount) if holding[i] < largest] or [i for i in range(1, amount) if holding[i] < bound]
        whole, left = sum([portions[i] for i in candidates]), surplus
        for i in candidates:
            more = min(bound - holding[i], max(1, left * portions[i] // whole), surplus)
            holding[i] = holding[i] + more
            surplus = surplus - more
    return np.array(holding)


def normal_values(stream_key, extent, spread, reach, split=(), kind=jnp.bfloat16):
    entries = spread * jax.random.normal(stream_key, extent, jnp.float32)
    if split:
        entries = entries * block_levels(stream_key, extent, split, -0.22, 0.18)
    return jnp.clip(entries, -reach, reach).astype(kind)


def setup_inputs(seed: int = 0) -> dict:
    key_list = jax.random.split(jax.random.key(seed), 6)
    hidden = draw_hidden(jax.random.fold_in(key_list[5], 71), 0)
    head_weight = normal_values(key_list[1], (VOCAB, D), 0.042, 0.25, ((0, 128),))
    tile_owners_keys = jax.random.split(jax.random.fold_in(key_list[2], 1), TILES // (TOK // TILE))
    tile_owners_turns = jax.random.permutation(jax.random.fold_in(key_list[2], 3), TILES // (TOK // TILE))
    tile_owners = jax.vmap(lambda own, number: deal_out(jax.random.fold_in(key_list[2], 2), own, number, TOK // TILE, N_TOK * N_VOC, NG, CAP, 2))(tile_owners_keys, tile_owners_turns).reshape((TILES, NG))
    cand_pos = draw_cand_pos(jax.random.fold_in(key_list[5], 71), 0)
    teacher_logp = jnp.clip(-16.0 + 14.0 * jax.random.uniform(key_list[4], (TOKENS, K), jnp.float32) ** block_levels(key_list[4], (TOKENS, K), ((0, 128),), -0.2, 0.2), -16.0, -2.0)
    return {"hidden": hidden, "head_weight": head_weight, "tile_owners": tile_owners, "cand_pos": cand_pos, "teacher_logp": teacher_logp}


loss_weight = 16.0


def reference(hidden, head_weight, tile_owners, cand_pos, teacher_logp):
    group_count = TOKENS // TOK
    tiles_group = TOK // TILE
    owner_table = tile_owners.reshape(group_count, tiles_group, 1, NG)
    positions = cand_pos.reshape(group_count, tiles_group, TILE, K)
    group_of = positions // VOC_DEV
    owner_of = jnp.zeros(positions.shape, jnp.int32)
    for slot_group in range(NG):
        owner_of = owner_of + jnp.where(group_of == slot_group, owner_table[..., slot_group:slot_group + 1], 0)
    vocab_ids = (owner_of * VOC_DEV + positions % VOC_DEV).astype(jnp.int32).reshape(group_count, TOK, K)
    group_of = group_of.reshape(group_count, TOK, K)
    row_blocks = hidden.reshape(group_count, TOK, D)
    teacher_blocks = teacher_logp.reshape(group_count, TOK, K)

    def accumulate(running, pieces):
        tok_rows, ident_rows, group_rows, teacher_rows = pieces
        panels_wide = head_weight[ident_rows].astype(jnp.float32)
        rows_wide = tok_rows.astype(jnp.float32)
        cand_logit = jnp.einsum("td,tkd->tk", rows_wide, panels_wide)
        row_max = jnp.max(cand_logit, axis=1, keepdims=True)
        log_total = row_max + jnp.log(jnp.sum(jnp.exp(cand_logit - row_max), axis=1, keepdims=True))
        target = jnp.exp(teacher_rows)
        teacher_mass = jnp.sum(target, axis=1, keepdims=True)
        token_loss = jnp.sum(target * (teacher_rows - cand_logit + log_total), axis=1)
        weights = (loss_weight * (teacher_mass * jnp.exp(cand_logit - log_total) - target)).astype(jnp.bfloat16)
        weights_wide = weights.astype(jnp.float32)
        grad_rows = jnp.zeros(rows_wide.shape, jnp.float32)
        for slot_group in range(NG):
            partial_value = jnp.einsum("tk,tkd->td", jnp.where(group_rows == slot_group, weights_wide, 0.0), panels_wide)
            rounded = lax.optimization_barrier(partial_value.astype(jnp.bfloat16))
            grad_rows = grad_rows + rounded.astype(jnp.float32)
        updates = weights_wide[:, :, None] * rows_wide[:, None, :]
        running = running.at[ident_rows.reshape(-1)].add(updates.reshape(-1, D))
        return running, (token_loss, grad_rows.astype(jnp.bfloat16))

    running, outputs = lax.scan(accumulate, jnp.zeros((VOCAB, D), jnp.float32), (row_blocks, vocab_ids, group_of, teacher_blocks))
    token_loss, grad_hidden = outputs
    return token_loss.reshape(TOKENS), grad_hidden.reshape(TOKENS, D), running.astype(jnp.bfloat16)
```

```python
import functools

import jax
import jax.numpy as jnp
from jax import lax
from jax.experimental import pallas as pl
from jax.experimental.pallas import tpu as pltpu
from jax.sharding import PartitionSpec as P

loss_weight = 16.0
nothing = -1e30
f32, bf16, i32 = jnp.float32, jnp.bfloat16, jnp.int32
HIGHEST = lax.Precision.HIGHEST


def settings(mib=32):
    return pltpu.CompilerParams(vmem_limit_bytes=mib * 1024 * 1024)


def by_rows(a, b, precision=None):
    return lax.dot_general(
        a, b, (((1,), (1,)), ((), ())), preferred_element_type=f32, precision=precision
    )


def plain(a, b, precision=None):
    return lax.dot_general(
        a, b, (((1,), (0,)), ((), ())), preferred_element_type=f32, precision=precision
    )


def iota(shape, dim):
    return lax.broadcasted_iota(i32, shape, dim)


def rows_of(codes, tiles, per_tile):
    entries = codes.shape[1]
    wide = entries * per_tile
    spread = (iota((entries, wide), 0) == iota((entries, wide), 1) // per_tile).astype(bf16)
    expanded = plain(codes.astype(bf16), spread).astype(i32)
    return expanded * per_tile + iota(expanded.shape, 1) % per_tile


def announce_kernel(panel, per_tile, owner_ref, cand_ref, teacher_ref, out_ref, rows_ref):
    entries = owner_ref.shape[1]
    tiles = entries // 2
    tokens = tiles * per_tile
    owners = jnp.broadcast_to(owner_ref[...].astype(f32), (entries, entries))
    earlier = iota((entries, entries), 0) % tiles < iota((entries, entries), 1) % tiles
    same = (owners == owners.T) & earlier
    rank = jnp.sum(jnp.where(same, 1.0, 0.0), axis=0, keepdims=True)
    code = owner_ref[...].astype(f32) * 2.0 + rank
    rows = rows_of(jnp.broadcast_to(code, (8, entries)), tiles, per_tile)
    rows_ref[...] = rows
    cand = cand_ref[...]
    teacher = teacher_ref[...]
    columns = (
        jnp.where(cand < panel, cand + 1, 0).astype(f32),
        jnp.where(cand >= panel, cand - panel + 1, 0).astype(f32),
    )
    slots = out_ref.shape[0]
    block = 32
    for at in range(0, slots, block):
        row = iota((block * 8, tokens), 0) + at * 8
        told = jnp.zeros((block * 8, 2 * cand.shape[0]), f32)
        for group in range(2):
            hot = jnp.where(row == rows[0:1, group * tokens : (group + 1) * tokens], 1.0, 0.0)
            told = told + by_rows(
                hot, jnp.concatenate([columns[group], teacher], axis=0), HIGHEST
            )
        width = told.shape[1]
        out_ref[at : at + block, :, 0:width] = told.reshape(block, 8, width)
        out_ref[at : at + block, :, width : width + entries] = jnp.broadcast_to(
            code.reshape(1, 1, entries), (block, 8, entries)
        )


def announce(owner_row, cand, teacher, panel, per_tile, owners):
    entries = owner_row.shape[1]
    return pl.pallas_call(
        functools.partial(announce_kernel, panel, per_tile),
        out_shape=(
            jax.ShapeDtypeStruct((owners, 8, 2 * cand.shape[0] + entries), f32),
            jax.ShapeDtypeStruct((8, entries * per_tile), i32),
        ),
        compiler_params=settings(),
        name="announce",
    )(owner_row, cand, teacher)


def route_kernel(blocks, per_tile, tok_ref, codes_ref, hidden_ref, out_ref, rows_ref, held_ref):
    step = pl.program_id(0)
    steps = blocks // 2
    width = hidden_ref.shape[0]
    tokens = hidden_ref.shape[1] // 2
    owners = held_ref.shape[0]

    @pl.when(step == 0)
    def _():
        codes = codes_ref[pl.ds(pl.multiple_of(tok_ref[0] * blocks, blocks), blocks), :]
        rows_ref[...] = rows_of(codes, tokens // per_tile, per_tile)

    @pl.when(step < steps)
    def _():
        chunk = owners // 2
        for at in range(0, owners, chunk):
            row = iota((chunk * 8, tokens), 0) + at * 8
            parts = []
            for which in range(2):
                first = rows_ref[pl.ds(step * 2 + which, 1), 0:tokens]
                second = rows_ref[pl.ds(step * 2 + which, 1), tokens : 2 * tokens]
                hot = jnp.where((row == first) | (row == second), 1.0, 0.0).astype(bf16)
                part = by_rows(hot, hidden_ref[:, which * tokens : (which + 1) * tokens])
                parts.append(part.reshape(chunk, 8, width))
            held_ref[at : at + chunk, pl.ds(pl.multiple_of(step * 16, 16), 16), :] = (
                jnp.concatenate(parts, axis=1).astype(bf16)
            )

    @pl.when(step >= steps)
    def _():
        count = out_ref.shape[0]
        eye = (iota((width, width), 0) == iota((width, width), 1)).astype(bf16)
        for k in range(count):
            out_ref[k] = by_rows(eye, held_ref[(step - steps) * count + k]).astype(bf16)


def route(tok, codes, hidden, per_tile, blocks):
    width, total = hidden.shape
    owners = codes.shape[0]
    steps = blocks // 2
    tokens = total // blocks
    turn = 8
    return pl.pallas_call(
        functools.partial(route_kernel, blocks, per_tile),
        grid_spec=pltpu.PrefetchScalarGridSpec(
            num_scalar_prefetch=1,
            grid=(steps + owners // turn,),
            in_specs=[
                pl.BlockSpec(codes.shape, lambda s, t: (0, 0)),
                pl.BlockSpec((width, 2 * tokens), lambda s, t: (0, jnp.minimum(s, steps - 1))),
            ],
            out_specs=pl.BlockSpec(
                (turn, width, blocks * 8), lambda s, t: (jnp.maximum(s - steps, 0), 0, 0)
            ),
            scratch_shapes=[
                pltpu.VMEM((blocks, codes.shape[1] * per_tile), i32),
                pltpu.VMEM((owners, blocks * 8, width), bf16),
            ],
        ),
        out_shape=jax.ShapeDtypeStruct((owners, width, blocks * 8), bf16),
        compiler_params=settings(40),
        name="route",
    )(tok, codes, hidden)


def place_kernel(per_tile, owner_ref, told_ref, dense_ref, facts_ref):
    sources, _, width = told_ref.shape
    lanes = sources * 8
    turned = told_ref[...].reshape(lanes, width).T
    picks = width // 4
    columns = turned[0:picks].astype(i32) - 1
    teacher = turned[picks : 2 * picks]
    target = jnp.exp(teacher)
    panel = dense_ref.shape[0]
    chunk = 128
    place = iota((chunk, lanes), 0)
    for at in range(0, panel, chunk):
        dense = jnp.zeros((chunk, lanes), f32)
        for k in range(picks):
            dense = jnp.where(place == columns[k : k + 1] - at, target[k : k + 1], dense)
        dense_ref[at : at + chunk, :] = dense
    codes = turned[2 * picks :]
    half = codes.shape[0] // 2
    other = jnp.concatenate([codes[half:], codes[:half]], axis=0)
    slot = (iota((1, lanes), 1) // per_tile) % 2
    mine = (owner_ref[0] * 2 + slot).astype(f32)
    partner = jnp.sum(jnp.where(codes == mine, other + 1.0, 0.0), axis=0, keepdims=True)
    mass = jnp.sum(target, axis=0, keepdims=True)
    entropy = jnp.sum(jnp.where(columns >= 0, target * teacher, 0.0), axis=0, keepdims=True)
    facts_ref[...] = jnp.concatenate(
        [partner, mass, entropy, jnp.zeros((5, lanes), f32)], axis=0
    )


def place(owner, told, panel, per_tile):
    sources, _, width = told.shape
    rows = sources * 8
    block = 16
    return pl.pallas_call(
        functools.partial(place_kernel, per_tile),
        grid_spec=pltpu.PrefetchScalarGridSpec(
            num_scalar_prefetch=1,
            grid=(sources // block,),
            in_specs=[pl.BlockSpec((block, 8, width), lambda s, o: (s, 0, 0))],
            out_specs=[
                pl.BlockSpec((panel, block * 8), lambda s, o: (0, s)),
                pl.BlockSpec((8, block * 8), lambda s, o: (0, s)),
            ],
        ),
        out_shape=(
            jax.ShapeDtypeStruct((panel, rows), f32),
            jax.ShapeDtypeStruct((8, rows), f32),
        ),
        compiler_params=settings(),
        cost_estimate=pl.CostEstimate(
            flops=2 * 64 * panel * rows, bytes_accessed=8 * panel * rows, transcendentals=64 * rows
        ),
        name="place",
    )(owner, told)


def score_kernel(head_ref, rows_ref, dense_ref, facts_ref, part_ref, own_ref, told_ref, total_ref):
    step = pl.program_id(0)
    groups, _, lanes = rows_ref.shape

    @pl.when(step == 0)
    def _():
        for t in range(groups):
            total_ref[:, t * lanes : (t + 1) * lanes] = plain(head_ref[...], rows_ref[t])

    @pl.when(step > 0)
    def _():
        for t in range(groups):
            total_ref[:, t * lanes : (t + 1) * lanes] += plain(head_ref[...], rows_ref[t])

    @pl.when(step == pl.num_programs(0) - 1)
    def _():
        count = total_ref.shape[1]
        chunk = 128
        logs, largest, shares = [], [], []
        for at in range(0, count, chunk):
            here = slice(at, at + chunk)
            dense = dense_ref[:, here]
            score = total_ref[:, here]
            named = dense > 0.0
            most = jnp.max(jnp.where(named, score, nothing), axis=0, keepdims=True)
            part = jnp.where(named, jnp.exp(score - most), 0.0)
            part_ref[:, here] = part
            whole = jnp.sum(part, axis=0, keepdims=True)
            log = jnp.where(whole > 0.0, most + jnp.log(jnp.maximum(whole, 1.0)), nothing)
            shares.append(
                facts_ref[2:3, here] - jnp.sum(dense * score, axis=0, keepdims=True)
            )
            logs.append(log)
            largest.append(most)
        logs = jnp.concatenate(logs, axis=1)
        largest = jnp.concatenate(largest, axis=1)
        shares = jnp.concatenate(shares, axis=1)
        own_ref[...] = jnp.concatenate([largest, logs, jnp.zeros((6, count), f32)], axis=0)
        owners = told_ref.shape[0]
        told_ref[:, 0:count] = jnp.broadcast_to(logs, (owners, count))
        home = iota((owners, count), 1) // 8 == iota((owners, count), 0)
        which = (iota((count, 128), 0) % 8 == iota((count, 128), 1)).astype(f32)
        told_ref[:, count : count + 128] = plain(
            jnp.where(home, jnp.broadcast_to(shares, (owners, count)), 0.0), which, HIGHEST
        )


def score(head, rows, dense, facts, owners):
    panel, width = head.shape
    groups, _, lanes = rows.shape
    count = groups * lanes
    block = 640
    whole = lambda s: (0, 0)
    return pl.pallas_call(
        score_kernel,
        grid=(width // block,),
        in_specs=[
            pl.BlockSpec((panel, block), lambda s: (0, s)),
            pl.BlockSpec((groups, block, lanes), lambda s: (0, s, 0)),
            pl.BlockSpec((panel, count), whole),
            pl.BlockSpec((8, count), whole),
        ],
        out_specs=[
            pl.BlockSpec((panel, count), whole),
            pl.BlockSpec((8, count), whole),
            pl.BlockSpec((owners, count + 128), whole),
        ],
        out_shape=(
            jax.ShapeDtypeStruct((panel, count), f32),
            jax.ShapeDtypeStruct((8, count), f32),
            jax.ShapeDtypeStruct((owners, count + 128), f32),
        ),
        scratch_shapes=[pltpu.VMEM((panel, count), f32)],
        compiler_params=settings(48),
        name="score",
    )(head, rows, dense, facts)


def log_sum(a, b):
    most = jnp.maximum(a, b)
    return most + jnp.log(jnp.exp(a - most) + jnp.exp(b - most))


def part_kernel(
    per_tile, logs_ref, facts_ref, own_ref, part_ref, dense_ref, head_ref, out_ref, turned_ref, weight_ref
):
    step = pl.program_id(0)

    @pl.when(step == 0)
    def _():
        panel, count = part_ref.shape
        owners = logs_ref.shape[0]
        chunk = 128
        for at in range(0, count, chunk):
            here = slice(at, at + chunk)
            logs = logs_ref[:, here]
            partner = facts_ref[0:1, here].astype(i32) - 1
            slot = (iota((1, chunk), 1) // per_tile) % 2
            across = jnp.where(
                slot == 0, pltpu.roll(logs, chunk - per_tile, 1), pltpu.roll(logs, per_tile, 1)
            )
            picked = jnp.where(
                iota((owners, chunk), 0) == partner // 2,
                jnp.where(partner % 2 == slot, logs, across),
                0.0,
            )
            other = jnp.sum(picked, axis=0, keepdims=True)
            total = log_sum(own_ref[1:2, here], other)
            scale = loss_weight * facts_ref[1:2, here] * jnp.exp(own_ref[0:1, here] - total)
            weight = part_ref[:, here] * scale - loss_weight * dense_ref[:, here]
            turned_ref[:, here] = weight.astype(bf16)
            weight_ref[here, :] = weight.T.astype(bf16)

    out_ref[...] = plain(weight_ref[...], head_ref[...]).astype(bf16)


def grad_parts(logs, facts, own, part, dense, head, per_tile):
    panel, width = head.shape
    count = part.shape[1]
    block = 512
    whole = lambda s: (0, 0)
    return pl.pallas_call(
        functools.partial(part_kernel, per_tile),
        grid=(width // block,),
        in_specs=[
            pl.BlockSpec(logs.shape, whole),
            pl.BlockSpec((8, count), whole),
            pl.BlockSpec((8, count), whole),
            pl.BlockSpec((panel, count), whole),
            pl.BlockSpec((panel, count), whole),
            pl.BlockSpec((panel, block), lambda s: (0, s)),
        ],
        out_specs=[
            pl.BlockSpec((count, block), lambda s: (0, s)),
            pl.BlockSpec((panel, count), whole),
        ],
        out_shape=(
            jax.ShapeDtypeStruct((count, width), bf16),
            jax.ShapeDtypeStruct((panel, count), bf16),
        ),
        scratch_shapes=[pltpu.VMEM((count, panel), bf16)],
        compiler_params=settings(48),
        name="grad_parts",
    )(logs, facts, own, part, dense, head)


def head_kernel(weight_ref, rows_ref, out_ref):
    groups, _, lanes = rows_ref.shape
    total = by_rows(weight_ref[:, 0:lanes], rows_ref[0])
    for t in range(1, groups):
        total = total + by_rows(weight_ref[:, t * lanes : (t + 1) * lanes], rows_ref[t])
    out_ref[...] = total.astype(bf16)


def grad_of_head(weight, rows):
    panel, count = weight.shape
    groups, width, lanes = rows.shape
    block = 512
    return pl.pallas_call(
        head_kernel,
        grid=(width // block,),
        in_specs=[
            pl.BlockSpec((panel, count), lambda s: (0, 0)),
            pl.BlockSpec((groups, block, lanes), lambda s: (0, s, 0)),
        ],
        out_specs=pl.BlockSpec((panel, block), lambda s: (0, s)),
        out_shape=jax.ShapeDtypeStruct((panel, width), bf16),
        compiler_params=settings(),
        cost_estimate=pl.CostEstimate(
            flops=2 * panel * count * width,
            bytes_accessed=2 * (panel + count) * width,
            transcendentals=0,
        ),
        name="grad_of_head",
    )(weight, rows)


def loss_kernel(me_ref, logs_ref, rows_ref, teacher_ref, loss_ref, table_ref):
    owners = logs_ref.shape[0]
    tokens = teacher_ref.shape[1]
    count = table_ref.shape[1]
    mine = iota((count, 128), 0) == me_ref[0] * 8 + iota((count, 128), 1)
    mine = jnp.where(mine & (iota((count, 128), 1) < 8), 1.0, 0.0)
    logs = plain(logs_ref[:, 0:count], mine, HIGHEST).T
    shares = logs_ref[:, count : count + 128].T
    found = []
    total = jnp.zeros((1, tokens), f32)
    for group in range(2):
        row = rows_ref[0:1, group * tokens : (group + 1) * tokens]
        owner = jnp.where(iota((owners, tokens), 0) == row // 8, 1.0, 0.0)
        slot = iota((128, tokens), 0) == row % 8
        for table, kept in ((logs, True), (shares, False)):
            got = jnp.where(slot, plain(table, owner, HIGHEST), 0.0)
            got = jnp.sum(got, axis=0, keepdims=True)
            if kept:
                found.append(got)
            else:
                total = total + got
    teacher = teacher_ref[...]
    mass = jnp.sum(jnp.exp(teacher), axis=0, keepdims=True)
    loss_ref[...] = total + mass * log_sum(found[0], found[1])
    first, second = rows_ref[0:1, 0:tokens], rows_ref[0:1, tokens : 2 * tokens]
    for at in range(0, count, 128):
        row = iota((128, tokens), 0) + at
        hot = jnp.where((row == first) | (row == second), 1.0, 0.0)
        table_ref[:, at : at + 128] = hot.T.astype(bf16)


def losses(me, logs, rows, teacher, count):
    tokens = teacher.shape[1]
    return pl.pallas_call(
        loss_kernel,
        in_specs=[pl.BlockSpec(memory_space=pltpu.SMEM)] + [pl.BlockSpec(memory_space=pltpu.VMEM)] * 3,
        out_shape=(
            jax.ShapeDtypeStruct((1, tokens), f32),
            jax.ShapeDtypeStruct((tokens, count), bf16),
        ),
        compiler_params=settings(),
        cost_estimate=pl.CostEstimate(
            flops=12 * 2 * count * tokens * 128, bytes_accessed=4 * count * tokens, transcendentals=0
        ),
        name="losses",
    )(me, logs, rows, teacher)


def combine_kernel(table_ref, parts_ref, out_ref):
    out_ref[...] = plain(table_ref[...], parts_ref[...]).astype(bf16)


def combine(table, parts):
    tokens, count = table.shape
    width = parts.shape[1]
    block = 512
    return pl.pallas_call(
        combine_kernel,
        grid=(width // block,),
        in_specs=[
            pl.BlockSpec((tokens, count), lambda s: (0, 0)),
            pl.BlockSpec((count, block), lambda s: (0, s)),
        ],
        out_specs=pl.BlockSpec((tokens, block), lambda s: (0, s)),
        out_shape=jax.ShapeDtypeStruct((tokens, width), bf16),
        compiler_params=settings(),
        name="combine",
    )(table, parts)


def exchange(values):
    return lax.all_to_all(values, ("tok", "voc"), split_axis=0, concat_axis=0, tiled=True)


def body(hidden, head_weight, tile_owners, cand_pos, teacher_logp):
    panel, width = head_weight.shape
    tiles = tile_owners.shape[0]
    tokens = cand_pos.shape[0]
    per_tile = tokens // tiles
    tok_size, blocks = lax.axis_size("tok"), lax.axis_size("voc")
    owners = tok_size * blocks
    count = owners * 8
    tok = lax.axis_index("tok")
    me = (tok * blocks + lax.axis_index("voc")).astype(i32).reshape(1)
    teacher = teacher_logp.T
    told, home_rows = announce(
        tile_owners.T.reshape(1, 2 * tiles), cand_pos.T, teacher, panel, per_tile, owners
    )
    told = exchange(told)
    codes = told[:, 0, 2 * cand_pos.shape[1] :]
    sent = route(tok.astype(i32).reshape(1), codes, hidden.T, per_tile, blocks)
    rows = exchange(sent).reshape(tok_size, width, blocks * 8)
    dense, facts = place(me, told, panel, per_tile)
    part, own, logs = score(head_weight, rows, dense, facts, owners)
    logs = exchange(logs.reshape(owners, 1, count + 128)).reshape(owners, count + 128)
    parts, weight = grad_parts(logs, facts, own, part, dense, head_weight, per_tile)
    home_parts = exchange(parts.reshape(owners, 8, width)).reshape(count, width)
    grad_head = grad_of_head(weight, rows)
    loss, table = losses(me, logs, home_rows, teacher, count)
    grad_hidden = combine(table, home_parts)
    return (loss.reshape(tokens), grad_hidden, grad_head)


def solution(mesh):
    placed = (
        P("tok", "voc"),
        P(("tok", "voc"), None),
        P(("tok", "voc"), None),
        P(("tok", "voc"), None),
        P(("tok", "voc"), None),
    )
    return jax.shard_map(
        body,
        mesh=mesh,
        in_specs=placed,
        out_specs=(P(("tok", "voc")), P(("tok", "voc"), None), P(("tok", "voc"), None)),
        check_vma=False,
    )
```

```python
import functools

import jax
import jax.numpy as jnp
from jax import lax
from jax.experimental import pallas as pl
from jax.experimental.pallas import tpu as pltpu
from jax.sharding import PartitionSpec as P

loss_weight = 16.0
nothing = -1e30
f32, bf16, i32 = jnp.float32, jnp.bfloat16, jnp.int32
HIGHEST = lax.Precision.HIGHEST


near, far = pl.BlockSpec(memory_space=pltpu.VMEM), pl.BlockSpec(memory_space=pl.ANY)


def settings(mib=32):
    return pltpu.CompilerParams(vmem_limit_bytes=mib * 1024 * 1024)


def by_rows(a, b, precision=None):
    return lax.dot_general(
        a, b, (((1,), (1,)), ((), ())), preferred_element_type=f32, precision=precision
    )


def plain(a, b, precision=None):
    return lax.dot_general(
        a, b, (((1,), (0,)), ((), ())), preferred_element_type=f32, precision=precision
    )


def iota(shape, dim):
    return lax.broadcasted_iota(i32, shape, dim)


def rows_of(codes, per_tile):
    entries = codes.shape[1]
    wide = entries * per_tile
    spread = (iota((entries, wide), 0) == iota((entries, wide), 1) // per_tile).astype(bf16)
    expanded = plain(codes.astype(bf16), spread).astype(i32)
    return expanded * per_tile + iota(expanded.shape, 1) % per_tile


def announce_kernel(panel, per_tile, owner_ref, cand_ref, teacher_ref, out_ref, rows_ref):
    tiles = owner_ref.shape[1]
    entries = 2 * tiles
    tokens = tiles * per_tile
    slots = out_ref.shape[0]
    owner = jnp.concatenate([owner_ref[0:1, :], owner_ref[1:2, :]], axis=1).astype(f32)
    owners = jnp.broadcast_to(owner, (entries, entries))
    earlier = iota((entries, entries), 0) % tiles < iota((entries, entries), 1) % tiles
    same = (owners == owners.T) & earlier
    rank = jnp.sum(jnp.where(same, 1.0, 0.0), axis=0, keepdims=True)
    code = owner * 2.0 + rank
    rows = rows_of(jnp.broadcast_to(code, (8, entries)), per_tile)
    rows_ref[...] = rows
    cand = cand_ref[...]
    teacher = teacher_ref[...]
    columns = (
        jnp.where(cand < panel, cand + 1, 0).astype(f32),
        jnp.where(cand >= panel, cand - panel + 1, 0).astype(f32),
    )
    width = 2 * cand.shape[0]
    for which in range(8):
        row = iota((slots, tokens), 0) * 8 + which
        told = jnp.zeros((slots, width), f32)
        for group in range(2):
            hot = jnp.where(row == rows[0:1, group * tokens : (group + 1) * tokens], 1.0, 0.0)
            told = told + by_rows(
                hot, jnp.concatenate([columns[group], teacher], axis=0), HIGHEST
            )
        out_ref[:, which * width : (which + 1) * width] = told
    out_ref[:, 8 * width : 8 * width + entries] = jnp.broadcast_to(code, (slots, entries))


def announce(tile_owners, cand, teacher, panel, per_tile, owners):
    entries = 2 * tile_owners.shape[1]
    return pl.pallas_call(
        functools.partial(announce_kernel, panel, per_tile),
        out_shape=(
            jax.ShapeDtypeStruct((owners, 16 * cand.shape[0] + entries), f32),
            jax.ShapeDtypeStruct((8, entries * per_tile), i32),
        ),
        compiler_params=settings(58),
        name="announce",
    )(tile_owners, cand, teacher)


def route_kernel(per_tile, tok_ref, codes_ref, hidden_ref, out_ref, rows_ref, held_ref):
    step = pl.program_id(0)
    width = hidden_ref.shape[0]
    owners, lanes, _ = held_ref.shape
    blocks = lanes // 8
    tokens = rows_ref.shape[1] // 2
    pairs = hidden_ref.shape[1] // (2 * tokens)
    steps = blocks // (2 * pairs)

    @pl.when(step == 0)
    def _():
        rows_ref[...] = rows_of(codes_ref[...], per_tile)

    @pl.when(step < steps)
    def _():
        chunk = 32
        row = iota((chunk * 8, tokens), 0).astype(f32).astype(bf16)
        for pair in range(pairs):
            first = step * (2 * pairs) + 2 * pair
            rows = [rows_ref[pl.ds(first + w, 1), :] for w in range(2)]
            for at in range(0, owners, chunk):
                here = [(r - at * 8).astype(f32).astype(bf16) for r in rows]
                parts = []
                for which in range(2):
                    hot = jnp.where(
                        (row == here[which][:, 0:tokens])
                        | (row == here[which][:, tokens : 2 * tokens]),
                        jnp.ones_like(row),
                        jnp.zeros_like(row),
                    )
                    lane = (2 * pair + which) * tokens
                    part = by_rows(hot, hidden_ref[:, lane : lane + tokens])
                    parts.append(part.reshape(chunk, 8, width))
                held_ref[at : at + chunk, pl.ds(pl.multiple_of(first * 8, 16), 16), :] = (
                    jnp.concatenate(parts, axis=1).astype(bf16)
                )

    @pl.when(step >= steps)
    def _():
        count = out_ref.shape[0]
        for k in range(count):
            out_ref[k] = held_ref[(step - steps) * count + k].T


def route(tok, told, hidden, per_tile, blocks):
    width, total = hidden.shape
    owners = told.shape[0]
    tokens = total // blocks
    entries = 2 * tokens // per_tile
    pairs = 4
    steps = blocks // (2 * pairs)
    turn = 32
    return pl.pallas_call(
        functools.partial(route_kernel, per_tile),
        grid_spec=pltpu.PrefetchScalarGridSpec(
            num_scalar_prefetch=1,
            grid=(steps + owners // turn,),
            in_specs=[
                pl.BlockSpec((blocks, entries), lambda s, t: (t[0], told.shape[1] // entries - 1)),
                pl.BlockSpec(
                    (width, 2 * pairs * tokens), lambda s, t: (0, jnp.minimum(s, steps - 1))
                ),
            ],
            out_specs=pl.BlockSpec(
                (turn, width, blocks * 8), lambda s, t: (jnp.maximum(s - steps, 0), 0, 0)
            ),
            scratch_shapes=[
                pltpu.VMEM((blocks, 2 * tokens), i32),
                pltpu.VMEM((owners, blocks * 8, width), bf16),
            ],
        ),
        out_shape=jax.ShapeDtypeStruct((owners, width, blocks * 8), bf16),
        compiler_params=settings(58),
        name="route",
    )(tok, told, hidden)


def place_kernel(per_tile, owner_ref, told_ref, dense_ref, facts_ref):
    sources = told_ref.shape[0]
    lanes = sources * 8
    width = told_ref.shape[1] // 9
    turned = jnp.stack(
        [told_ref[:, k * width : (k + 1) * width] for k in range(8)], axis=1
    ).reshape(lanes, width).T
    codes = jnp.broadcast_to(
        told_ref[:, 8 * width :].reshape(sources, 1, width), (sources, 8, width)
    ).reshape(lanes, width).T
    picks = width // 2
    columns = turned[0:picks].astype(i32) - 1
    teacher = turned[picks:]
    target = jnp.exp(teacher)
    panel = dense_ref.shape[0]
    chunk = 128
    place = iota((chunk, lanes), 0)
    for at in range(0, panel, chunk):
        dense = jnp.zeros((chunk, lanes), f32)
        for k in range(picks):
            dense = jnp.where(place == columns[k : k + 1] - at, target[k : k + 1], dense)
        dense_ref[at : at + chunk, :] = dense
    half = codes.shape[0] // 2
    other = jnp.concatenate([codes[half:], codes[:half]], axis=0)
    slot = (iota((1, lanes), 1) // per_tile) % 2
    mine = (owner_ref[0] * 2 + slot).astype(f32)
    partner = jnp.sum(jnp.where(codes == mine, other + 1.0, 0.0), axis=0, keepdims=True)
    mass = jnp.sum(target, axis=0, keepdims=True)
    entropy = jnp.sum(jnp.where(columns >= 0, target * teacher, 0.0), axis=0, keepdims=True)
    facts_ref[...] = jnp.concatenate(
        [partner, mass, entropy, jnp.zeros((5, lanes), f32)], axis=0
    )


def place(owner, told, panel, per_tile):
    sources, width = told.shape
    rows = sources * 8
    block = 16
    return pl.pallas_call(
        functools.partial(place_kernel, per_tile),
        grid_spec=pltpu.PrefetchScalarGridSpec(
            num_scalar_prefetch=1,
            grid=(sources // block,),
            in_specs=[pl.BlockSpec((block, width), lambda s, o: (s, 0))],
            out_specs=[
                pl.BlockSpec((panel, block * 8), lambda s, o: (0, s)),
                pl.BlockSpec((8, block * 8), lambda s, o: (0, s)),
            ],
        ),
        out_shape=(
            jax.ShapeDtypeStruct((panel, rows), f32),
            jax.ShapeDtypeStruct((8, rows), f32),
        ),
        compiler_params=settings(),
        cost_estimate=pl.CostEstimate(
            flops=2 * 64 * panel * rows, bytes_accessed=8 * panel * rows, transcendentals=64 * rows
        ),
        name="place",
    )(owner, told)


def score_kernel(
    bounds, head_ref, rows_ref, dense_ref, facts_ref, part_ref, own_ref, told_ref, total_ref, held_ref, sems
):
    groups, _, lanes = rows_ref.shape
    copies = []
    for k, (low, high) in enumerate(bounds):
        copies.append(
            pltpu.make_async_copy(
                rows_ref.at[:, low:high, :], held_ref.at[:, low:high, :], sems.at[k]
            )
        )
    for copy in copies:
        copy.start()
    for k, (low, high) in enumerate(bounds):
        copies[k].wait()
        for t in range(groups):
            here = slice(t * lanes, (t + 1) * lanes)
            product = plain(head_ref[:, low:high], held_ref[t, low:high, :])
            total_ref[:, here] = product if k == 0 else total_ref[:, here] + product
    count = total_ref.shape[1]
    chunk = 128
    logs, largest, shares = [], [], []
    for at in range(0, count, chunk):
        here = slice(at, at + chunk)
        dense = dense_ref[:, here]
        score = total_ref[:, here]
        named = dense > 0.0
        most = jnp.max(jnp.where(named, score, nothing), axis=0, keepdims=True)
        part = jnp.where(named, jnp.exp(score - most), 0.0)
        part_ref[:, here] = part
        whole = jnp.sum(part, axis=0, keepdims=True)
        log = jnp.where(whole > 0.0, most + jnp.log(jnp.maximum(whole, 1.0)), nothing)
        shares.append(
            facts_ref[2:3, here] - jnp.sum(dense * score, axis=0, keepdims=True)
        )
        logs.append(log)
        largest.append(most)
    logs = jnp.concatenate(logs, axis=1)
    largest = jnp.concatenate(largest, axis=1)
    shares = jnp.concatenate(shares, axis=1)
    own_ref[...] = jnp.concatenate([largest, logs, jnp.zeros((6, count), f32)], axis=0)
    owners = told_ref.shape[0]
    told_ref[:, 0:count] = jnp.broadcast_to(logs, (owners, count))
    home = iota((owners, count), 1) // 8 == iota((owners, count), 0)
    which = (iota((count, 128), 0) % 8 == iota((count, 128), 1)).astype(f32)
    told_ref[:, count : count + 128] = plain(
        jnp.where(home, jnp.broadcast_to(shares, (owners, count)), 0.0), which, HIGHEST
    )


def score(head, rows, dense, facts, owners):
    panel, width = head.shape
    groups, _, lanes = rows.shape
    count = groups * lanes
    block = 1024
    cuts = [0, block // 4] + list(range(block, width, block)) + [width]
    bounds = list(zip(cuts[:-1], cuts[1:]))
    return pl.pallas_call(
        functools.partial(score_kernel, bounds),
        in_specs=[near, far, near, near],
        out_specs=[near, near, near],
        out_shape=(
            jax.ShapeDtypeStruct((panel, count), f32),
            jax.ShapeDtypeStruct((8, count), f32),
            jax.ShapeDtypeStruct((owners, count + 128), f32),
        ),
        scratch_shapes=[
            pltpu.VMEM((panel, count), f32),
            pltpu.VMEM((groups, width, lanes), bf16),
            pltpu.SemaphoreType.DMA((len(bounds),)),
        ],
        compiler_params=settings(24),
        name="score",
    )(head, rows, dense, facts)


def log_sum(a, b):
    most = jnp.maximum(a, b)
    return most + jnp.log(jnp.exp(a - most) + jnp.exp(b - most))


def turn_kernel(part_ref, dense_ref, part_out, dense_out):
    part_out[...] = part_ref[...].T
    dense_out[...] = (loss_weight * dense_ref[...]).T


def turn(part, dense):
    panel, count = part.shape
    block = 256
    columns = pl.BlockSpec((panel, block), lambda s: (0, s))
    rows = pl.BlockSpec((block, panel), lambda s: (s, 0))
    return pl.pallas_call(
        turn_kernel,
        grid=(count // block,),
        in_specs=[columns, columns],
        out_specs=[rows, rows],
        out_shape=[jax.ShapeDtypeStruct((count, panel), f32)] * 2,
        compiler_params=settings(24),
        cost_estimate=pl.CostEstimate(
            flops=4 * panel * count, bytes_accessed=16 * panel * count, transcendentals=0
        ),
        name="turn",
    )(part, dense)


def part_kernel(
    per_tile, logs_ref, facts_ref, own_ref, part_ref, dense_ref, head_ref, out_ref, weight_ref, held_ref, sems
):
    count, panel = part_ref.shape
    owners = logs_ref.shape[0]
    chunk = 128
    for at in range(0, count, chunk):
        here = slice(at, at + chunk)
        logs = logs_ref[:, here]
        partner = facts_ref[0:1, here].astype(i32) - 1
        slot = (iota((1, chunk), 1) // per_tile) % 2
        across = jnp.where(
            slot == 0, pltpu.roll(logs, chunk - per_tile, 1), pltpu.roll(logs, per_tile, 1)
        )
        picked = jnp.where(
            iota((owners, chunk), 0) == partner // 2,
            jnp.where(partner % 2 == slot, logs, across),
            0.0,
        )
        other = jnp.sum(picked, axis=0, keepdims=True)
        total = log_sum(own_ref[1:2, here], other)
        scale = loss_weight * facts_ref[1:2, here] * jnp.exp(own_ref[0:1, here] - total)
        scale = jnp.broadcast_to(scale, (chunk, chunk)).T
        for col in range(0, panel, chunk):
            there = slice(col, col + chunk)
            weight = part_ref[here, there] * scale - dense_ref[here, there]
            weight_ref[here, there] = weight.astype(bf16)
    slots, _, block = held_ref.shape

    def leave(k):
        place = pl.ds(pl.multiple_of(k * block, block), block)
        return pltpu.make_async_copy(
            held_ref.at[k % slots], out_ref.at[:, place], sems.at[k % slots]
        )

    def one(k, carry):
        @pl.when(k >= slots)
        def _():
            leave(k - slots).wait()

        place = pl.ds(pl.multiple_of(k * block, block), block)
        held_ref[k % slots] = plain(weight_ref[...], head_ref[:, place]).astype(bf16)
        leave(k).start()
        return carry

    blocks = out_ref.shape[1] // block
    lax.fori_loop(0, blocks, one, 0)
    for k in range(blocks - slots, blocks):
        leave(k).wait()


def grad_parts(logs, facts, own, part, dense, head, per_tile):
    panel, width = head.shape
    count = part.shape[0]
    block = 512
    return pl.pallas_call(
        functools.partial(part_kernel, per_tile),
        in_specs=[near] * 6,
        out_specs=[far, near],
        out_shape=(
            jax.ShapeDtypeStruct((count, width), bf16),
            jax.ShapeDtypeStruct((count, panel), bf16),
        ),
        scratch_shapes=[
            pltpu.VMEM((2, count, block), bf16),
            pltpu.SemaphoreType.DMA((2,)),
        ],
        compiler_params=settings(16),
        name="grad_parts",
    )(logs, facts, own, part, dense, head)


def head_kernel(weight_ref, rows_ref, out_ref, turned_ref):
    groups, _, lanes = rows_ref.shape

    @pl.when(pl.program_id(0) == 0)
    def _():
        for at in range(0, weight_ref.shape[0], 128):
            turned_ref[:, at : at + 128] = weight_ref[at : at + 128, :].T

    total = by_rows(turned_ref[:, 0:lanes], rows_ref[0])
    for t in range(1, groups):
        total = total + by_rows(turned_ref[:, t * lanes : (t + 1) * lanes], rows_ref[t])
    out_ref[...] = total.astype(bf16)


def grad_of_head(weight, rows):
    count, panel = weight.shape
    groups, width, lanes = rows.shape
    block = 512
    return pl.pallas_call(
        head_kernel,
        grid=(width // block,),
        in_specs=[
            pl.BlockSpec((count, panel), lambda s: (0, 0)),
            pl.BlockSpec((groups, block, lanes), lambda s: (0, s, 0)),
        ],
        out_specs=pl.BlockSpec((panel, block), lambda s: (0, s)),
        out_shape=jax.ShapeDtypeStruct((panel, width), bf16),
        scratch_shapes=[pltpu.VMEM((panel, count), bf16)],
        compiler_params=settings(),
        cost_estimate=pl.CostEstimate(
            flops=2 * panel * count * width,
            bytes_accessed=2 * (panel + count) * width,
            transcendentals=0,
        ),
        name="grad_of_head",
    )(weight, rows)


def loss_kernel(me_ref, logs_ref, rows_ref, teacher_ref, loss_ref, table_ref):
    owners = logs_ref.shape[0]
    tokens = teacher_ref.shape[1]
    count = table_ref.shape[1]
    mine = iota((count, 128), 0) == me_ref[0] * 8 + iota((count, 128), 1)
    mine = jnp.where(mine & (iota((count, 128), 1) < 8), 1.0, 0.0)
    logs = plain(logs_ref[:, 0:count], mine, HIGHEST).T
    shares = logs_ref[:, count : count + 128].T
    found = []
    total = jnp.zeros((1, tokens), f32)
    for group in range(2):
        row = rows_ref[0:1, group * tokens : (group + 1) * tokens]
        owner = jnp.where(iota((owners, tokens), 0) == row // 8, 1.0, 0.0)
        slot = iota((128, tokens), 0) == row % 8
        for table, kept in ((logs, True), (shares, False)):
            got = jnp.where(slot, plain(table, owner, HIGHEST), 0.0)
            got = jnp.sum(got, axis=0, keepdims=True)
            if kept:
                found.append(got)
            else:
                total = total + got
    teacher = teacher_ref[...]
    mass = jnp.sum(jnp.exp(teacher), axis=0, keepdims=True)
    loss_ref[...] = total + mass * log_sum(found[0], found[1])
    first, second = rows_ref[0:1, 0:tokens], rows_ref[0:1, tokens : 2 * tokens]
    for at in range(0, count, 128):
        row = iota((128, tokens), 0) + at
        hot = jnp.where((row == first) | (row == second), 1.0, 0.0)
        table_ref[:, at : at + 128] = hot.T.astype(bf16)


def losses(me, logs, rows, teacher, count):
    tokens = teacher.shape[1]
    return pl.pallas_call(
        loss_kernel,
        in_specs=[pl.BlockSpec(memory_space=pltpu.SMEM)] + [pl.BlockSpec(memory_space=pltpu.VMEM)] * 3,
        out_shape=(
            jax.ShapeDtypeStruct((1, tokens), f32),
            jax.ShapeDtypeStruct((tokens, count), bf16),
        ),
        compiler_params=settings(),
        cost_estimate=pl.CostEstimate(
            flops=12 * 2 * count * tokens * 128, bytes_accessed=4 * count * tokens, transcendentals=0
        ),
        name="losses",
    )(me, logs, rows, teacher)


def combine_kernel(table_ref, parts_ref, out_ref):
    out_ref[...] = plain(table_ref[...], parts_ref[...]).astype(bf16)


def combine(table, parts):
    tokens, count = table.shape
    width = parts.shape[1]
    block = width // 2
    return pl.pallas_call(
        combine_kernel,
        grid=(width // block,),
        in_specs=[
            pl.BlockSpec((tokens, count), lambda s: (0, 0)),
            pl.BlockSpec((count, block), lambda s: (0, s)),
        ],
        out_specs=pl.BlockSpec((tokens, block), lambda s: (0, s)),
        out_shape=jax.ShapeDtypeStruct((tokens, width), bf16),
        compiler_params=settings(58),
        name="combine",
    )(table, parts)


def exchange(values):
    owners, width = values.shape
    moved = lax.all_to_all(
        values.reshape(owners, 1, width), ("tok", "voc"), split_axis=0, concat_axis=0, tiled=True
    )
    return moved.reshape(owners, width)


def exchange_tiles(values):
    return lax.all_to_all(values, ("tok", "voc"), split_axis=0, concat_axis=0, tiled=True)


def body(hidden, head_weight, tile_owners, cand_pos, teacher_logp):
    panel, width = head_weight.shape
    tiles = tile_owners.shape[0]
    tokens = cand_pos.shape[0]
    per_tile = tokens // tiles
    tok_size, blocks = lax.axis_size("tok"), lax.axis_size("voc")
    owners = tok_size * blocks
    count = owners * 8
    tok = lax.axis_index("tok")
    me = (tok * blocks + lax.axis_index("voc")).astype(i32).reshape(1)
    teacher = teacher_logp.T
    told, home_rows = announce(tile_owners.T, cand_pos.T, teacher, panel, per_tile, owners)
    told = exchange(told)
    sent = route(tok.astype(i32).reshape(1), told, hidden.T, per_tile, blocks)
    rows = exchange_tiles(sent).reshape(tok_size, width, blocks * 8)
    dense, facts = place(me, told, panel, per_tile)
    part, own, logs = score(head_weight, rows, dense, facts, owners)
    logs = exchange(logs)
    part_rows, dense_rows = turn(part, dense)
    parts, weight = grad_parts(logs, facts, own, part_rows, dense_rows, head_weight, per_tile)
    home_parts = exchange_tiles(parts.reshape(owners, 8, width)).reshape(count, width)
    grad_head = grad_of_head(weight, rows)
    loss, table = losses(me, logs, home_rows, teacher, count)
    grad_hidden = combine(table, home_parts)
    return (loss.reshape(tokens), grad_hidden, grad_head)


def solution(mesh):
    placed = (
        P("tok", "voc"),
        P(("tok", "voc"), None),
        P(("tok", "voc"), None),
        P(("tok", "voc"), None),
        P(("tok", "voc"), None),
    )
    return jax.shard_map(
        body,
        mesh=mesh,
        in_specs=placed,
        out_specs=(P(("tok", "voc")), P(("tok", "voc"), None), P(("tok", "voc"), None)),
        check_vma=False,
    )
```

```python
import functools

import jax
import jax.numpy as jnp
from jax import lax
from jax.experimental import pallas as pl
from jax.experimental.pallas import tpu as pltpu
from jax.sharding import PartitionSpec as P

loss_weight = 16.0
nothing = -1e30
f32, bf16, i32 = jnp.float32, jnp.bfloat16, jnp.int32
HIGHEST = lax.Precision.HIGHEST


near, far = pl.BlockSpec(memory_space=pltpu.VMEM), pl.BlockSpec(memory_space=pl.ANY)


def settings(mib=32):
    return pltpu.CompilerParams(vmem_limit_bytes=mib * 1024 * 1024)


def by_rows(a, b, precision=None):
    return lax.dot_general(
        a, b, (((1,), (1,)), ((), ())), preferred_element_type=f32, precision=precision
    )


def plain(a, b, precision=None):
    return lax.dot_general(
        a, b, (((1,), (0,)), ((), ())), preferred_element_type=f32, precision=precision
    )


def iota(shape, dim):
    return lax.broadcasted_iota(i32, shape, dim)


def rows_of(codes, per_tile):
    entries = codes.shape[1]
    wide = entries * per_tile
    spread = (iota((entries, wide), 0) == iota((entries, wide), 1) // per_tile).astype(bf16)
    expanded = plain(codes.astype(bf16), spread).astype(i32)
    return expanded * per_tile + iota(expanded.shape, 1) % per_tile


def announce_kernel(panel, per_tile, owner_ref, cand_ref, teacher_ref, out_ref, rows_ref):
    tiles = owner_ref.shape[1]
    entries = 2 * tiles
    tokens = tiles * per_tile
    slots = out_ref.shape[0]
    owner = jnp.concatenate([owner_ref[0:1, :], owner_ref[1:2, :]], axis=1).astype(f32)
    owners = jnp.broadcast_to(owner, (entries, entries))
    earlier = iota((entries, entries), 0) % tiles < iota((entries, entries), 1) % tiles
    same = (owners == owners.T) & earlier
    rank = jnp.sum(jnp.where(same, 1.0, 0.0), axis=0, keepdims=True)
    code = owner * 2.0 + rank
    rows = rows_of(jnp.broadcast_to(code, (8, entries)), per_tile)
    rows_ref[...] = rows
    cand = cand_ref[...]
    teacher = teacher_ref[...]
    columns = (
        jnp.where(cand < panel, cand + 1, 0).astype(f32),
        jnp.where(cand >= panel, cand - panel + 1, 0).astype(f32),
    )
    width = 2 * cand.shape[0]
    for which in range(8):
        row = iota((slots, tokens), 0) * 8 + which
        told = jnp.zeros((slots, width), f32)
        for group in range(2):
            hot = jnp.where(row == rows[0:1, group * tokens : (group + 1) * tokens], 1.0, 0.0)
            told = told + by_rows(
                hot, jnp.concatenate([columns[group], teacher], axis=0), HIGHEST
            )
        out_ref[:, 0, which * width : (which + 1) * width] = told
    out_ref[:, 0, 8 * width : 8 * width + entries] = jnp.broadcast_to(code, (slots, entries))


def announce(tile_owners, cand, teacher, panel, per_tile, owners):
    entries = 2 * tile_owners.shape[1]
    return pl.pallas_call(
        functools.partial(announce_kernel, panel, per_tile),
        out_shape=(
            jax.ShapeDtypeStruct((owners, 1, 16 * cand.shape[0] + entries), f32),
            jax.ShapeDtypeStruct((8, entries * per_tile), i32),
        ),
        compiler_params=settings(58),
        name="announce",
    )(tile_owners, cand, teacher)


def route_kernel(per_tile, tok_ref, codes_ref, hidden_ref, out_ref, rows_ref, held_ref):
    step = pl.program_id(0)
    width = hidden_ref.shape[0]
    owners, lanes, _ = held_ref.shape
    blocks = lanes // 8
    tokens = rows_ref.shape[1] // 2
    pairs = hidden_ref.shape[1] // (2 * tokens)
    steps = blocks // (2 * pairs)

    @pl.when(step == 0)
    def _():
        rows_ref[...] = rows_of(codes_ref[:, 0, :], per_tile)

    @pl.when(step < steps)
    def _():
        chunk = 32
        row = iota((chunk * 8, tokens), 0).astype(f32).astype(bf16)
        for pair in range(pairs):
            first = step * (2 * pairs) + 2 * pair
            rows = [rows_ref[pl.ds(first + w, 1), :] for w in range(2)]
            for at in range(0, owners, chunk):
                here = [(r - at * 8).astype(f32).astype(bf16) for r in rows]
                parts = []
                for which in range(2):
                    hot = jnp.where(
                        (row == here[which][:, 0:tokens])
                        | (row == here[which][:, tokens : 2 * tokens]),
                        jnp.ones_like(row),
                        jnp.zeros_like(row),
                    )
                    lane = (2 * pair + which) * tokens
                    part = by_rows(hot, hidden_ref[:, lane : lane + tokens])
                    parts.append(part.reshape(chunk, 8, width))
                held_ref[at : at + chunk, pl.ds(pl.multiple_of(first * 8, 16), 16), :] = (
                    jnp.concatenate(parts, axis=1).astype(bf16)
                )

    @pl.when(step >= steps)
    def _():
        count = out_ref.shape[0]
        for k in range(count):
            out_ref[k] = held_ref[(step - steps) * count + k].T


def route(tok, told, hidden, per_tile, blocks):
    width, total = hidden.shape
    owners = told.shape[0]
    tokens = total // blocks
    entries = 2 * tokens // per_tile
    pairs = 4
    steps = blocks // (2 * pairs)
    turn = 32
    return pl.pallas_call(
        functools.partial(route_kernel, per_tile),
        grid_spec=pltpu.PrefetchScalarGridSpec(
            num_scalar_prefetch=1,
            grid=(steps + owners // turn,),
            in_specs=[
                pl.BlockSpec((blocks, 1, entries), lambda s, t: (t[0], 0, told.shape[2] // entries - 1)),
                pl.BlockSpec(
                    (width, 2 * pairs * tokens), lambda s, t: (0, jnp.minimum(s, steps - 1))
                ),
            ],
            out_specs=pl.BlockSpec(
                (turn, width, blocks * 8), lambda s, t: (jnp.maximum(s - steps, 0), 0, 0)
            ),
            scratch_shapes=[
                pltpu.VMEM((blocks, 2 * tokens), i32),
                pltpu.VMEM((owners, blocks * 8, width), bf16),
            ],
        ),
        out_shape=jax.ShapeDtypeStruct((owners, width, blocks * 8), bf16),
        compiler_params=settings(58),
        name="route",
    )(tok, told, hidden)


def place_kernel(per_tile, owner_ref, told_ref, dense_ref, facts_ref):
    sources = told_ref.shape[0]
    lanes = sources * 8
    width = told_ref.shape[2] // 9
    turned = jnp.stack(
        [told_ref[:, 0, k * width : (k + 1) * width] for k in range(8)], axis=1
    ).reshape(lanes, width).T
    codes = jnp.broadcast_to(
        told_ref[:, :, 8 * width :], (sources, 8, width)
    ).reshape(lanes, width).T
    picks = width // 2
    columns = turned[0:picks].astype(i32) - 1
    teacher = turned[picks:]
    target = jnp.exp(teacher)
    panel = dense_ref.shape[0]
    chunk = 128
    place = iota((chunk, lanes), 0)
    for at in range(0, panel, chunk):
        dense = jnp.zeros((chunk, lanes), f32)
        for k in range(picks):
            dense = jnp.where(place == columns[k : k + 1] - at, target[k : k + 1], dense)
        dense_ref[at : at + chunk, :] = dense
    half = codes.shape[0] // 2
    other = jnp.concatenate([codes[half:], codes[:half]], axis=0)
    slot = (iota((1, lanes), 1) // per_tile) % 2
    mine = (owner_ref[0] * 2 + slot).astype(f32)
    partner = jnp.sum(jnp.where(codes == mine, other + 1.0, 0.0), axis=0, keepdims=True)
    mass = jnp.sum(target, axis=0, keepdims=True)
    entropy = jnp.sum(jnp.where(columns >= 0, target * teacher, 0.0), axis=0, keepdims=True)
    facts_ref[...] = jnp.concatenate(
        [partner, mass, entropy, jnp.zeros((5, lanes), f32)], axis=0
    )


def place(owner, told, panel, per_tile):
    sources, _, width = told.shape
    rows = sources * 8
    block = 16
    return pl.pallas_call(
        functools.partial(place_kernel, per_tile),
        grid_spec=pltpu.PrefetchScalarGridSpec(
            num_scalar_prefetch=1,
            grid=(sources // block,),
            in_specs=[pl.BlockSpec((block, 1, width), lambda s, o: (s, 0, 0))],
            out_specs=[
                pl.BlockSpec((panel, block * 8), lambda s, o: (0, s)),
                pl.BlockSpec((8, block * 8), lambda s, o: (0, s)),
            ],
        ),
        out_shape=(
            jax.ShapeDtypeStruct((panel, rows), f32),
            jax.ShapeDtypeStruct((8, rows), f32),
        ),
        compiler_params=settings(),
        cost_estimate=pl.CostEstimate(
            flops=2 * 64 * panel * rows, bytes_accessed=8 * panel * rows, transcendentals=64 * rows
        ),
        name="place",
    )(owner, told)


def score_kernel(
    bounds, head_ref, rows_ref, dense_ref, facts_ref, part_ref, own_ref, told_ref,
    total_ref, head_held, rows_held, dense_held, part_held, sems, last_sem, out_sems
):
    groups, _, lanes = rows_ref.shape
    panel, count = total_ref.shape
    copies = []
    for k, (low, high) in enumerate(bounds):
        copies.append(
            (
                pltpu.make_async_copy(
                    head_ref.at[:, low:high], head_held.at[:, low:high], sems.at[0, k]
                ),
                pltpu.make_async_copy(
                    rows_ref.at[:, low:high, :], rows_held.at[:, low:high, :], sems.at[1, k]
                ),
            )
        )
    last = pltpu.make_async_copy(dense_ref, dense_held, last_sem)
    ahead = 3
    for pair in copies[:ahead]:
        pair[0].start()
        pair[1].start()
    for k, (low, high) in enumerate(bounds):
        if k + ahead < len(bounds):
            copies[k + ahead][0].start()
            copies[k + ahead][1].start()
        if k + ahead == len(bounds):
            last.start()
        copies[k][0].wait()
        copies[k][1].wait()
        for t in range(groups):
            here = slice(t * lanes, (t + 1) * lanes)
            product = plain(head_held[:, low:high], rows_held[t, low:high, :])
            total_ref[:, here] = product if k == 0 else total_ref[:, here] + product
    last.wait()
    chunk = 128
    logs, largest, shares, leave = [], [], [], []
    for k, at in enumerate(range(0, count, chunk)):
        here = slice(at, at + chunk)
        dense = dense_held[:, here]
        score = total_ref[:, here]
        named = dense > 0.0
        most = jnp.max(jnp.where(named, score, nothing), axis=0, keepdims=True)
        part = jnp.where(named, jnp.exp(score - most), 0.0)
        part_held[:, here] = part
        leave.append(
            pltpu.make_async_copy(part_held.at[:, here], part_ref.at[:, here], out_sems.at[k])
        )
        leave[-1].start()
        whole = jnp.sum(part, axis=0, keepdims=True)
        log = jnp.where(whole > 0.0, most + jnp.log(jnp.maximum(whole, 1.0)), nothing)
        shares.append(facts_ref[2:3, here] - jnp.sum(dense * score, axis=0, keepdims=True))
        logs.append(log)
        largest.append(most)
    logs = jnp.concatenate(logs, axis=1)
    largest = jnp.concatenate(largest, axis=1)
    own_ref[...] = jnp.concatenate([largest, logs, jnp.zeros((6, count), f32)], axis=0)
    owners = told_ref.shape[0]
    told_ref[:, 0, 0:count] = jnp.broadcast_to(logs, (owners, count))
    group = chunk // 8
    home = iota((group, chunk), 1) // 8 == iota((group, chunk), 0)
    which = (iota((chunk, chunk), 0) % 8 == iota((chunk, chunk), 1)).astype(f32)
    spread = [jnp.where(home, jnp.broadcast_to(share, (group, chunk)), 0.0) for share in shares]
    told_ref[:, 0, count : count + chunk] = plain(
        jnp.concatenate(spread, axis=0), which, HIGHEST
    )
    for copy in leave:
        copy.wait()


def score(head, rows, dense, facts, owners):
    panel, width = head.shape
    groups, _, lanes = rows.shape
    count = groups * lanes
    block = 1024
    cuts = [0, block // 4] + list(range(block, width, block)) + [width]
    bounds = list(zip(cuts[:-1], cuts[1:]))
    return pl.pallas_call(
        functools.partial(score_kernel, bounds),
        in_specs=[far, far, far, near],
        out_specs=[far, near, near],
        out_shape=(
            jax.ShapeDtypeStruct((panel, count), f32),
            jax.ShapeDtypeStruct((8, count), f32),
            jax.ShapeDtypeStruct((owners, 1, count + 128), f32),
        ),
        scratch_shapes=[
            pltpu.VMEM((panel, count), f32),
            pltpu.VMEM((panel, width), bf16),
            pltpu.VMEM((groups, width, lanes), bf16),
            pltpu.VMEM((panel, count), f32),
            pltpu.VMEM((panel, count), f32),
            pltpu.SemaphoreType.DMA((2, len(bounds))),
            pltpu.SemaphoreType.DMA,
            pltpu.SemaphoreType.DMA((count // 128,)),
        ],
        compiler_params=settings(56),
        name="score",
    )(head, rows, dense, facts)


def log_sum(a, b):
    most = jnp.maximum(a, b)
    return most + jnp.log(jnp.exp(a - most) + jnp.exp(b - most))


def turn_kernel(part_ref, dense_ref, part_out, dense_out):
    part_out[...] = part_ref[...].T
    dense_out[...] = (loss_weight * dense_ref[...]).T


def turn(part, dense):
    panel, count = part.shape
    block = 256
    columns = pl.BlockSpec((panel, block), lambda s: (0, s))
    rows = pl.BlockSpec((block, panel), lambda s: (s, 0))
    return pl.pallas_call(
        turn_kernel,
        grid=(count // block,),
        in_specs=[columns, columns],
        out_specs=[rows, rows],
        out_shape=[jax.ShapeDtypeStruct((count, panel), f32)] * 2,
        compiler_params=settings(56),
        cost_estimate=pl.CostEstimate(
            flops=4 * panel * count, bytes_accessed=16 * panel * count, transcendentals=0
        ),
        name="turn",
    )(part, dense)


def part_kernel(
    per_tile, logs_ref, facts_ref, own_ref, part_ref, dense_ref, head_ref, out_ref, weight_ref,
    part_held, dense_held, head_held, out_held, sems, head_sems, out_sems
):
    count, panel = part_ref.shape
    owners = logs_ref.shape[0]
    chunk = 128
    slots, _, block = out_held.shape
    blocks = out_ref.shape[1] // block
    tables, heads = [], []
    for k in range(count // chunk):
        here = slice(k * chunk, (k + 1) * chunk)
        tables.append(
            (
                pltpu.make_async_copy(part_ref.at[here], part_held.at[here], sems.at[0, k]),
                pltpu.make_async_copy(dense_ref.at[here], dense_held.at[here], sems.at[1, k]),
            )
        )
        tables[-1][0].start()
        tables[-1][1].start()
    for k in range(blocks):
        here = slice(k * block, (k + 1) * block)
        heads.append(
            pltpu.make_async_copy(head_ref.at[:, here], head_held.at[:, here], head_sems.at[k])
        )
    for k, at in enumerate(range(0, count, chunk)):
        here = slice(at, at + chunk)
        logs = logs_ref[:, 0, here]
        partner = facts_ref[0:1, here].astype(i32) - 1
        slot = (iota((1, chunk), 1) // per_tile) % 2
        across = jnp.where(
            slot == 0, pltpu.roll(logs, chunk - per_tile, 1), pltpu.roll(logs, per_tile, 1)
        )
        picked = jnp.where(
            iota((owners, chunk), 0) == partner // 2,
            jnp.where(partner % 2 == slot, logs, across),
            0.0,
        )
        other = jnp.sum(picked, axis=0, keepdims=True)
        total = log_sum(own_ref[1:2, here], other)
        scale = loss_weight * facts_ref[1:2, here] * jnp.exp(own_ref[0:1, here] - total)
        scale = jnp.broadcast_to(scale, (chunk, chunk)).T
        tables[k][0].wait()
        tables[k][1].wait()
        if k == 2:
            for copy in heads[:2]:
                copy.start()
        for col in range(0, panel, chunk):
            there = slice(col, col + chunk)
            weight = part_held[here, there] * scale - dense_held[here, there]
            weight_ref[here, there] = weight.astype(bf16)
    leave = []
    for k in range(blocks):
        here = slice(k * block, (k + 1) * block)
        if k >= slots:
            leave[k - slots].wait()
        if k + 2 < blocks:
            heads[k + 2].start()
        heads[k].wait()
        out_held[k % slots] = plain(weight_ref[...], head_held[:, here]).astype(bf16)
        leave.append(
            pltpu.make_async_copy(out_held.at[k % slots], out_ref.at[:, here], out_sems.at[k % slots])
        )
        leave[-1].start()
    for copy in leave[blocks - slots :]:
        copy.wait()


def grad_parts(logs, facts, own, part, dense, head, per_tile):
    panel, width = head.shape
    count = part.shape[0]
    block = 512
    return pl.pallas_call(
        functools.partial(part_kernel, per_tile),
        in_specs=[near, near, near, far, far, far],
        out_specs=[far, near],
        out_shape=(
            jax.ShapeDtypeStruct((count, width), bf16),
            jax.ShapeDtypeStruct((count, panel), bf16),
        ),
        scratch_shapes=[
            pltpu.VMEM((count, panel), f32),
            pltpu.VMEM((count, panel), f32),
            pltpu.VMEM((panel, width), bf16),
            pltpu.VMEM((2, count, block), bf16),
            pltpu.SemaphoreType.DMA((2, count // 128)),
            pltpu.SemaphoreType.DMA((width // block,)),
            pltpu.SemaphoreType.DMA((2,)),
        ],
        compiler_params=settings(56),
        name="grad_parts",
    )(logs, facts, own, part, dense, head)


def head_kernel(weight_ref, rows_ref, out_ref, turned_ref):
    groups, _, lanes = rows_ref.shape

    @pl.when(pl.program_id(0) == 0)
    def _():
        for at in range(0, weight_ref.shape[0], 128):
            turned_ref[:, at : at + 128] = weight_ref[at : at + 128, :].T

    total = by_rows(turned_ref[:, 0:lanes], rows_ref[0])
    for t in range(1, groups):
        total = total + by_rows(turned_ref[:, t * lanes : (t + 1) * lanes], rows_ref[t])
    out_ref[...] = total.astype(bf16)


def grad_of_head(weight, rows):
    count, panel = weight.shape
    groups, width, lanes = rows.shape
    block = 512
    return pl.pallas_call(
        head_kernel,
        grid=(width // block,),
        in_specs=[
            pl.BlockSpec((count, panel), lambda s: (0, 0)),
            pl.BlockSpec((groups, block, lanes), lambda s: (0, s, 0)),
        ],
        out_specs=pl.BlockSpec((panel, block), lambda s: (0, s)),
        out_shape=jax.ShapeDtypeStruct((panel, width), bf16),
        scratch_shapes=[pltpu.VMEM((panel, count), bf16)],
        compiler_params=settings(),
        cost_estimate=pl.CostEstimate(
            flops=2 * panel * count * width,
            bytes_accessed=2 * (panel + count) * width,
            transcendentals=0,
        ),
        name="grad_of_head",
    )(weight, rows)


def loss_kernel(me_ref, logs_ref, rows_ref, teacher_ref, loss_ref, table_ref):
    owners = logs_ref.shape[0]
    tokens = teacher_ref.shape[1]
    count = table_ref.shape[1]
    mine = iota((count, 128), 0) == me_ref[0] * 8 + iota((count, 128), 1)
    mine = jnp.where(mine & (iota((count, 128), 1) < 8), 1.0, 0.0)
    logs = plain(logs_ref[:, 0, 0:count], mine, HIGHEST).T
    shares = logs_ref[:, 0, count : count + 128].T
    found = []
    total = jnp.zeros((1, tokens), f32)
    for group in range(2):
        row = rows_ref[0:1, group * tokens : (group + 1) * tokens]
        owner = jnp.where(iota((owners, tokens), 0) == row // 8, 1.0, 0.0)
        slot = iota((128, tokens), 0) == row % 8
        for table, kept in ((logs, True), (shares, False)):
            got = jnp.where(slot, plain(table, owner, HIGHEST), 0.0)
            got = jnp.sum(got, axis=0, keepdims=True)
            if kept:
                found.append(got)
            else:
                total = total + got
    teacher = teacher_ref[...]
    mass = jnp.sum(jnp.exp(teacher), axis=0, keepdims=True)
    loss_ref[...] = total + mass * log_sum(found[0], found[1])
    first, second = rows_ref[0:1, 0:tokens], rows_ref[0:1, tokens : 2 * tokens]
    for at in range(0, count, 128):
        row = iota((128, tokens), 0) + at
        hot = jnp.where((row == first) | (row == second), 1.0, 0.0)
        table_ref[:, at : at + 128] = hot.T.astype(bf16)


def losses(me, logs, rows, teacher, count):
    tokens = teacher.shape[1]
    return pl.pallas_call(
        loss_kernel,
        in_specs=[pl.BlockSpec(memory_space=pltpu.SMEM)] + [pl.BlockSpec(memory_space=pltpu.VMEM)] * 3,
        out_shape=(
            jax.ShapeDtypeStruct((1, tokens), f32),
            jax.ShapeDtypeStruct((tokens, count), bf16),
        ),
        compiler_params=settings(),
        cost_estimate=pl.CostEstimate(
            flops=12 * 2 * count * tokens * 128, bytes_accessed=4 * count * tokens, transcendentals=0
        ),
        name="losses",
    )(me, logs, rows, teacher)


def combine_kernel(table_ref, parts_ref, out_ref):
    out_ref[...] = plain(table_ref[...], parts_ref[...]).astype(bf16)


def combine(table, parts):
    tokens, count = table.shape
    width = parts.shape[1]
    block = width // 2
    return pl.pallas_call(
        combine_kernel,
        grid=(width // block,),
        in_specs=[
            pl.BlockSpec((tokens, count), lambda s: (0, 0)),
            pl.BlockSpec((count, block), lambda s: (0, s)),
        ],
        out_specs=pl.BlockSpec((tokens, block), lambda s: (0, s)),
        out_shape=jax.ShapeDtypeStruct((tokens, width), bf16),
        compiler_params=settings(58),
        name="combine",
    )(table, parts)


def exchange(values):
    return lax.all_to_all(values, ("tok", "voc"), split_axis=0, concat_axis=0, tiled=True)


def body(hidden, head_weight, tile_owners, cand_pos, teacher_logp):
    panel, width = head_weight.shape
    tiles = tile_owners.shape[0]
    tokens = cand_pos.shape[0]
    per_tile = tokens // tiles
    tok_size, blocks = lax.axis_size("tok"), lax.axis_size("voc")
    owners = tok_size * blocks
    count = owners * 8
    tok = lax.axis_index("tok")
    me = (tok * blocks + lax.axis_index("voc")).astype(i32).reshape(1)
    teacher = teacher_logp.T
    told, home_rows = announce(tile_owners.T, cand_pos.T, teacher, panel, per_tile, owners)
    told = exchange(told)
    sent = route(tok.astype(i32).reshape(1), told, hidden.T, per_tile, blocks)
    rows = exchange(sent).reshape(tok_size, width, blocks * 8)
    dense, facts = place(me, told, panel, per_tile)
    part, own, logs = score(head_weight, rows, dense, facts, owners)
    logs = exchange(logs)
    part_rows, dense_rows = turn(part, dense)
    parts, weight = grad_parts(logs, facts, own, part_rows, dense_rows, head_weight, per_tile)
    home_parts = exchange(parts.reshape(owners, 8, width)).reshape(count, width)
    grad_head = grad_of_head(weight, rows)
    loss, table = losses(me, logs, home_rows, teacher, count)
    grad_hidden = combine(table, home_parts)
    return (loss.reshape(tokens), grad_hidden, grad_head)


def solution(mesh):
    placed = (
        P("tok", "voc"),
        P(("tok", "voc"), None),
        P(("tok", "voc"), None),
        P(("tok", "voc"), None),
        P(("tok", "voc"), None),
    )
    return jax.shard_map(
        body,
        mesh=mesh,
        in_specs=placed,
        out_specs=(P(("tok", "voc")), P(("tok", "voc"), None), P(("tok", "voc"), None)),
        check_vma=False,
    )
```

```python
import functools

import jax
import jax.numpy as jnp
from jax import lax
from jax.experimental import pallas as pl
from jax.experimental.pallas import tpu as pltpu
from jax.sharding import PartitionSpec as P

loss_weight = 16.0
nothing = -1e30
f32, bf16, i32 = jnp.float32, jnp.bfloat16, jnp.int32
HIGHEST = lax.Precision.HIGHEST


near, far = pl.BlockSpec(memory_space=pltpu.VMEM), pl.BlockSpec(memory_space=pl.ANY)


def settings(mib=32):
    return pltpu.CompilerParams(vmem_limit_bytes=mib * 1024 * 1024)


def by_rows(a, b, precision=None):
    return lax.dot_general(
        a, b, (((1,), (1,)), ((), ())), preferred_element_type=f32, precision=precision
    )


def plain(a, b, precision=None):
    return lax.dot_general(
        a, b, (((1,), (0,)), ((), ())), preferred_element_type=f32, precision=precision
    )


def iota(shape, dim):
    return lax.broadcasted_iota(i32, shape, dim)


def rows_of(codes, per_tile):
    entries = codes.shape[1]
    wide = entries * per_tile
    spread = (iota((entries, wide), 0) == iota((entries, wide), 1) // per_tile).astype(bf16)
    expanded = plain(codes.astype(bf16), spread).astype(i32)
    return expanded * per_tile + iota(expanded.shape, 1) % per_tile


def announce_kernel(panel, per_tile, owner_ref, cand_ref, teacher_ref, out_ref, rows_ref):
    tiles = owner_ref.shape[1]
    entries = 2 * tiles
    tokens = tiles * per_tile
    slots = out_ref.shape[0]
    owner = jnp.concatenate([owner_ref[0:1, :], owner_ref[1:2, :]], axis=1).astype(f32)
    owners = jnp.broadcast_to(owner, (entries, entries))
    earlier = iota((entries, entries), 0) % tiles < iota((entries, entries), 1) % tiles
    same = (owners == owners.T) & earlier
    rank = jnp.sum(jnp.where(same, 1.0, 0.0), axis=0, keepdims=True)
    code = owner * 2.0 + rank
    rows = rows_of(jnp.broadcast_to(code, (8, entries)), per_tile)
    rows_ref[...] = rows
    cand = cand_ref[...]
    first = teacher_ref[...].astype(bf16)
    rest = teacher_ref[...] - first.astype(f32)
    second = rest.astype(bf16)
    third = (rest - second.astype(f32)).astype(bf16)
    sides = []
    for column in (
        jnp.where(cand < panel, cand + 1, 0),
        jnp.where(cand >= panel, cand - panel + 1, 0),
    ):
        high, low = column // 32, column % 32
        sides.append(
            jnp.concatenate(
                [
                    high.astype(f32).astype(bf16),
                    first,
                    low.astype(f32).astype(bf16),
                    second,
                    jnp.zeros_like(first),
                    third,
                ],
                axis=0,
            )
        )
    sides = jnp.concatenate(sides, axis=1)
    width = 2 * cand.shape[0]
    times = jnp.where(iota((slots, width), 1) < cand.shape[0], 32.0, 1.0)
    for which in range(8):
        row = iota((slots, 2 * tokens), 0) * 8 + which
        hot = jnp.where(row == rows[0:1, :], 1.0, 0.0).astype(bf16)
        told = by_rows(hot, sides)
        out_ref[:, 0, which * width : (which + 1) * width] = (
            told[:, 0:width] * times + told[:, width : 2 * width] + told[:, 2 * width :]
        )
    out_ref[:, 0, 8 * width : 8 * width + entries] = jnp.broadcast_to(code, (slots, entries))


def announce(tile_owners, cand, teacher, panel, per_tile, owners):
    entries = 2 * tile_owners.shape[1]
    return pl.pallas_call(
        functools.partial(announce_kernel, panel, per_tile),
        out_shape=(
            jax.ShapeDtypeStruct((owners, 1, 16 * cand.shape[0] + entries), f32),
            jax.ShapeDtypeStruct((8, entries * per_tile), i32),
        ),
        compiler_params=settings(58),
        name="announce",
    )(tile_owners, cand, teacher)


def route_kernel(per_tile, tok_ref, codes_ref, hidden_ref, out_ref, rows_ref, held_ref):
    step = pl.program_id(0)
    width = hidden_ref.shape[0]
    owners, lanes, _ = held_ref.shape
    blocks = lanes // 8
    tokens = rows_ref.shape[1] // 2
    pairs = hidden_ref.shape[1] // (2 * tokens)
    steps = blocks // (2 * pairs)

    @pl.when(step == 0)
    def _():
        rows_ref[...] = rows_of(codes_ref[:, 0, :], per_tile)

    @pl.when(step < steps)
    def _():
        chunk = 32
        row = iota((chunk * 8, tokens), 0).astype(f32).astype(bf16)
        for pair in range(pairs):
            first = step * (2 * pairs) + 2 * pair
            rows = [rows_ref[pl.ds(first + w, 1), :] for w in range(2)]
            for at in range(0, owners, chunk):
                here = [(r - at * 8).astype(f32).astype(bf16) for r in rows]
                parts = []
                for which in range(2):
                    hot = jnp.where(
                        (row == here[which][:, 0:tokens])
                        | (row == here[which][:, tokens : 2 * tokens]),
                        jnp.ones_like(row),
                        jnp.zeros_like(row),
                    )
                    lane = (2 * pair + which) * tokens
                    part = by_rows(hot, hidden_ref[:, lane : lane + tokens])
                    parts.append(part.reshape(chunk, 8, width))
                held_ref[at : at + chunk, pl.ds(pl.multiple_of(first * 8, 16), 16), :] = (
                    jnp.concatenate(parts, axis=1).astype(bf16)
                )

    @pl.when(step >= steps)
    def _():
        count = out_ref.shape[0]
        for k in range(count):
            out_ref[k] = held_ref[(step - steps) * count + k].T


def route(tok, told, hidden, per_tile, blocks):
    width, total = hidden.shape
    owners = told.shape[0]
    tokens = total // blocks
    entries = 2 * tokens // per_tile
    pairs = 4
    steps = blocks // (2 * pairs)
    turn = 32
    return pl.pallas_call(
        functools.partial(route_kernel, per_tile),
        grid_spec=pltpu.PrefetchScalarGridSpec(
            num_scalar_prefetch=1,
            grid=(steps + owners // turn,),
            in_specs=[
                pl.BlockSpec((blocks, 1, entries), lambda s, t: (t[0], 0, told.shape[2] // entries - 1)),
                pl.BlockSpec(
                    (width, 2 * pairs * tokens), lambda s, t: (0, jnp.minimum(s, steps - 1))
                ),
            ],
            out_specs=pl.BlockSpec(
                (turn, width, blocks * 8), lambda s, t: (jnp.maximum(s - steps, 0), 0, 0)
            ),
            scratch_shapes=[
                pltpu.VMEM((blocks, 2 * tokens), i32),
                pltpu.VMEM((owners, blocks * 8, width), bf16),
            ],
        ),
        out_shape=jax.ShapeDtypeStruct((owners, width, blocks * 8), bf16),
        compiler_params=settings(58),
        name="route",
    )(tok, told, hidden)


def place_kernel(per_tile, owner_ref, told_ref, dense_ref, facts_ref):
    sources = told_ref.shape[0]
    lanes = sources * 8
    width = told_ref.shape[2] // 9
    turned = jnp.stack(
        [told_ref[:, 0, k * width : (k + 1) * width] for k in range(8)], axis=1
    ).reshape(lanes, width).T
    codes = jnp.broadcast_to(
        told_ref[:, :, 8 * width :], (sources, 8, width)
    ).reshape(lanes, width).T
    picks = width // 2
    columns = turned[0:picks].astype(i32) - 1
    teacher = turned[picks:]
    target = jnp.exp(teacher)
    panel = dense_ref.shape[0]
    chunk = 128
    place = iota((chunk, lanes), 0)
    for at in range(0, panel, chunk):
        dense = jnp.zeros((chunk, lanes), f32)
        for k in range(picks):
            dense = jnp.where(place == columns[k : k + 1] - at, target[k : k + 1], dense)
        dense_ref[at : at + chunk, :] = dense
    half = codes.shape[0] // 2
    other = jnp.concatenate([codes[half:], codes[:half]], axis=0)
    slot = (iota((1, lanes), 1) // per_tile) % 2
    mine = (owner_ref[0] * 2 + slot).astype(f32)
    partner = jnp.sum(jnp.where(codes == mine, other + 1.0, 0.0), axis=0, keepdims=True)
    mass = jnp.sum(target, axis=0, keepdims=True)
    entropy = jnp.sum(jnp.where(columns >= 0, target * teacher, 0.0), axis=0, keepdims=True)
    facts_ref[...] = jnp.concatenate(
        [partner, mass, entropy, jnp.zeros((5, lanes), f32)], axis=0
    )


def place(owner, told, panel, per_tile):
    sources, _, width = told.shape
    rows = sources * 8
    block = 16
    return pl.pallas_call(
        functools.partial(place_kernel, per_tile),
        grid_spec=pltpu.PrefetchScalarGridSpec(
            num_scalar_prefetch=1,
            grid=(sources // block,),
            in_specs=[pl.BlockSpec((block, 1, width), lambda s, o: (s, 0, 0))],
            out_specs=[
                pl.BlockSpec((panel, block * 8), lambda s, o: (0, s)),
                pl.BlockSpec((8, block * 8), lambda s, o: (0, s)),
            ],
        ),
        out_shape=(
            jax.ShapeDtypeStruct((panel, rows), f32),
            jax.ShapeDtypeStruct((8, rows), f32),
        ),
        compiler_params=settings(58),
        cost_estimate=pl.CostEstimate(
            flops=2 * 64 * panel * rows, bytes_accessed=8 * panel * rows, transcendentals=64 * rows
        ),
        name="place",
    )(owner, told)


def score_kernel(
    bounds, head_ref, rows_ref, dense_ref, facts_ref, part_ref, own_ref, told_ref,
    total_ref, head_held, rows_held, dense_held, part_held, sems, last_sem, out_sems
):
    groups, _, lanes = rows_ref.shape
    panel, count = total_ref.shape
    copies = []
    for k, (low, high) in enumerate(bounds):
        copies.append(
            (
                pltpu.make_async_copy(
                    head_ref.at[:, low:high], head_held.at[:, low:high], sems.at[0, k]
                ),
                pltpu.make_async_copy(
                    rows_ref.at[:, low:high, :], rows_held.at[:, low:high, :], sems.at[1, k]
                ),
            )
        )
    last = pltpu.make_async_copy(dense_ref, dense_held, last_sem)
    ahead = 4
    for pair in copies[:ahead]:
        pair[0].start()
        pair[1].start()
    for k, (low, high) in enumerate(bounds):
        if k + ahead < len(bounds):
            copies[k + ahead][0].start()
            copies[k + ahead][1].start()
        if k + ahead == len(bounds):
            last.start()
        copies[k][0].wait()
        copies[k][1].wait()
        for t in range(groups):
            here = slice(t * lanes, (t + 1) * lanes)
            product = plain(head_held[:, low:high], rows_held[t, low:high, :])
            total_ref[:, here] = product if k == 0 else total_ref[:, here] + product
    last.wait()
    chunk = 128
    logs, largest, shares, leave = [], [], [], []
    for k, at in enumerate(range(0, count, chunk)):
        here = slice(at, at + chunk)
        dense = dense_held[:, here]
        score = total_ref[:, here]
        named = dense > 0.0
        most = jnp.max(jnp.where(named, score, nothing), axis=0, keepdims=True)
        part = jnp.where(named, jnp.exp(score - most), 0.0)
        part_held[:, here] = part
        leave.append(
            pltpu.make_async_copy(part_held.at[:, here], part_ref.at[:, here], out_sems.at[k])
        )
        leave[-1].start()
        whole = jnp.sum(part, axis=0, keepdims=True)
        log = jnp.where(whole > 0.0, most + jnp.log(jnp.maximum(whole, 1.0)), nothing)
        shares.append(facts_ref[2:3, here] - jnp.sum(dense * score, axis=0, keepdims=True))
        logs.append(log)
        largest.append(most)
    logs = jnp.concatenate(logs, axis=1)
    largest = jnp.concatenate(largest, axis=1)
    own_ref[...] = jnp.concatenate([largest, logs, jnp.zeros((6, count), f32)], axis=0)
    owners = told_ref.shape[0]
    told_ref[:, 0, 0:count] = jnp.broadcast_to(logs, (owners, count))
    group = chunk // 8
    home = iota((group, chunk), 1) // 8 == iota((group, chunk), 0)
    which = (iota((chunk, chunk), 0) % 8 == iota((chunk, chunk), 1)).astype(f32)
    spread = [jnp.where(home, jnp.broadcast_to(share, (group, chunk)), 0.0) for share in shares]
    told_ref[:, 0, count : count + chunk] = plain(
        jnp.concatenate(spread, axis=0), which, HIGHEST
    )
    for copy in leave:
        copy.wait()


def score(head, rows, dense, facts, owners):
    panel, width = head.shape
    groups, _, lanes = rows.shape
    count = groups * lanes
    block = 1024
    cuts = [0, 512, 1280, 2560, 3840, 5120]
    bounds = list(zip(cuts[:-1], cuts[1:]))
    return pl.pallas_call(
        functools.partial(score_kernel, bounds),
        in_specs=[far, far, far, near],
        out_specs=[far, near, near],
        out_shape=(
            jax.ShapeDtypeStruct((panel, count), f32),
            jax.ShapeDtypeStruct((8, count), f32),
            jax.ShapeDtypeStruct((owners, 1, count + 128), f32),
        ),
        scratch_shapes=[
            pltpu.VMEM((panel, count), f32),
            pltpu.VMEM((panel, width), bf16),
            pltpu.VMEM((groups, width, lanes), bf16),
            pltpu.VMEM((panel, count), f32),
            pltpu.VMEM((panel, count), f32),
            pltpu.SemaphoreType.DMA((2, len(bounds))),
            pltpu.SemaphoreType.DMA,
            pltpu.SemaphoreType.DMA((count // 128,)),
        ],
        compiler_params=settings(56),
        name="score",
    )(head, rows, dense, facts)


def log_sum(a, b):
    most = jnp.maximum(a, b)
    return most + jnp.log(jnp.exp(a - most) + jnp.exp(b - most))


def turn_kernel(part_ref, dense_ref, part_out, dense_out):
    part_out[...] = part_ref[...].T
    dense_out[...] = (loss_weight * dense_ref[...]).T


def turn(part, dense):
    panel, count = part.shape
    block = 256
    columns = pl.BlockSpec((panel, block), lambda s: (0, s))
    rows = pl.BlockSpec((block, panel), lambda s: (s, 0))
    return pl.pallas_call(
        turn_kernel,
        grid=(count // block,),
        in_specs=[columns, columns],
        out_specs=[rows, rows],
        out_shape=[jax.ShapeDtypeStruct((count, panel), f32)] * 2,
        compiler_params=settings(56),
        cost_estimate=pl.CostEstimate(
            flops=4 * panel * count, bytes_accessed=16 * panel * count, transcendentals=0
        ),
        name="turn",
    )(part, dense)


def part_kernel(
    per_tile, logs_ref, facts_ref, own_ref, part_ref, dense_ref, head_ref, out_ref, weight_ref,
    logs_held, facts_held, own_held, part_held, dense_held, head_held, out_held,
    small_sems, sems, head_sems, out_sems
):
    count, panel = part_ref.shape
    owners = logs_ref.shape[0]
    chunk = 128
    small = [
        pltpu.make_async_copy(facts_ref, facts_held, small_sems.at[0]),
        pltpu.make_async_copy(own_ref, own_held, small_sems.at[1]),
        pltpu.make_async_copy(logs_ref, logs_held, small_sems.at[2]),
    ]
    for copy in small:
        copy.start()
    slots, _, block = out_held.shape
    blocks = out_ref.shape[1] // block
    tables, heads = [], []
    for k in range(count // chunk):
        here = slice(k * chunk, (k + 1) * chunk)
        tables.append(
            (
                pltpu.make_async_copy(part_ref.at[here], part_held.at[here], sems.at[0, k]),
                pltpu.make_async_copy(dense_ref.at[here], dense_held.at[here], sems.at[1, k]),
            )
        )
        tables[-1][0].start()
        tables[-1][1].start()
    for k in range(blocks):
        here = slice(k * block, (k + 1) * block)
        heads.append(
            pltpu.make_async_copy(head_ref.at[:, here], head_held.at[:, here], head_sems.at[k])
        )
    for copy in small:
        copy.wait()
    for k, at in enumerate(range(0, count, chunk)):
        here = slice(at, at + chunk)
        logs = logs_held[:, 0, here]
        partner = facts_held[0:1, here].astype(i32) - 1
        slot = (iota((1, chunk), 1) // per_tile) % 2
        across = jnp.where(
            slot == 0, pltpu.roll(logs, chunk - per_tile, 1), pltpu.roll(logs, per_tile, 1)
        )
        picked = jnp.where(
            iota((owners, chunk), 0) == partner // 2,
            jnp.where(partner % 2 == slot, logs, across),
            0.0,
        )
        other = jnp.sum(picked, axis=0, keepdims=True)
        total = log_sum(own_held[1:2, here], other)
        scale = loss_weight * facts_held[1:2, here] * jnp.exp(own_held[0:1, here] - total)
        scale = jnp.broadcast_to(scale, (chunk, chunk)).T
        tables[k][0].wait()
        tables[k][1].wait()
        if k == 2:
            for copy in heads[:2]:
                copy.start()
        for col in range(0, panel, chunk):
            there = slice(col, col + chunk)
            weight = part_held[here, there] * scale - dense_held[here, there]
            weight_ref[here, there] = weight.astype(bf16)
    leave = []
    for k in range(blocks):
        here = slice(k * block, (k + 1) * block)
        if k >= slots:
            leave[k - slots].wait()
        if k + 2 < blocks:
            heads[k + 2].start()
        heads[k].wait()
        out_held[k % slots] = plain(weight_ref[...], head_held[:, here]).astype(bf16)
        leave.append(
            pltpu.make_async_copy(out_held.at[k % slots], out_ref.at[:, here], out_sems.at[k % slots])
        )
        leave[-1].start()
    for copy in leave[blocks - slots :]:
        copy.wait()


def grad_parts(logs, facts, own, part, dense, head, per_tile):
    panel, width = head.shape
    count = part.shape[0]
    block = 512
    return pl.pallas_call(
        functools.partial(part_kernel, per_tile),
        in_specs=[far] * 6,
        out_specs=[far, near],
        out_shape=(
            jax.ShapeDtypeStruct((count, width), bf16),
            jax.ShapeDtypeStruct((count, panel), bf16),
        ),
        scratch_shapes=[
            pltpu.VMEM(logs.shape, f32),
            pltpu.VMEM(facts.shape, f32),
            pltpu.VMEM(own.shape, f32),
            pltpu.VMEM((count, panel), f32),
            pltpu.VMEM((count, panel), f32),
            pltpu.VMEM((panel, width), bf16),
            pltpu.VMEM((2, count, block), bf16),
            pltpu.SemaphoreType.DMA((3,)),
            pltpu.SemaphoreType.DMA((2, count // 128)),
            pltpu.SemaphoreType.DMA((width // block,)),
            pltpu.SemaphoreType.DMA((2,)),
        ],
        compiler_params=settings(56),
        name="grad_parts",
    )(logs, facts, own, part, dense, head)


def head_kernel(weight_ref, rows_ref, out_ref, turned_ref):
    groups, _, lanes = rows_ref.shape

    @pl.when(pl.program_id(0) == 0)
    def _():
        for at in range(0, weight_ref.shape[0], 128):
            turned_ref[:, at : at + 128] = weight_ref[at : at + 128, :].T

    total = by_rows(turned_ref[:, 0:lanes], rows_ref[0])
    for t in range(1, groups):
        total = total + by_rows(turned_ref[:, t * lanes : (t + 1) * lanes], rows_ref[t])
    out_ref[...] = total.astype(bf16)


def grad_of_head(weight, rows):
    count, panel = weight.shape
    groups, width, lanes = rows.shape
    block = 512
    return pl.pallas_call(
        head_kernel,
        grid=(width // block,),
        in_specs=[
            pl.BlockSpec((count, panel), lambda s: (0, 0)),
            pl.BlockSpec((groups, block, lanes), lambda s: (0, s, 0)),
        ],
        out_specs=pl.BlockSpec((panel, block), lambda s: (0, s)),
        out_shape=jax.ShapeDtypeStruct((panel, width), bf16),
        scratch_shapes=[pltpu.VMEM((panel, count), bf16)],
        compiler_params=settings(),
        cost_estimate=pl.CostEstimate(
            flops=2 * panel * count * width,
            bytes_accessed=2 * (panel + count) * width,
            transcendentals=0,
        ),
        name="grad_of_head",
    )(weight, rows)


def loss_kernel(me_ref, logs_ref, rows_ref, teacher_ref, loss_ref, table_ref):
    owners = logs_ref.shape[0]
    tokens = teacher_ref.shape[1]
    count = table_ref.shape[1]
    mine = iota((count, 128), 0) == me_ref[0] * 8 + iota((count, 128), 1)
    mine = jnp.where(mine & (iota((count, 128), 1) < 8), 1.0, 0.0)
    logs = plain(logs_ref[:, 0, 0:count], mine, HIGHEST).T
    shares = logs_ref[:, 0, count : count + 128].T
    found = []
    total = jnp.zeros((1, tokens), f32)
    for group in range(2):
        row = rows_ref[0:1, group * tokens : (group + 1) * tokens]
        owner = jnp.where(iota((owners, tokens), 0) == row // 8, 1.0, 0.0)
        slot = iota((128, tokens), 0) == row % 8
        for table, kept in ((logs, True), (shares, False)):
            got = jnp.where(slot, plain(table, owner, HIGHEST), 0.0)
            got = jnp.sum(got, axis=0, keepdims=True)
            if kept:
                found.append(got)
            else:
                total = total + got
    teacher = teacher_ref[...]
    mass = jnp.sum(jnp.exp(teacher), axis=0, keepdims=True)
    loss_ref[...] = total + mass * log_sum(found[0], found[1])
    first, second = rows_ref[0:1, 0:tokens], rows_ref[0:1, tokens : 2 * tokens]
    for at in range(0, count, 128):
        row = iota((128, tokens), 0) + at
        hot = jnp.where((row == first) | (row == second), 1.0, 0.0)
        table_ref[:, at : at + 128] = hot.T.astype(bf16)


def losses(me, logs, rows, teacher, count):
    tokens = teacher.shape[1]
    return pl.pallas_call(
        loss_kernel,
        in_specs=[pl.BlockSpec(memory_space=pltpu.SMEM)] + [pl.BlockSpec(memory_space=pltpu.VMEM)] * 3,
        out_shape=(
            jax.ShapeDtypeStruct((1, tokens), f32),
            jax.ShapeDtypeStruct((tokens, count), bf16),
        ),
        compiler_params=settings(58),
        cost_estimate=pl.CostEstimate(
            flops=12 * 2 * count * tokens * 128, bytes_accessed=4 * count * tokens, transcendentals=0
        ),
        name="losses",
    )(me, logs, rows, teacher)


def combine_kernel(table_ref, parts_ref, out_ref):
    out_ref[...] = plain(table_ref[...], parts_ref[...]).astype(bf16)


def combine(table, parts):
    tokens, count = table.shape
    width = parts.shape[1]
    block = width // 2
    return pl.pallas_call(
        combine_kernel,
        grid=(width // block,),
        in_specs=[
            pl.BlockSpec((tokens, count), lambda s: (0, 0)),
            pl.BlockSpec((count, block), lambda s: (0, s)),
        ],
        out_specs=pl.BlockSpec((tokens, block), lambda s: (0, s)),
        out_shape=jax.ShapeDtypeStruct((tokens, width), bf16),
        compiler_params=settings(58),
        name="combine",
    )(table, parts)


def exchange(values):
    return lax.all_to_all(values, ("tok", "voc"), split_axis=0, concat_axis=0, tiled=True)


def body(hidden, head_weight, tile_owners, cand_pos, teacher_logp):
    panel, width = head_weight.shape
    tiles = tile_owners.shape[0]
    tokens = cand_pos.shape[0]
    per_tile = tokens // tiles
    tok_size, blocks = lax.axis_size("tok"), lax.axis_size("voc")
    owners = tok_size * blocks
    count = owners * 8
    tok = lax.axis_index("tok")
    me = (tok * blocks + lax.axis_index("voc")).astype(i32).reshape(1)
    teacher = teacher_logp.T
    told, home_rows = announce(tile_owners.T, cand_pos.T, teacher, panel, per_tile, owners)
    told = exchange(told)
    sent = route(tok.astype(i32).reshape(1), told, hidden.T, per_tile, blocks)
    rows = exchange(sent).reshape(tok_size, width, blocks * 8)
    dense, facts = place(me, told, panel, per_tile)
    part, own, logs = score(head_weight, rows, dense, facts, owners)
    logs = exchange(logs)
    part_rows, dense_rows = turn(part, dense)
    parts, weight = grad_parts(logs, facts, own, part_rows, dense_rows, head_weight, per_tile)
    home_parts = exchange(parts.reshape(owners, 8, width)).reshape(count, width)
    grad_head = grad_of_head(weight, rows)
    loss, table = losses(me, logs, home_rows, teacher, count)
    grad_hidden = combine(table, home_parts)
    return (loss.reshape(tokens), grad_hidden, grad_head)


def solution(mesh):
    placed = (
        P("tok", "voc"),
        P(("tok", "voc"), None),
        P(("tok", "voc"), None),
        P(("tok", "voc"), None),
        P(("tok", "voc"), None),
    )
    return jax.shard_map(
        body,
        mesh=mesh,
        in_specs=placed,
        out_specs=(P(("tok", "voc")), P(("tok", "voc"), None), P(("tok", "voc"), None)),
        check_vma=False,
    )
```

```python
import functools

import jax
import jax.numpy as jnp
from jax import lax
from jax.experimental import pallas as pl
from jax.experimental.pallas import tpu as pltpu
from jax.sharding import PartitionSpec as P

loss_weight = 16.0
nothing = -1e30
f32, bf16, i32 = jnp.float32, jnp.bfloat16, jnp.int32
HIGHEST = lax.Precision.HIGHEST


near, far = pl.BlockSpec(memory_space=pltpu.VMEM), pl.BlockSpec(memory_space=pl.ANY)


def settings(mib=32):
    return pltpu.CompilerParams(vmem_limit_bytes=mib * 1024 * 1024)


def by_rows(a, b, precision=None):
    return lax.dot_general(
        a, b, (((1,), (1,)), ((), ())), preferred_element_type=f32, precision=precision
    )


def plain(a, b, precision=None):
    return lax.dot_general(
        a, b, (((1,), (0,)), ((), ())), preferred_element_type=f32, precision=precision
    )


def iota(shape, dim):
    return lax.broadcasted_iota(i32, shape, dim)


def rows_of(codes, per_tile):
    entries = codes.shape[1]
    wide = entries * per_tile
    spread = (iota((entries, wide), 0) == iota((entries, wide), 1) // per_tile).astype(bf16)
    expanded = plain(codes.astype(bf16), spread).astype(i32)
    return expanded * per_tile + iota(expanded.shape, 1) % per_tile


def announce_kernel(panel, per_tile, owner_ref, cand_ref, teacher_ref, out_ref, rows_ref):
    tiles = owner_ref.shape[1]
    entries = 2 * tiles
    tokens = tiles * per_tile
    slots = out_ref.shape[0]
    owner = jnp.concatenate([owner_ref[0:1, :], owner_ref[1:2, :]], axis=1).astype(f32)
    owners = jnp.broadcast_to(owner, (entries, entries))
    earlier = iota((entries, entries), 0) % tiles < iota((entries, entries), 1) % tiles
    same = (owners == owners.T) & earlier
    rank = jnp.sum(jnp.where(same, 1.0, 0.0), axis=0, keepdims=True)
    code = owner * 2.0 + rank
    rows = rows_of(jnp.broadcast_to(code, (8, entries)), per_tile)
    rows_ref[...] = rows
    cand = cand_ref[...]
    first = teacher_ref[...].astype(bf16)
    rest = teacher_ref[...] - first.astype(f32)
    second = rest.astype(bf16)
    third = (rest - second.astype(f32)).astype(bf16)
    sides = []
    for column in (
        jnp.where(cand < panel, cand + 1, 0),
        jnp.where(cand >= panel, cand - panel + 1, 0),
    ):
        high, low = column // 32, column % 32
        sides.append(
            jnp.concatenate(
                [
                    high.astype(f32).astype(bf16),
                    first,
                    low.astype(f32).astype(bf16),
                    second,
                    jnp.zeros_like(first),
                    third,
                ],
                axis=0,
            )
        )
    sides = jnp.concatenate(sides, axis=1)
    width = 2 * cand.shape[0]
    times = jnp.where(iota((slots, width), 1) < cand.shape[0], 32.0, 1.0)
    for which in range(8):
        row = iota((slots, 2 * tokens), 0) * 8 + which
        hot = jnp.where(row == rows[0:1, :], 1.0, 0.0).astype(bf16)
        told = by_rows(hot, sides)
        out_ref[:, 0, which * width : (which + 1) * width] = (
            told[:, 0:width] * times + told[:, width : 2 * width] + told[:, 2 * width :]
        )
    out_ref[:, 0, 8 * width : 8 * width + entries] = jnp.broadcast_to(code, (slots, entries))


def announce(tile_owners, cand, teacher, panel, per_tile, owners):
    entries = 2 * tile_owners.shape[1]
    return pl.pallas_call(
        functools.partial(announce_kernel, panel, per_tile),
        out_shape=(
            jax.ShapeDtypeStruct((owners, 1, 16 * cand.shape[0] + entries), f32),
            jax.ShapeDtypeStruct((8, entries * per_tile), i32),
        ),
        compiler_params=settings(59),
        name="announce",
    )(tile_owners, cand, teacher)


def route_kernel(per_tile, tok_ref, codes_ref, hidden_ref, out_ref, rows_ref, held_ref):
    step = pl.program_id(0)
    width = hidden_ref.shape[0]
    owners, lanes, _ = held_ref.shape
    blocks = lanes // 8
    tokens = rows_ref.shape[1] // 2
    pairs = hidden_ref.shape[1] // (2 * tokens)
    steps = blocks // (2 * pairs)

    @pl.when(step == 0)
    def _():
        rows_ref[...] = rows_of(codes_ref[:, 0, :], per_tile)

    @pl.when(step < steps)
    def _():
        chunk = 32
        row = iota((chunk * 8, tokens), 0).astype(f32).astype(bf16)
        for pair in range(pairs):
            first = step * (2 * pairs) + 2 * pair
            rows = [rows_ref[pl.ds(first + w, 1), :] for w in range(2)]
            for at in range(0, owners, chunk):
                here = [(r - at * 8).astype(f32).astype(bf16) for r in rows]
                parts = []
                for which in range(2):
                    hot = jnp.where(
                        (row == here[which][:, 0:tokens])
                        | (row == here[which][:, tokens : 2 * tokens]),
                        jnp.ones_like(row),
                        jnp.zeros_like(row),
                    )
                    lane = (2 * pair + which) * tokens
                    part = by_rows(hot, hidden_ref[:, lane : lane + tokens])
                    parts.append(part.reshape(chunk, 8, width))
                held_ref[at : at + chunk, pl.ds(pl.multiple_of(first * 8, 16), 16), :] = (
                    jnp.concatenate(parts, axis=1).astype(bf16)
                )

    @pl.when(step >= steps)
    def _():
        count = out_ref.shape[0]
        for k in range(count):
            out_ref[k] = held_ref[(step - steps) * count + k].T


def route(tok, told, hidden, per_tile, blocks):
    width, total = hidden.shape
    owners = told.shape[0]
    tokens = total // blocks
    entries = 2 * tokens // per_tile
    pairs = 4
    steps = blocks // (2 * pairs)
    turn = 32
    return pl.pallas_call(
        functools.partial(route_kernel, per_tile),
        grid_spec=pltpu.PrefetchScalarGridSpec(
            num_scalar_prefetch=1,
            grid=(steps + owners // turn,),
            in_specs=[
                pl.BlockSpec((blocks, 1, entries), lambda s, t: (t[0], 0, told.shape[2] // entries - 1)),
                pl.BlockSpec(
                    (width, 2 * pairs * tokens), lambda s, t: (0, jnp.minimum(s, steps - 1))
                ),
            ],
            out_specs=pl.BlockSpec(
                (turn, width, blocks * 8), lambda s, t: (jnp.maximum(s - steps, 0), 0, 0)
            ),
            scratch_shapes=[
                pltpu.VMEM((blocks, 2 * tokens), i32),
                pltpu.VMEM((owners, blocks * 8, width), bf16),
            ],
        ),
        out_shape=jax.ShapeDtypeStruct((owners, width, blocks * 8), bf16),
        compiler_params=settings(59),
        name="route",
    )(tok, told, hidden)


def place_kernel(per_tile, owner_ref, told_ref, dense_ref, facts_ref):
    sources = told_ref.shape[0]
    lanes = sources * 8
    width = told_ref.shape[2] // 9
    turned = jnp.stack(
        [told_ref[:, 0, k * width : (k + 1) * width] for k in range(8)], axis=1
    ).reshape(lanes, width).T
    codes = jnp.broadcast_to(
        told_ref[:, :, 8 * width :], (sources, 8, width)
    ).reshape(lanes, width).T
    picks = width // 2
    columns = turned[0:picks].astype(i32) - 1
    teacher = turned[picks:]
    target = jnp.exp(teacher)
    panel = dense_ref.shape[0]
    chunk = 128
    place = iota((chunk, lanes), 0)
    for at in range(0, panel, chunk):
        dense = jnp.zeros((chunk, lanes), f32)
        for k in range(picks):
            dense = jnp.where(place == columns[k : k + 1] - at, target[k : k + 1], dense)
        dense_ref[at : at + chunk, :] = dense
    half = codes.shape[0] // 2
    other = jnp.concatenate([codes[half:], codes[:half]], axis=0)
    slot = (iota((1, lanes), 1) // per_tile) % 2
    mine = (owner_ref[0] * 2 + slot).astype(f32)
    partner = jnp.sum(jnp.where(codes == mine, other + 1.0, 0.0), axis=0, keepdims=True)
    mass = jnp.sum(target, axis=0, keepdims=True)
    entropy = jnp.sum(jnp.where(columns >= 0, target * teacher, 0.0), axis=0, keepdims=True)
    facts_ref[...] = jnp.concatenate(
        [partner, mass, entropy, jnp.zeros((5, lanes), f32)], axis=0
    )


def place(owner, told, panel, per_tile):
    sources, _, width = told.shape
    rows = sources * 8
    block = 16
    return pl.pallas_call(
        functools.partial(place_kernel, per_tile),
        grid_spec=pltpu.PrefetchScalarGridSpec(
            num_scalar_prefetch=1,
            grid=(sources // block,),
            in_specs=[pl.BlockSpec((block, 1, width), lambda s, o: (s, 0, 0))],
            out_specs=[
                pl.BlockSpec((panel, block * 8), lambda s, o: (0, s)),
                pl.BlockSpec((8, block * 8), lambda s, o: (0, s)),
            ],
        ),
        out_shape=(
            jax.ShapeDtypeStruct((panel, rows), f32),
            jax.ShapeDtypeStruct((8, rows), f32),
        ),
        compiler_params=settings(59),
        cost_estimate=pl.CostEstimate(
            flops=2 * 64 * panel * rows, bytes_accessed=8 * panel * rows, transcendentals=64 * rows
        ),
        name="place",
    )(owner, told)


def score_kernel(
    bounds, head_ref, rows_ref, dense_ref, facts_ref, part_ref, own_ref, told_ref,
    total_ref, head_held, rows_held, dense_held, part_held, sems, last_sem, out_sems
):
    groups, _, lanes = rows_ref.shape
    panel, count = total_ref.shape
    copies = []
    for k, (low, high) in enumerate(bounds):
        copies.append(
            (
                pltpu.make_async_copy(
                    head_ref.at[:, low:high], head_held.at[:, low:high], sems.at[0, k]
                ),
                pltpu.make_async_copy(
                    rows_ref.at[:, low:high, :], rows_held.at[:, low:high, :], sems.at[1, k]
                ),
            )
        )
    last = pltpu.make_async_copy(dense_ref, dense_held, last_sem)
    ahead = 4
    for pair in copies[:ahead]:
        pair[0].start()
        pair[1].start()
    for k, (low, high) in enumerate(bounds):
        if k + ahead < len(bounds):
            copies[k + ahead][0].start()
            copies[k + ahead][1].start()
        if k + ahead == len(bounds):
            last.start()
        copies[k][0].wait()
        copies[k][1].wait()
        for t in range(groups):
            here = slice(t * lanes, (t + 1) * lanes)
            product = plain(head_held[:, low:high], rows_held[t, low:high, :])
            total_ref[:, here] = product if k == 0 else total_ref[:, here] + product
    last.wait()
    chunk = 128
    logs, largest, shares, leave = [], [], [], []
    for k, at in enumerate(range(0, count, chunk)):
        here = slice(at, at + chunk)
        dense = dense_held[:, here]
        score = total_ref[:, here]
        named = dense > 0.0
        most = jnp.max(jnp.where(named, score, nothing), axis=0, keepdims=True)
        part = jnp.where(named, jnp.exp(score - most), 0.0)
        part_held[:, here] = part
        leave.append(
            pltpu.make_async_copy(part_held.at[:, here], part_ref.at[:, here], out_sems.at[k])
        )
        leave[-1].start()
        whole = jnp.sum(part, axis=0, keepdims=True)
        log = jnp.where(whole > 0.0, most + jnp.log(jnp.maximum(whole, 1.0)), nothing)
        shares.append(facts_ref[2:3, here] - jnp.sum(dense * score, axis=0, keepdims=True))
        logs.append(log)
        largest.append(most)
    logs = jnp.concatenate(logs, axis=1)
    largest = jnp.concatenate(largest, axis=1)
    own_ref[...] = jnp.concatenate([largest, logs, jnp.zeros((6, count), f32)], axis=0)
    owners = told_ref.shape[0]
    told_ref[:, 0, 0:count] = jnp.broadcast_to(logs, (owners, count))
    group = chunk // 8
    home = iota((group, chunk), 1) // 8 == iota((group, chunk), 0)
    which = (iota((chunk, chunk), 0) % 8 == iota((chunk, chunk), 1)).astype(f32)
    spread = [jnp.where(home, jnp.broadcast_to(share, (group, chunk)), 0.0) for share in shares]
    told_ref[:, 0, count : count + chunk] = plain(
        jnp.concatenate(spread, axis=0), which, HIGHEST
    )
    for copy in leave:
        copy.wait()


def score(head, rows, dense, facts, owners):
    panel, width = head.shape
    groups, _, lanes = rows.shape
    count = groups * lanes
    block = 1024
    cuts = [0, 512, 1280, 2560, 3840, 5120]
    bounds = list(zip(cuts[:-1], cuts[1:]))
    return pl.pallas_call(
        functools.partial(score_kernel, bounds),
        in_specs=[far, far, far, near],
        out_specs=[far, near, near],
        out_shape=(
            jax.ShapeDtypeStruct((panel, count), f32),
            jax.ShapeDtypeStruct((8, count), f32),
            jax.ShapeDtypeStruct((owners, 1, count + 128), f32),
        ),
        scratch_shapes=[
            pltpu.VMEM((panel, count), f32),
            pltpu.VMEM((panel, width), bf16),
            pltpu.VMEM((groups, width, lanes), bf16),
            pltpu.VMEM((panel, count), f32),
            pltpu.VMEM((panel, count), f32),
            pltpu.SemaphoreType.DMA((2, len(bounds))),
            pltpu.SemaphoreType.DMA,
            pltpu.SemaphoreType.DMA((count // 128,)),
        ],
        compiler_params=settings(59),
        name="score",
    )(head, rows, dense, facts)


def log_sum(a, b):
    most = jnp.maximum(a, b)
    return most + jnp.log(jnp.exp(a - most) + jnp.exp(b - most))


def turn_kernel(part_ref, dense_ref, part_out, dense_out):
    part_out[...] = part_ref[...].T
    dense_out[...] = (loss_weight * dense_ref[...]).T


def turn(part, dense):
    panel, count = part.shape
    block = 256
    columns = pl.BlockSpec((panel, block), lambda s: (0, s))
    rows = pl.BlockSpec((block, panel), lambda s: (s, 0))
    return pl.pallas_call(
        turn_kernel,
        grid=(count // block,),
        in_specs=[columns, columns],
        out_specs=[rows, rows],
        out_shape=[jax.ShapeDtypeStruct((count, panel), f32)] * 2,
        compiler_params=settings(59),
        cost_estimate=pl.CostEstimate(
            flops=4 * panel * count, bytes_accessed=16 * panel * count, transcendentals=0
        ),
        name="turn",
    )(part, dense)


def part_kernel(
    per_tile, logs_ref, facts_ref, own_ref, part_ref, dense_ref, head_ref, out_ref, weight_ref,
    logs_held, facts_held, own_held, part_held, dense_held, head_held, out_held,
    small_sems, sems, head_sems, out_sems
):
    count, panel = part_ref.shape
    owners = logs_ref.shape[0]
    chunk = 128
    small = [
        pltpu.make_async_copy(facts_ref, facts_held, small_sems.at[0]),
        pltpu.make_async_copy(own_ref, own_held, small_sems.at[1]),
        pltpu.make_async_copy(logs_ref, logs_held, small_sems.at[2]),
    ]
    for copy in small:
        copy.start()
    slots, _, block = out_held.shape
    blocks = out_ref.shape[1] // block
    tables, heads = [], []
    for k in range(count // chunk):
        here = slice(k * chunk, (k + 1) * chunk)
        tables.append(
            (
                pltpu.make_async_copy(part_ref.at[here], part_held.at[here], sems.at[0, k]),
                pltpu.make_async_copy(dense_ref.at[here], dense_held.at[here], sems.at[1, k]),
            )
        )
        tables[-1][0].start()
        tables[-1][1].start()
    for k in range(blocks):
        here = slice(k * block, (k + 1) * block)
        heads.append(
            pltpu.make_async_copy(head_ref.at[:, here], head_held.at[:, here], head_sems.at[k])
        )
    for copy in small:
        copy.wait()
    for k, at in enumerate(range(0, count, chunk)):
        here = slice(at, at + chunk)
        logs = logs_held[:, 0, here]
        partner = facts_held[0:1, here].astype(i32) - 1
        slot = (iota((1, chunk), 1) // per_tile) % 2
        across = jnp.where(
            slot == 0, pltpu.roll(logs, chunk - per_tile, 1), pltpu.roll(logs, per_tile, 1)
        )
        picked = jnp.where(
            iota((owners, chunk), 0) == partner // 2,
            jnp.where(partner % 2 == slot, logs, across),
            0.0,
        )
        other = jnp.sum(picked, axis=0, keepdims=True)
        total = log_sum(own_held[1:2, here], other)
        scale = loss_weight * facts_held[1:2, here] * jnp.exp(own_held[0:1, here] - total)
        scale = jnp.broadcast_to(scale, (chunk, chunk)).T
        tables[k][0].wait()
        tables[k][1].wait()
        if k == 0:
            for copy in heads[:2]:
                copy.start()
        for col in range(0, panel, chunk):
            there = slice(col, col + chunk)
            weight = part_held[here, there] * scale - dense_held[here, there]
            weight_ref[here, there] = weight.astype(bf16)
    leave = []
    for k in range(blocks):
        here = slice(k * block, (k + 1) * block)
        if k >= slots:
            leave[k - slots].wait()
        if k + 2 < blocks:
            heads[k + 2].start()
        heads[k].wait()
        out_held[k % slots] = plain(weight_ref[...], head_held[:, here]).astype(bf16)
        leave.append(
            pltpu.make_async_copy(out_held.at[k % slots], out_ref.at[:, here], out_sems.at[k % slots])
        )
        leave[-1].start()
    for copy in leave[blocks - slots :]:
        copy.wait()


def grad_parts(logs, facts, own, part, dense, head, per_tile):
    panel, width = head.shape
    count = part.shape[0]
    block = 1024
    return pl.pallas_call(
        functools.partial(part_kernel, per_tile),
        in_specs=[far] * 6,
        out_specs=[far, near],
        out_shape=(
            jax.ShapeDtypeStruct((count, width), bf16),
            jax.ShapeDtypeStruct((count, panel), bf16),
        ),
        scratch_shapes=[
            pltpu.VMEM(logs.shape, f32),
            pltpu.VMEM(facts.shape, f32),
            pltpu.VMEM(own.shape, f32),
            pltpu.VMEM((count, panel), f32),
            pltpu.VMEM((count, panel), f32),
            pltpu.VMEM((panel, width), bf16),
            pltpu.VMEM((2, count, block), bf16),
            pltpu.SemaphoreType.DMA((3,)),
            pltpu.SemaphoreType.DMA((2, count // 128)),
            pltpu.SemaphoreType.DMA((width // block,)),
            pltpu.SemaphoreType.DMA((2,)),
        ],
        compiler_params=settings(59),
        name="grad_parts",
    )(logs, facts, own, part, dense, head)


def head_kernel(weight_ref, rows_ref, out_ref, turned_ref):
    groups, _, lanes = rows_ref.shape

    @pl.when(pl.program_id(0) == 0)
    def _():
        for at in range(0, weight_ref.shape[0], 128):
            turned_ref[:, at : at + 128] = weight_ref[at : at + 128, :].T

    total = by_rows(turned_ref[:, 0:lanes], rows_ref[0])
    for t in range(1, groups):
        total = total + by_rows(turned_ref[:, t * lanes : (t + 1) * lanes], rows_ref[t])
    out_ref[...] = total.astype(bf16)


def grad_of_head(weight, rows):
    count, panel = weight.shape
    groups, width, lanes = rows.shape
    block = 512
    return pl.pallas_call(
        head_kernel,
        grid=(width // block,),
        in_specs=[
            pl.BlockSpec((count, panel), lambda s: (0, 0)),
            pl.BlockSpec((groups, block, lanes), lambda s: (0, s, 0)),
        ],
        out_specs=pl.BlockSpec((panel, block), lambda s: (0, s)),
        out_shape=jax.ShapeDtypeStruct((panel, width), bf16),
        scratch_shapes=[pltpu.VMEM((panel, count), bf16)],
        compiler_params=settings(),
        cost_estimate=pl.CostEstimate(
            flops=2 * panel * count * width,
            bytes_accessed=2 * (panel + count) * width,
            transcendentals=0,
        ),
        name="grad_of_head",
    )(weight, rows)


def loss_kernel(me_ref, logs_ref, rows_ref, teacher_ref, loss_ref, table_ref):
    owners = logs_ref.shape[0]
    tokens = teacher_ref.shape[1]
    count = table_ref.shape[1]
    mine = iota((count, 128), 0) == me_ref[0] * 8 + iota((count, 128), 1)
    mine = jnp.where(mine & (iota((count, 128), 1) < 8), 1.0, 0.0)
    logs = plain(logs_ref[:, 0, 0:count], mine, HIGHEST).T
    shares = logs_ref[:, 0, count : count + 128].T
    found = []
    total = jnp.zeros((1, tokens), f32)
    for group in range(2):
        row = rows_ref[0:1, group * tokens : (group + 1) * tokens]
        owner = jnp.where(iota((owners, tokens), 0) == row // 8, 1.0, 0.0)
        slot = iota((128, tokens), 0) == row % 8
        for table, kept in ((logs, True), (shares, False)):
            got = jnp.where(slot, plain(table, owner, HIGHEST), 0.0)
            got = jnp.sum(got, axis=0, keepdims=True)
            if kept:
                found.append(got)
            else:
                total = total + got
    teacher = teacher_ref[...]
    mass = jnp.sum(jnp.exp(teacher), axis=0, keepdims=True)
    loss_ref[...] = total + mass * log_sum(found[0], found[1])
    first, second = rows_ref[0:1, 0:tokens], rows_ref[0:1, tokens : 2 * tokens]
    for at in range(0, count, 128):
        row = iota((128, tokens), 0) + at
        hot = jnp.where((row == first) | (row == second), 1.0, 0.0)
        table_ref[:, at : at + 128] = hot.T.astype(bf16)


def losses(me, logs, rows, teacher, count):
    tokens = teacher.shape[1]
    return pl.pallas_call(
        loss_kernel,
        in_specs=[pl.BlockSpec(memory_space=pltpu.SMEM)] + [pl.BlockSpec(memory_space=pltpu.VMEM)] * 3,
        out_shape=(
            jax.ShapeDtypeStruct((1, tokens), f32),
            jax.ShapeDtypeStruct((tokens, count), bf16),
        ),
        compiler_params=settings(59),
        cost_estimate=pl.CostEstimate(
            flops=12 * 2 * count * tokens * 128, bytes_accessed=4 * count * tokens, transcendentals=0
        ),
        name="losses",
    )(me, logs, rows, teacher)


def combine_kernel(table_ref, parts_ref, out_ref):
    out_ref[...] = plain(table_ref[...], parts_ref[...]).astype(bf16)


def combine(table, parts):
    tokens, count = table.shape
    width = parts.shape[1]
    block = width // 2
    return pl.pallas_call(
        combine_kernel,
        grid=(width // block,),
        in_specs=[
            pl.BlockSpec((tokens, count), lambda s: (0, 0)),
            pl.BlockSpec((count, block), lambda s: (0, s)),
        ],
        out_specs=pl.BlockSpec((tokens, block), lambda s: (0, s)),
        out_shape=jax.ShapeDtypeStruct((tokens, width), bf16),
        compiler_params=settings(59),
        name="combine",
    )(table, parts)


def exchange(values):
    return lax.all_to_all(values, ("tok", "voc"), split_axis=0, concat_axis=0, tiled=True)


def body(hidden, head_weight, tile_owners, cand_pos, teacher_logp):
    panel, width = head_weight.shape
    tiles = tile_owners.shape[0]
    tokens = cand_pos.shape[0]
    per_tile = tokens // tiles
    tok_size, blocks = lax.axis_size("tok"), lax.axis_size("voc")
    owners = tok_size * blocks
    count = owners * 8
    tok = lax.axis_index("tok")
    me = (tok * blocks + lax.axis_index("voc")).astype(i32).reshape(1)
    teacher = teacher_logp.T
    told, home_rows = announce(tile_owners.T, cand_pos.T, teacher, panel, per_tile, owners)
    told = exchange(told)
    sent = route(tok.astype(i32).reshape(1), told, hidden.T, per_tile, blocks)
    rows = exchange(sent).reshape(tok_size, width, blocks * 8)
    dense, facts = place(me, told, panel, per_tile)
    part, own, logs = score(head_weight, rows, dense, facts, owners)
    logs = exchange(logs)
    part_rows, dense_rows = turn(part, dense)
    parts, weight = grad_parts(logs, facts, own, part_rows, dense_rows, head_weight, per_tile)
    home_parts = exchange(parts.reshape(owners, 8, width)).reshape(count, width)
    grad_head = grad_of_head(weight, rows)
    loss, table = losses(me, logs, home_rows, teacher, count)
    grad_hidden = combine(table, home_parts)
    return (loss.reshape(tokens), grad_hidden, grad_head)


def solution(mesh):
    placed = (
        P("tok", "voc"),
        P(("tok", "voc"), None),
        P(("tok", "voc"), None),
        P(("tok", "voc"), None),
        P(("tok", "voc"), None),
    )
    return jax.shard_map(
        body,
        mesh=mesh,
        in_specs=placed,
        out_specs=(P(("tok", "voc")), P(("tok", "voc"), None), P(("tok", "voc"), None)),
        check_vma=False,
    )
```

```python
import functools

import jax
import jax.numpy as jnp
from jax import lax
from jax.experimental import pallas as pl
from jax.experimental.pallas import tpu as pltpu
from jax.sharding import PartitionSpec as P

loss_weight = 16.0
nothing = -1e30
f32, bf16, i32 = jnp.float32, jnp.bfloat16, jnp.int32
HIGHEST = lax.Precision.HIGHEST


near, far = pl.BlockSpec(memory_space=pltpu.VMEM), pl.BlockSpec(memory_space=pl.ANY)


def settings(mib=32):
    return pltpu.CompilerParams(vmem_limit_bytes=mib * 1024 * 1024)


def by_rows(a, b, precision=None):
    return lax.dot_general(
        a, b, (((1,), (1,)), ((), ())), preferred_element_type=f32, precision=precision
    )


def plain(a, b, precision=None):
    return lax.dot_general(
        a, b, (((1,), (0,)), ((), ())), preferred_element_type=f32, precision=precision
    )


def iota(shape, dim):
    return lax.broadcasted_iota(i32, shape, dim)


def rows_of(codes, per_tile):
    entries = codes.shape[1]
    wide = entries * per_tile
    spread = (iota((entries, wide), 0) == iota((entries, wide), 1) // per_tile).astype(bf16)
    expanded = plain(codes.astype(bf16), spread).astype(i32)
    return expanded * per_tile + iota(expanded.shape, 1) % per_tile


def announce_kernel(panel, per_tile, owner_ref, cand_ref, teacher_ref, out_ref, rows_ref):
    tiles = owner_ref.shape[1]
    entries = 2 * tiles
    tokens = tiles * per_tile
    slots = out_ref.shape[0]
    owner = jnp.concatenate([owner_ref[0:1, :], owner_ref[1:2, :]], axis=1).astype(f32)
    owners = jnp.broadcast_to(owner, (entries, entries))
    earlier = iota((entries, entries), 0) % tiles < iota((entries, entries), 1) % tiles
    same = (owners == owners.T) & earlier
    rank = jnp.sum(jnp.where(same, 1.0, 0.0), axis=0, keepdims=True)
    code = owner * 2.0 + rank
    rows = rows_of(jnp.broadcast_to(code, (8, entries)), per_tile)
    rows_ref[...] = rows
    cand = cand_ref[...]
    first = teacher_ref[...].astype(bf16)
    rest = teacher_ref[...] - first.astype(f32)
    second = rest.astype(bf16)
    third = (rest - second.astype(f32)).astype(bf16)
    sides = []
    for column in (
        jnp.where(cand < panel, cand + 1, 0),
        jnp.where(cand >= panel, cand - panel + 1, 0),
    ):
        high, low = column // 32, column % 32
        sides.append(
            jnp.concatenate(
                [
                    high.astype(f32).astype(bf16),
                    first,
                    low.astype(f32).astype(bf16),
                    second,
                    jnp.zeros_like(first),
                    third,
                ],
                axis=0,
            )
        )
    sides = jnp.concatenate(sides, axis=1)
    width = 2 * cand.shape[0]
    times = jnp.where(iota((slots, width), 1) < cand.shape[0], 32.0, 1.0)
    for which in range(8):
        row = iota((slots, 2 * tokens), 0) * 8 + which
        hot = jnp.where(row == rows[0:1, :], 1.0, 0.0).astype(bf16)
        told = by_rows(hot, sides)
        out_ref[:, 0, which * width : (which + 1) * width] = (
            told[:, 0:width] * times + told[:, width : 2 * width] + told[:, 2 * width :]
        )
    out_ref[:, 0, 8 * width : 8 * width + entries] = jnp.broadcast_to(code, (slots, entries))


def announce(tile_owners, cand, teacher, panel, per_tile, owners):
    entries = 2 * tile_owners.shape[1]
    return pl.pallas_call(
        functools.partial(announce_kernel, panel, per_tile),
        out_shape=(
            jax.ShapeDtypeStruct((owners, 1, 16 * cand.shape[0] + entries), f32),
            jax.ShapeDtypeStruct((8, entries * per_tile), i32),
        ),
        compiler_params=settings(59),
        name="announce",
    )(tile_owners, cand, teacher)


def route_kernel(
    per_tile, tok_ref, codes_ref, hidden_ref, told_ref, out_ref, kept_ref, rows_ref, held_ref, pass_ref, sems
):
    step = pl.program_id(0)
    width = hidden_ref.shape[0]
    owners, lanes, _ = held_ref.shape
    blocks = lanes // 8
    tokens = rows_ref.shape[1] // 2
    pairs = hidden_ref.shape[1] // (2 * tokens)
    steps = blocks // (2 * pairs)

    @pl.when(step == 0)
    def _():
        rows_ref[...] = rows_of(codes_ref[:, 0, :], per_tile)
        pltpu.make_async_copy(told_ref, pass_ref, sems.at[0]).start()

    @pl.when(step < steps)
    def _():
        chunk = 32
        row = iota((chunk * 8, tokens), 0).astype(f32).astype(bf16)
        for pair in range(pairs):
            first = step * (2 * pairs) + 2 * pair
            rows = [rows_ref[pl.ds(first + w, 1), :] for w in range(2)]
            for at in range(0, owners, chunk):
                here = [(r - at * 8).astype(f32).astype(bf16) for r in rows]
                parts = []
                for which in range(2):
                    hot = jnp.where(
                        (row == here[which][:, 0:tokens])
                        | (row == here[which][:, tokens : 2 * tokens]),
                        jnp.ones_like(row),
                        jnp.zeros_like(row),
                    )
                    lane = (2 * pair + which) * tokens
                    part = by_rows(hot, hidden_ref[:, lane : lane + tokens])
                    parts.append(part.reshape(chunk, 8, width))
                held_ref[at : at + chunk, pl.ds(pl.multiple_of(first * 8, 16), 16), :] = (
                    jnp.concatenate(parts, axis=1).astype(bf16)
                )

    @pl.when(step >= steps)
    def _():
        count = out_ref.shape[0]
        for k in range(count):
            out_ref[k] = held_ref[(step - steps) * count + k].T

    @pl.when(step == 1)
    def _():
        pltpu.make_async_copy(told_ref, pass_ref, sems.at[0]).wait()
        pltpu.make_async_copy(pass_ref, kept_ref, sems.at[1]).start()

    @pl.when(step == pl.num_programs(0) - 1)
    def _():
        pltpu.make_async_copy(pass_ref, kept_ref, sems.at[1]).wait()


def route(tok, told, hidden, per_tile, blocks):
    width, total = hidden.shape
    owners = told.shape[0]
    tokens = total // blocks
    entries = 2 * tokens // per_tile
    pairs = 4
    steps = blocks // (2 * pairs)
    turn = 32
    return pl.pallas_call(
        functools.partial(route_kernel, per_tile),
        grid_spec=pltpu.PrefetchScalarGridSpec(
            num_scalar_prefetch=1,
            grid=(steps + owners // turn,),
            in_specs=[
                pl.BlockSpec((blocks, 1, entries), lambda s, t: (t[0], 0, told.shape[2] // entries - 1)),
                pl.BlockSpec(
                    (width, 2 * pairs * tokens), lambda s, t: (0, jnp.minimum(s, steps - 1))
                ),
                far,
            ],
            out_specs=[
                pl.BlockSpec(
                    (turn, width, blocks * 8), lambda s, t: (jnp.maximum(s - steps, 0), 0, 0)
                ),
                far,
            ],
            scratch_shapes=[
                pltpu.VMEM((blocks, 2 * tokens), i32),
                pltpu.VMEM((owners, blocks * 8, width), bf16),
                pltpu.VMEM(told.shape, f32),
                pltpu.SemaphoreType.DMA((2,)),
            ],
        ),
        out_shape=(
            jax.ShapeDtypeStruct((owners, width, blocks * 8), bf16),
            jax.ShapeDtypeStruct(told.shape, f32),
        ),
        compiler_params=settings(59),
        name="route",
    )(tok, told, hidden, told)


def place_kernel(per_tile, owner_ref, told_ref, dense_ref, facts_ref):
    sources = told_ref.shape[0]
    lanes = sources * 8
    width = told_ref.shape[2] // 9
    turned = jnp.stack(
        [told_ref[:, 0, k * width : (k + 1) * width] for k in range(8)], axis=1
    ).reshape(lanes, width).T
    codes = jnp.broadcast_to(
        told_ref[:, :, 8 * width :], (sources, 8, width)
    ).reshape(lanes, width).T
    picks = width // 2
    columns = turned[0:picks].astype(i32) - 1
    teacher = turned[picks:]
    target = jnp.exp(teacher)
    panel = dense_ref.shape[0]
    chunk = 128
    place = iota((chunk, lanes), 0)
    for at in range(0, panel, chunk):
        dense = jnp.zeros((chunk, lanes), f32)
        for k in range(picks):
            dense = jnp.where(place == columns[k : k + 1] - at, target[k : k + 1], dense)
        dense_ref[at : at + chunk, :] = dense
    half = codes.shape[0] // 2
    other = jnp.concatenate([codes[half:], codes[:half]], axis=0)
    slot = (iota((1, lanes), 1) // per_tile) % 2
    mine = (owner_ref[0] * 2 + slot).astype(f32)
    partner = jnp.sum(jnp.where(codes == mine, other + 1.0, 0.0), axis=0, keepdims=True)
    mass = jnp.sum(target, axis=0, keepdims=True)
    entropy = jnp.sum(jnp.where(columns >= 0, target * teacher, 0.0), axis=0, keepdims=True)
    facts_ref[...] = jnp.concatenate(
        [partner, mass, entropy, jnp.zeros((5, lanes), f32)], axis=0
    )


def place(owner, told, panel, per_tile):
    sources, _, width = told.shape
    rows = sources * 8
    block = 16
    return pl.pallas_call(
        functools.partial(place_kernel, per_tile),
        grid_spec=pltpu.PrefetchScalarGridSpec(
            num_scalar_prefetch=1,
            grid=(sources // block,),
            in_specs=[pl.BlockSpec((block, 1, width), lambda s, o: (s, 0, 0))],
            out_specs=[
                pl.BlockSpec((panel, block * 8), lambda s, o: (0, s)),
                pl.BlockSpec((8, block * 8), lambda s, o: (0, s)),
            ],
        ),
        out_shape=(
            jax.ShapeDtypeStruct((panel, rows), f32),
            jax.ShapeDtypeStruct((8, rows), f32),
        ),
        compiler_params=settings(59),
        cost_estimate=pl.CostEstimate(
            flops=2 * 64 * panel * rows, bytes_accessed=8 * panel * rows, transcendentals=64 * rows
        ),
        name="place",
    )(owner, told)


def score_kernel(
    bounds, head_ref, rows_ref, dense_ref, facts_ref, part_ref, own_ref, told_ref,
    total_ref, head_held, rows_held, dense_held, part_held, sems, last_sem, out_sems
):
    groups, _, lanes = rows_ref.shape
    panel, count = total_ref.shape
    copies = []
    for k, (low, high) in enumerate(bounds):
        copies.append(
            (
                pltpu.make_async_copy(
                    head_ref.at[:, low:high], head_held.at[:, low:high], sems.at[0, k]
                ),
                pltpu.make_async_copy(
                    rows_ref.at[:, low:high, :], rows_held.at[:, low:high, :], sems.at[1, k]
                ),
            )
        )
    last = pltpu.make_async_copy(dense_ref, dense_held, last_sem)
    ahead = 4
    for pair in copies[:ahead]:
        pair[0].start()
        pair[1].start()
    for k, (low, high) in enumerate(bounds):
        if k + ahead < len(bounds):
            copies[k + ahead][0].start()
            copies[k + ahead][1].start()
        if k + ahead == len(bounds):
            last.start()
        copies[k][0].wait()
        copies[k][1].wait()
        for t in range(groups):
            here = slice(t * lanes, (t + 1) * lanes)
            product = plain(head_held[:, low:high], rows_held[t, low:high, :])
            total_ref[:, here] = product if k == 0 else total_ref[:, here] + product
    last.wait()
    chunk = 128
    logs, largest, shares, leave = [], [], [], []
    for k, at in enumerate(range(0, count, chunk)):
        here = slice(at, at + chunk)
        dense = dense_held[:, here]
        score = total_ref[:, here]
        named = dense > 0.0
        most = jnp.max(jnp.where(named, score, nothing), axis=0, keepdims=True)
        part = jnp.where(named, jnp.exp(score - most), 0.0)
        part_held[:, here] = part
        leave.append(
            pltpu.make_async_copy(part_held.at[:, here], part_ref.at[:, here], out_sems.at[k])
        )
        leave[-1].start()
        whole = jnp.sum(part, axis=0, keepdims=True)
        log = jnp.where(whole > 0.0, most + jnp.log(jnp.maximum(whole, 1.0)), nothing)
        shares.append(facts_ref[2:3, here] - jnp.sum(dense * score, axis=0, keepdims=True))
        logs.append(log)
        largest.append(most)
    logs = jnp.concatenate(logs, axis=1)
    largest = jnp.concatenate(largest, axis=1)
    own_ref[...] = jnp.concatenate([largest, logs, jnp.zeros((6, count), f32)], axis=0)
    owners = told_ref.shape[0]
    told_ref[:, 0, 0:count] = jnp.broadcast_to(logs, (owners, count))
    group = chunk // 8
    home = iota((group, chunk), 1) // 8 == iota((group, chunk), 0)
    which = (iota((chunk, chunk), 0) % 8 == iota((chunk, chunk), 1)).astype(f32)
    spread = [jnp.where(home, jnp.broadcast_to(share, (group, chunk)), 0.0) for share in shares]
    told_ref[:, 0, count : count + chunk] = plain(
        jnp.concatenate(spread, axis=0), which, HIGHEST
    )
    for copy in leave:
        copy.wait()


def score(head, rows, dense, facts, owners):
    panel, width = head.shape
    groups, _, lanes = rows.shape
    count = groups * lanes
    block = 1024
    cuts = [0, 512, 1280, 2560, 3840, 5120]
    bounds = list(zip(cuts[:-1], cuts[1:]))
    return pl.pallas_call(
        functools.partial(score_kernel, bounds),
        in_specs=[far, far, far, near],
        out_specs=[far, near, near],
        out_shape=(
            jax.ShapeDtypeStruct((panel, count), f32),
            jax.ShapeDtypeStruct((8, count), f32),
            jax.ShapeDtypeStruct((owners, 1, count + 128), f32),
        ),
        scratch_shapes=[
            pltpu.VMEM((panel, count), f32),
            pltpu.VMEM((panel, width), bf16),
            pltpu.VMEM((groups, width, lanes), bf16),
            pltpu.VMEM((panel, count), f32),
            pltpu.VMEM((panel, count), f32),
            pltpu.SemaphoreType.DMA((2, len(bounds))),
            pltpu.SemaphoreType.DMA,
            pltpu.SemaphoreType.DMA((count // 128,)),
        ],
        compiler_params=settings(59),
        name="score",
    )(head, rows, dense, facts)


def log_sum(a, b):
    most = jnp.maximum(a, b)
    return most + jnp.log(jnp.exp(a - most) + jnp.exp(b - most))


def turn_kernel(part_ref, dense_ref, part_out, dense_out):
    part_out[...] = part_ref[...].T
    dense_out[...] = (loss_weight * dense_ref[...]).T


def turn(part, dense):
    panel, count = part.shape
    block = 256
    columns = pl.BlockSpec((panel, block), lambda s: (0, s))
    rows = pl.BlockSpec((block, panel), lambda s: (s, 0))
    return pl.pallas_call(
        turn_kernel,
        grid=(count // block,),
        in_specs=[columns, columns],
        out_specs=[rows, rows],
        out_shape=[jax.ShapeDtypeStruct((count, panel), f32)] * 2,
        compiler_params=settings(59),
        cost_estimate=pl.CostEstimate(
            flops=4 * panel * count, bytes_accessed=16 * panel * count, transcendentals=0
        ),
        name="turn",
    )(part, dense)


def part_kernel(
    per_tile, logs_ref, facts_ref, own_ref, part_ref, dense_ref, head_ref, out_ref, weight_ref, kept_ref,
    logs_held, facts_held, own_held, part_held, dense_held, head_held, out_held,
    small_sems, kept_sem, sems, head_sems, out_sems
):
    count, panel = part_ref.shape
    owners = logs_ref.shape[0]
    chunk = 128
    small = [
        pltpu.make_async_copy(facts_ref, facts_held, small_sems.at[0]),
        pltpu.make_async_copy(own_ref, own_held, small_sems.at[1]),
        pltpu.make_async_copy(logs_ref, logs_held, small_sems.at[2]),
    ]
    for copy in small:
        copy.start()
    slots, _, block = out_held.shape
    blocks = out_ref.shape[1] // block
    tables, heads = [], []
    for k in range(count // chunk):
        here = slice(k * chunk, (k + 1) * chunk)
        tables.append(
            (
                pltpu.make_async_copy(part_ref.at[here], part_held.at[here], sems.at[0, k]),
                pltpu.make_async_copy(dense_ref.at[here], dense_held.at[here], sems.at[1, k]),
            )
        )
        tables[-1][0].start()
        tables[-1][1].start(priority=1)
    for k in range(blocks):
        here = slice(k * block, (k + 1) * block)
        heads.append(
            pltpu.make_async_copy(head_ref.at[:, here], head_held.at[:, here], head_sems.at[k])
        )
    for copy in small:
        copy.wait()
    keep = pltpu.make_async_copy(logs_held, kept_ref, kept_sem)
    keep.start(priority=1)
    for k, at in enumerate(range(0, count, chunk)):
        here = slice(at, at + chunk)
        logs = logs_held[:, 0, here]
        partner = facts_held[0:1, here].astype(i32) - 1
        slot = (iota((1, chunk), 1) // per_tile) % 2
        across = jnp.where(
            slot == 0, pltpu.roll(logs, chunk - per_tile, 1), pltpu.roll(logs, per_tile, 1)
        )
        picked = jnp.where(
            iota((owners, chunk), 0) == partner // 2,
            jnp.where(partner % 2 == slot, logs, across),
            0.0,
        )
        other = jnp.sum(picked, axis=0, keepdims=True)
        total = log_sum(own_held[1:2, here], other)
        scale = loss_weight * facts_held[1:2, here] * jnp.exp(own_held[0:1, here] - total)
        scale = jnp.broadcast_to(scale, (chunk, chunk)).T
        tables[k][0].wait()
        tables[k][1].wait()
        if k == 0:
            for copy in heads[:2]:
                copy.start()
        for col in range(0, panel, chunk):
            there = slice(col, col + chunk)
            weight = part_held[here, there] * scale - dense_held[here, there]
            weight_ref[here, there] = weight.astype(bf16)
    leave = []
    for k in range(blocks):
        here = slice(k * block, (k + 1) * block)
        if k >= slots:
            leave[k - slots].wait()
        if k + 2 < blocks:
            heads[k + 2].start()
        heads[k].wait()
        out_held[k % slots] = plain(weight_ref[...], head_held[:, here]).astype(bf16)
        leave.append(
            pltpu.make_async_copy(out_held.at[k % slots], out_ref.at[:, here], out_sems.at[k % slots])
        )
        leave[-1].start(priority=1)
    for copy in leave[blocks - slots :]:
        copy.wait()
    keep.wait()


def grad_parts(logs, facts, own, part, dense, head, per_tile):
    panel, width = head.shape
    count = part.shape[0]
    block = 1024
    return pl.pallas_call(
        functools.partial(part_kernel, per_tile),
        in_specs=[far] * 6,
        out_specs=[far, near, far],
        out_shape=(
            jax.ShapeDtypeStruct((count, width), bf16),
            jax.ShapeDtypeStruct((count, panel), bf16),
            jax.ShapeDtypeStruct(logs.shape, f32),
        ),
        scratch_shapes=[
            pltpu.VMEM(logs.shape, f32),
            pltpu.VMEM(facts.shape, f32),
            pltpu.VMEM(own.shape, f32),
            pltpu.VMEM((count, panel), f32),
            pltpu.VMEM((count, panel), f32),
            pltpu.VMEM((panel, width), bf16),
            pltpu.VMEM((2, count, block), bf16),
            pltpu.SemaphoreType.DMA((3,)),
            pltpu.SemaphoreType.DMA,
            pltpu.SemaphoreType.DMA((2, count // 128)),
            pltpu.SemaphoreType.DMA((width // block,)),
            pltpu.SemaphoreType.DMA((2,)),
        ],
        compiler_params=settings(59),
        name="grad_parts",
    )(logs, facts, own, part, dense, head)


def head_kernel(weight_ref, rows_ref, out_ref, turned_ref):
    groups, _, lanes = rows_ref.shape

    @pl.when(pl.program_id(0) == 0)
    def _():
        for at in range(0, weight_ref.shape[0], 128):
            turned_ref[:, at : at + 128] = weight_ref[at : at + 128, :].T

    total = by_rows(turned_ref[:, 0:lanes], rows_ref[0])
    for t in range(1, groups):
        total = total + by_rows(turned_ref[:, t * lanes : (t + 1) * lanes], rows_ref[t])
    out_ref[...] = total.astype(bf16)


def grad_of_head(weight, rows):
    count, panel = weight.shape
    groups, width, lanes = rows.shape
    block = 512
    return pl.pallas_call(
        head_kernel,
        grid=(width // block,),
        in_specs=[
            pl.BlockSpec((count, panel), lambda s: (0, 0)),
            pl.BlockSpec((groups, block, lanes), lambda s: (0, s, 0)),
        ],
        out_specs=pl.BlockSpec((panel, block), lambda s: (0, s)),
        out_shape=jax.ShapeDtypeStruct((panel, width), bf16),
        scratch_shapes=[pltpu.VMEM((panel, count), bf16)],
        compiler_params=settings(),
        cost_estimate=pl.CostEstimate(
            flops=2 * panel * count * width,
            bytes_accessed=2 * (panel + count) * width,
            transcendentals=0,
        ),
        name="grad_of_head",
    )(weight, rows)


def loss_kernel(me_ref, logs_ref, rows_ref, teacher_ref, loss_ref, table_ref):
    owners = logs_ref.shape[0]
    tokens = teacher_ref.shape[1]
    count = table_ref.shape[1]
    mine = iota((count, 128), 0) == me_ref[0] * 8 + iota((count, 128), 1)
    mine = jnp.where(mine & (iota((count, 128), 1) < 8), 1.0, 0.0)
    logs = plain(logs_ref[:, 0, 0:count], mine, HIGHEST).T
    shares = logs_ref[:, 0, count : count + 128].T
    found = []
    total = jnp.zeros((1, tokens), f32)
    for group in range(2):
        row = rows_ref[0:1, group * tokens : (group + 1) * tokens]
        owner = jnp.where(iota((owners, tokens), 0) == row // 8, 1.0, 0.0)
        slot = iota((128, tokens), 0) == row % 8
        for table, kept in ((logs, True), (shares, False)):
            got = jnp.where(slot, plain(table, owner, HIGHEST), 0.0)
            got = jnp.sum(got, axis=0, keepdims=True)
            if kept:
                found.append(got)
            else:
                total = total + got
    teacher = teacher_ref[...]
    mass = jnp.sum(jnp.exp(teacher), axis=0, keepdims=True)
    loss_ref[...] = total + mass * log_sum(found[0], found[1])
    first, second = rows_ref[0:1, 0:tokens], rows_ref[0:1, tokens : 2 * tokens]
    for at in range(0, count, 128):
        row = iota((128, tokens), 0) + at
        hot = jnp.where((row == first) | (row == second), 1.0, 0.0)
        table_ref[:, at : at + 128] = hot.T.astype(bf16)


def losses(me, logs, rows, teacher, count):
    tokens = teacher.shape[1]
    return pl.pallas_call(
        loss_kernel,
        in_specs=[pl.BlockSpec(memory_space=pltpu.SMEM)] + [pl.BlockSpec(memory_space=pltpu.VMEM)] * 3,
        out_shape=(
            jax.ShapeDtypeStruct((1, tokens), f32),
            jax.ShapeDtypeStruct((tokens, count), bf16),
        ),
        compiler_params=settings(59),
        cost_estimate=pl.CostEstimate(
            flops=12 * 2 * count * tokens * 128, bytes_accessed=4 * count * tokens, transcendentals=0
        ),
        name="losses",
    )(me, logs, rows, teacher)


def combine_kernel(table_ref, parts_ref, out_ref):
    out_ref[...] = plain(table_ref[...], parts_ref[...]).astype(bf16)


def combine(table, parts):
    tokens, count = table.shape
    width = parts.shape[1]
    block = width // 2
    return pl.pallas_call(
        combine_kernel,
        grid=(width // block,),
        in_specs=[
            pl.BlockSpec((tokens, count), lambda s: (0, 0)),
            pl.BlockSpec((count, block), lambda s: (0, s)),
        ],
        out_specs=pl.BlockSpec((tokens, block), lambda s: (0, s)),
        out_shape=jax.ShapeDtypeStruct((tokens, width), bf16),
        compiler_params=settings(59),
        name="combine",
    )(table, parts)


def exchange(values):
    return lax.all_to_all(values, ("tok", "voc"), split_axis=0, concat_axis=0, tiled=True)


def body(hidden, head_weight, tile_owners, cand_pos, teacher_logp):
    panel, width = head_weight.shape
    tiles = tile_owners.shape[0]
    tokens = cand_pos.shape[0]
    per_tile = tokens // tiles
    tok_size, blocks = lax.axis_size("tok"), lax.axis_size("voc")
    owners = tok_size * blocks
    count = owners * 8
    tok = lax.axis_index("tok")
    me = (tok * blocks + lax.axis_index("voc")).astype(i32).reshape(1)
    teacher = teacher_logp.T
    told, home_rows = announce(tile_owners.T, cand_pos.T, teacher, panel, per_tile, owners)
    told = exchange(told)
    sent, told = route(tok.astype(i32).reshape(1), told, hidden.T, per_tile, blocks)
    rows = exchange(sent).reshape(tok_size, width, blocks * 8)
    dense, facts = place(me, told, panel, per_tile)
    part, own, logs = score(head_weight, rows, dense, facts, owners)
    logs = exchange(logs)
    part_rows, dense_rows = turn(part, dense)
    parts, weight, logs = grad_parts(logs, facts, own, part_rows, dense_rows, head_weight, per_tile)
    home_parts = exchange(parts.reshape(owners, 8, width)).reshape(count, width)
    grad_head = grad_of_head(weight, rows)
    loss, table = losses(me, logs, home_rows, teacher, count)
    grad_hidden = combine(table, home_parts)
    return (loss.reshape(tokens), grad_hidden, grad_head)


def solution(mesh):
    placed = (
        P("tok", "voc"),
        P(("tok", "voc"), None),
        P(("tok", "voc"), None),
        P(("tok", "voc"), None),
        P(("tok", "voc"), None),
    )
    return jax.shard_map(
        body,
        mesh=mesh,
        in_specs=placed,
        out_specs=(P(("tok", "voc")), P(("tok", "voc"), None), P(("tok", "voc"), None)),
        check_vma=False,
    )
```

```python
import functools

import jax
import jax.numpy as jnp
from jax import lax
from jax.experimental import pallas as pl
from jax.experimental.pallas import tpu as pltpu
from jax.sharding import PartitionSpec as P

loss_weight = 16.0
nothing = -1e30
f32, bf16, i32 = jnp.float32, jnp.bfloat16, jnp.int32
HIGHEST = lax.Precision.HIGHEST


near, far = pl.BlockSpec(memory_space=pltpu.VMEM), pl.BlockSpec(memory_space=pl.ANY)


def settings(mib=32):
    return pltpu.CompilerParams(vmem_limit_bytes=mib * 1024 * 1024)


def by_rows(a, b, precision=None):
    return lax.dot_general(
        a, b, (((1,), (1,)), ((), ())), preferred_element_type=f32, precision=precision
    )


def plain(a, b, precision=None):
    return lax.dot_general(
        a, b, (((1,), (0,)), ((), ())), preferred_element_type=f32, precision=precision
    )


def iota(shape, dim):
    return lax.broadcasted_iota(i32, shape, dim)


def rows_of(codes, per_tile):
    entries = codes.shape[1]
    wide = entries * per_tile
    spread = (iota((entries, wide), 0) == iota((entries, wide), 1) // per_tile).astype(bf16)
    expanded = plain(codes.astype(bf16), spread).astype(i32)
    return expanded * per_tile + iota(expanded.shape, 1) % per_tile


def announce_kernel(panel, per_tile, owner_ref, cand_ref, teacher_ref, out_ref, rows_ref):
    tiles = owner_ref.shape[1]
    entries = 2 * tiles
    tokens = tiles * per_tile
    slots = out_ref.shape[0]
    owner = jnp.concatenate([owner_ref[0:1, :], owner_ref[1:2, :]], axis=1).astype(f32)
    owners = jnp.broadcast_to(owner, (entries, entries))
    earlier = iota((entries, entries), 0) % tiles < iota((entries, entries), 1) % tiles
    same = (owners == owners.T) & earlier
    rank = jnp.sum(jnp.where(same, 1.0, 0.0), axis=0, keepdims=True)
    code = owner * 2.0 + rank
    rows = rows_of(jnp.broadcast_to(code, (8, entries)), per_tile)
    rows_ref[...] = rows
    cand = cand_ref[...]
    first = teacher_ref[...].astype(bf16)
    rest = teacher_ref[...] - first.astype(f32)
    second = rest.astype(bf16)
    third = (rest - second.astype(f32)).astype(bf16)
    sides = []
    for column in (
        jnp.where(cand < panel, cand + 1, 0),
        jnp.where(cand >= panel, cand - panel + 1, 0),
    ):
        high, low = column // 32, column % 32
        sides.append(
            jnp.concatenate(
                [
                    high.astype(f32).astype(bf16),
                    first,
                    low.astype(f32).astype(bf16),
                    second,
                    jnp.zeros_like(first),
                    third,
                ],
                axis=0,
            )
        )
    sides = jnp.concatenate(sides, axis=1)
    width = 2 * cand.shape[0]
    times = jnp.where(iota((slots, width), 1) < cand.shape[0], 32.0, 1.0)
    for which in range(8):
        row = iota((slots, 2 * tokens), 0) * 8 + which
        hot = jnp.where(row == rows[0:1, :], 1.0, 0.0).astype(bf16)
        told = by_rows(hot, sides)
        out_ref[:, 0, which * width : (which + 1) * width] = (
            told[:, 0:width] * times + told[:, width : 2 * width] + told[:, 2 * width :]
        )
    out_ref[:, 0, 8 * width : 8 * width + entries] = jnp.broadcast_to(code, (slots, entries))


def announce(tile_owners, cand, teacher, panel, per_tile, owners):
    entries = 2 * tile_owners.shape[1]
    return pl.pallas_call(
        functools.partial(announce_kernel, panel, per_tile),
        out_shape=(
            jax.ShapeDtypeStruct((owners, 1, 16 * cand.shape[0] + entries), f32),
            jax.ShapeDtypeStruct((8, entries * per_tile), i32),
        ),
        compiler_params=settings(59),
        name="announce",
    )(tile_owners, cand, teacher)


def route_kernel(
    per_tile, tok_ref, codes_ref, hidden_ref, told_ref, out_ref, kept_ref, rows_ref, held_ref, pass_ref, sems
):
    step = pl.program_id(0)
    width = hidden_ref.shape[0]
    owners, lanes, _ = held_ref.shape
    blocks = lanes // 8
    tokens = rows_ref.shape[1] // 2
    pairs = hidden_ref.shape[1] // (2 * tokens)
    steps = blocks // (2 * pairs)

    @pl.when(step == 0)
    def _():
        rows_ref[...] = rows_of(codes_ref[:, 0, :], per_tile)
        pltpu.make_async_copy(told_ref, pass_ref, sems.at[0]).start()

    @pl.when(step < steps)
    def _():
        chunk = 32
        row = iota((chunk * 8, tokens), 0).astype(f32).astype(bf16)
        for pair in range(pairs):
            first = step * (2 * pairs) + 2 * pair
            rows = [rows_ref[pl.ds(first + w, 1), :] for w in range(2)]
            for at in range(0, owners, chunk):
                here = [(r - at * 8).astype(f32).astype(bf16) for r in rows]
                parts = []
                for which in range(2):
                    hot = jnp.where(
                        (row == here[which][:, 0:tokens])
                        | (row == here[which][:, tokens : 2 * tokens]),
                        jnp.ones_like(row),
                        jnp.zeros_like(row),
                    )
                    lane = (2 * pair + which) * tokens
                    part = by_rows(hot, hidden_ref[:, lane : lane + tokens])
                    parts.append(part.reshape(chunk, 8, width))
                held_ref[at : at + chunk, pl.ds(pl.multiple_of(first * 8, 16), 16), :] = (
                    jnp.concatenate(parts, axis=1).astype(bf16)
                )

    @pl.when(step >= steps)
    def _():
        count = out_ref.shape[0]
        for k in range(count):
            out_ref[k] = held_ref[(step - steps) * count + k].T

    @pl.when(step == 1)
    def _():
        pltpu.make_async_copy(told_ref, pass_ref, sems.at[0]).wait()
        pltpu.make_async_copy(pass_ref, kept_ref, sems.at[1]).start()

    @pl.when(step == pl.num_programs(0) - 1)
    def _():
        pltpu.make_async_copy(pass_ref, kept_ref, sems.at[1]).wait()


def route(tok, told, hidden, per_tile, blocks):
    width, total = hidden.shape
    owners = told.shape[0]
    tokens = total // blocks
    entries = 2 * tokens // per_tile
    pairs = 4
    steps = blocks // (2 * pairs)
    turn = 32
    return pl.pallas_call(
        functools.partial(route_kernel, per_tile),
        grid_spec=pltpu.PrefetchScalarGridSpec(
            num_scalar_prefetch=1,
            grid=(steps + owners // turn,),
            in_specs=[
                pl.BlockSpec((blocks, 1, entries), lambda s, t: (t[0], 0, told.shape[2] // entries - 1)),
                pl.BlockSpec(
                    (width, 2 * pairs * tokens), lambda s, t: (0, jnp.minimum(s, steps - 1))
                ),
                far,
            ],
            out_specs=[
                pl.BlockSpec(
                    (turn, width, blocks * 8), lambda s, t: (jnp.maximum(s - steps, 0), 0, 0)
                ),
                far,
            ],
            scratch_shapes=[
                pltpu.VMEM((blocks, 2 * tokens), i32),
                pltpu.VMEM((owners, blocks * 8, width), bf16),
                pltpu.VMEM(told.shape, f32),
                pltpu.SemaphoreType.DMA((2,)),
            ],
        ),
        out_shape=(
            jax.ShapeDtypeStruct((owners, width, blocks * 8), bf16),
            jax.ShapeDtypeStruct(told.shape, f32),
        ),
        compiler_params=settings(59),
        name="route",
    )(tok, told, hidden, told)


def place_kernel(per_tile, owner_ref, told_ref, dense_ref, facts_ref):
    sources = told_ref.shape[0]
    lanes = sources * 8
    width = told_ref.shape[2] // 9
    turned = jnp.stack(
        [told_ref[:, 0, k * width : (k + 1) * width] for k in range(8)], axis=1
    ).reshape(lanes, width).T
    codes = jnp.broadcast_to(
        told_ref[:, :, 8 * width :], (sources, 8, width)
    ).reshape(lanes, width).T
    picks = width // 2
    columns = turned[0:picks].astype(i32) - 1
    teacher = turned[picks:]
    target = jnp.exp(teacher)
    panel = dense_ref.shape[0]
    chunk = 128
    place = iota((chunk, lanes), 0)
    for at in range(0, panel, chunk):
        dense = jnp.zeros((chunk, lanes), f32)
        for k in range(picks):
            dense = jnp.where(place == columns[k : k + 1] - at, target[k : k + 1], dense)
        dense_ref[at : at + chunk, :] = dense
    half = codes.shape[0] // 2
    other = jnp.concatenate([codes[half:], codes[:half]], axis=0)
    slot = (iota((1, lanes), 1) // per_tile) % 2
    mine = (owner_ref[0] * 2 + slot).astype(f32)
    partner = jnp.sum(jnp.where(codes == mine, other + 1.0, 0.0), axis=0, keepdims=True)
    mass = jnp.sum(target, axis=0, keepdims=True)
    entropy = jnp.sum(jnp.where(columns >= 0, target * teacher, 0.0), axis=0, keepdims=True)
    facts_ref[...] = jnp.concatenate(
        [partner, mass, entropy, jnp.zeros((5, lanes), f32)], axis=0
    )


def place(owner, told, panel, per_tile):
    sources, _, width = told.shape
    rows = sources * 8
    block = 16
    return pl.pallas_call(
        functools.partial(place_kernel, per_tile),
        grid_spec=pltpu.PrefetchScalarGridSpec(
            num_scalar_prefetch=1,
            grid=(sources // block,),
            in_specs=[pl.BlockSpec((block, 1, width), lambda s, o: (s, 0, 0))],
            out_specs=[
                pl.BlockSpec((panel, block * 8), lambda s, o: (0, s)),
                pl.BlockSpec((8, block * 8), lambda s, o: (0, s)),
            ],
        ),
        out_shape=(
            jax.ShapeDtypeStruct((panel, rows), f32),
            jax.ShapeDtypeStruct((8, rows), f32),
        ),
        compiler_params=settings(59),
        cost_estimate=pl.CostEstimate(
            flops=2 * 64 * panel * rows, bytes_accessed=8 * panel * rows, transcendentals=64 * rows
        ),
        name="place",
    )(owner, told)


def score_kernel(
    bounds, head_ref, rows_ref, dense_ref, facts_ref, part_ref, own_ref, told_ref,
    total_ref, head_held, rows_held, dense_held, part_held, sems, last_sem, out_sems
):
    groups, _, lanes = rows_ref.shape
    panel, count = total_ref.shape
    copies = []
    for k, (low, high) in enumerate(bounds):
        copies.append(
            (
                pltpu.make_async_copy(
                    head_ref.at[:, low:high], head_held.at[:, low:high], sems.at[0, k]
                ),
                pltpu.make_async_copy(
                    rows_ref.at[:, low:high, :], rows_held.at[:, low:high, :], sems.at[1, k]
                ),
            )
        )
    last = pltpu.make_async_copy(dense_ref, dense_held, last_sem)
    ahead = 4
    for pair in copies[:ahead]:
        pair[0].start()
        pair[1].start()
    for k, (low, high) in enumerate(bounds):
        if k + ahead < len(bounds):
            copies[k + ahead][0].start()
            copies[k + ahead][1].start()
        if k + ahead == len(bounds):
            last.start()
        copies[k][0].wait()
        copies[k][1].wait()
        for t in range(groups):
            here = slice(t * lanes, (t + 1) * lanes)
            product = plain(head_held[:, low:high], rows_held[t, low:high, :])
            total_ref[:, here] = product if k == 0 else total_ref[:, here] + product
    last.wait()
    chunk = 128
    logs, largest, shares, leave = [], [], [], []
    for k, at in enumerate(range(0, count, chunk)):
        here = slice(at, at + chunk)
        dense = dense_held[:, here]
        score = total_ref[:, here]
        named = dense > 0.0
        most = jnp.max(jnp.where(named, score, nothing), axis=0, keepdims=True)
        part = jnp.where(named, jnp.exp(score - most), 0.0)
        part_held[:, here] = part
        leave.append(
            pltpu.make_async_copy(part_held.at[:, here], part_ref.at[:, here], out_sems.at[k])
        )
        leave[-1].start()
        whole = jnp.sum(part, axis=0, keepdims=True)
        log = jnp.where(whole > 0.0, most + jnp.log(jnp.maximum(whole, 1.0)), nothing)
        shares.append(
            facts_ref[2:3, here] - jnp.sum(dense * (score - log), axis=0, keepdims=True)
        )
        logs.append(log)
        largest.append(most)
    logs = jnp.concatenate(logs, axis=1)
    largest = jnp.concatenate(largest, axis=1)
    own_ref[...] = jnp.concatenate([largest, logs, jnp.zeros((6, count), f32)], axis=0)
    owners = told_ref.shape[0]
    told_ref[:, 0, 0:count] = jnp.broadcast_to(logs, (owners, count))
    group = chunk // 8
    home = iota((group, chunk), 1) // 8 == iota((group, chunk), 0)
    which = (iota((chunk, chunk), 0) % 8 == iota((chunk, chunk), 1)).astype(f32)
    spread = [jnp.where(home, jnp.broadcast_to(share, (group, chunk)), 0.0) for share in shares]
    told_ref[:, 0, count : count + chunk] = plain(
        jnp.concatenate(spread, axis=0), which, HIGHEST
    )
    for copy in leave:
        copy.wait()


def score(head, rows, dense, facts, owners):
    panel, width = head.shape
    groups, _, lanes = rows.shape
    count = groups * lanes
    block = 1024
    cuts = [0, 512, 1280, 2560, 3840, 5120]
    bounds = list(zip(cuts[:-1], cuts[1:]))
    return pl.pallas_call(
        functools.partial(score_kernel, bounds),
        in_specs=[far, far, far, near],
        out_specs=[far, near, near],
        out_shape=(
            jax.ShapeDtypeStruct((panel, count), f32),
            jax.ShapeDtypeStruct((8, count), f32),
            jax.ShapeDtypeStruct((owners, 1, count + 128), f32),
        ),
        scratch_shapes=[
            pltpu.VMEM((panel, count), f32),
            pltpu.VMEM((panel, width), bf16),
            pltpu.VMEM((groups, width, lanes), bf16),
            pltpu.VMEM((panel, count), f32),
            pltpu.VMEM((panel, count), f32),
            pltpu.SemaphoreType.DMA((2, len(bounds))),
            pltpu.SemaphoreType.DMA,
            pltpu.SemaphoreType.DMA((count // 128,)),
        ],
        compiler_params=settings(59),
        name="score",
    )(head, rows, dense, facts)


def log_sum(a, b):
    most = jnp.maximum(a, b)
    return most + jnp.log(jnp.exp(a - most) + jnp.exp(b - most))


def turn_kernel(part_ref, dense_ref, part_out, dense_out):
    part_out[...] = part_ref[...].T
    dense_out[...] = (loss_weight * dense_ref[...]).T


def turn(part, dense):
    panel, count = part.shape
    block = 256
    columns = pl.BlockSpec((panel, block), lambda s: (0, s))
    rows = pl.BlockSpec((block, panel), lambda s: (s, 0))
    return pl.pallas_call(
        turn_kernel,
        grid=(count // block,),
        in_specs=[columns, columns],
        out_specs=[rows, rows],
        out_shape=[jax.ShapeDtypeStruct((count, panel), f32)] * 2,
        compiler_params=settings(59),
        cost_estimate=pl.CostEstimate(
            flops=4 * panel * count, bytes_accessed=16 * panel * count, transcendentals=0
        ),
        name="turn",
    )(part, dense)


def part_kernel(
    per_tile, logs_ref, facts_ref, own_ref, part_ref, dense_ref, head_ref, out_ref, weight_ref, kept_ref,
    logs_held, facts_held, own_held, part_held, dense_held, head_held, out_held,
    small_sems, kept_sem, sems, head_sems, out_sems
):
    count, panel = part_ref.shape
    owners = logs_ref.shape[0]
    chunk = 128
    small = [
        pltpu.make_async_copy(facts_ref, facts_held, small_sems.at[0]),
        pltpu.make_async_copy(own_ref, own_held, small_sems.at[1]),
        pltpu.make_async_copy(logs_ref, logs_held, small_sems.at[2]),
    ]
    for copy in small:
        copy.start()
    slots, _, block = out_held.shape
    blocks = out_ref.shape[1] // block
    tables, heads = [], []
    for k in range(count // chunk):
        here = slice(k * chunk, (k + 1) * chunk)
        tables.append(
            (
                pltpu.make_async_copy(part_ref.at[here], part_held.at[here], sems.at[0, k]),
                pltpu.make_async_copy(dense_ref.at[here], dense_held.at[here], sems.at[1, k]),
            )
        )
        tables[-1][0].start()
        tables[-1][1].start(priority=1)
    for k in range(blocks):
        here = slice(k * block, (k + 1) * block)
        heads.append(
            pltpu.make_async_copy(head_ref.at[:, here], head_held.at[:, here], head_sems.at[k])
        )
    for copy in small:
        copy.wait()
    keep = pltpu.make_async_copy(logs_held, kept_ref, kept_sem)
    keep.start(priority=1)
    for k, at in enumerate(range(0, count, chunk)):
        here = slice(at, at + chunk)
        logs = logs_held[:, 0, here]
        partner = facts_held[0:1, here].astype(i32) - 1
        slot = (iota((1, chunk), 1) // per_tile) % 2
        across = jnp.where(
            slot == 0, pltpu.roll(logs, chunk - per_tile, 1), pltpu.roll(logs, per_tile, 1)
        )
        picked = jnp.where(
            iota((owners, chunk), 0) == partner // 2,
            jnp.where(partner % 2 == slot, logs, across),
            0.0,
        )
        other = jnp.sum(picked, axis=0, keepdims=True)
        total = log_sum(own_held[1:2, here], other)
        scale = loss_weight * facts_held[1:2, here] * jnp.exp(own_held[0:1, here] - total)
        scale = jnp.broadcast_to(scale, (chunk, chunk)).T
        tables[k][0].wait()
        tables[k][1].wait()
        if k == 0:
            for copy in heads[:2]:
                copy.start()
        for col in range(0, panel, chunk):
            there = slice(col, col + chunk)
            weight = part_held[here, there] * scale - dense_held[here, there]
            weight_ref[here, there] = weight.astype(bf16)
    leave = []
    for k in range(blocks):
        here = slice(k * block, (k + 1) * block)
        if k >= slots:
            leave[k - slots].wait()
        if k + 2 < blocks:
            heads[k + 2].start()
        heads[k].wait()
        out_held[k % slots] = plain(weight_ref[...], head_held[:, here]).astype(bf16)
        leave.append(
            pltpu.make_async_copy(out_held.at[k % slots], out_ref.at[:, here], out_sems.at[k % slots])
        )
        leave[-1].start(priority=1)
    for copy in leave[blocks - slots :]:
        copy.wait()
    keep.wait()


def grad_parts(logs, facts, own, part, dense, head, per_tile):
    panel, width = head.shape
    count = part.shape[0]
    block = 1024
    return pl.pallas_call(
        functools.partial(part_kernel, per_tile),
        in_specs=[far] * 6,
        out_specs=[far, near, far],
        out_shape=(
            jax.ShapeDtypeStruct((count, width), bf16),
            jax.ShapeDtypeStruct((count, panel), bf16),
            jax.ShapeDtypeStruct(logs.shape, f32),
        ),
        scratch_shapes=[
            pltpu.VMEM(logs.shape, f32),
            pltpu.VMEM(facts.shape, f32),
            pltpu.VMEM(own.shape, f32),
            pltpu.VMEM((count, panel), f32),
            pltpu.VMEM((count, panel), f32),
            pltpu.VMEM((panel, width), bf16),
            pltpu.VMEM((2, count, block), bf16),
            pltpu.SemaphoreType.DMA((3,)),
            pltpu.SemaphoreType.DMA,
            pltpu.SemaphoreType.DMA((2, count // 128)),
            pltpu.SemaphoreType.DMA((width // block,)),
            pltpu.SemaphoreType.DMA((2,)),
        ],
        compiler_params=settings(59),
        name="grad_parts",
    )(logs, facts, own, part, dense, head)


def head_kernel(weight_ref, rows_ref, out_ref, turned_ref):
    groups, _, lanes = rows_ref.shape

    @pl.when(pl.program_id(0) == 0)
    def _():
        for at in range(0, weight_ref.shape[0], 128):
            turned_ref[:, at : at + 128] = weight_ref[at : at + 128, :].T

    total = by_rows(turned_ref[:, 0:lanes], rows_ref[0])
    for t in range(1, groups):
        total = total + by_rows(turned_ref[:, t * lanes : (t + 1) * lanes], rows_ref[t])
    out_ref[...] = total.astype(bf16)


def grad_of_head(weight, rows):
    count, panel = weight.shape
    groups, width, lanes = rows.shape
    block = 512
    return pl.pallas_call(
        head_kernel,
        grid=(width // block,),
        in_specs=[
            pl.BlockSpec((count, panel), lambda s: (0, 0)),
            pl.BlockSpec((groups, block, lanes), lambda s: (0, s, 0)),
        ],
        out_specs=pl.BlockSpec((panel, block), lambda s: (0, s)),
        out_shape=jax.ShapeDtypeStruct((panel, width), bf16),
        scratch_shapes=[pltpu.VMEM((panel, count), bf16)],
        compiler_params=settings(),
        cost_estimate=pl.CostEstimate(
            flops=2 * panel * count * width,
            bytes_accessed=2 * (panel + count) * width,
            transcendentals=0,
        ),
        name="grad_of_head",
    )(weight, rows)


def loss_kernel(panel, me_ref, logs_ref, rows_ref, cand_ref, teacher_ref, loss_ref, table_ref):
    owners = logs_ref.shape[0]
    tokens = teacher_ref.shape[1]
    count = table_ref.shape[1]
    mine = iota((count, 128), 0) == me_ref[0] * 8 + iota((count, 128), 1)
    mine = jnp.where(mine & (iota((count, 128), 1) < 8), 1.0, 0.0)
    logs = plain(logs_ref[:, 0, 0:count], mine, HIGHEST).T
    shares = logs_ref[:, 0, count : count + 128].T
    found = []
    total = jnp.zeros((1, tokens), f32)
    for group in range(2):
        row = rows_ref[0:1, group * tokens : (group + 1) * tokens]
        owner = jnp.where(iota((owners, tokens), 0) == row // 8, 1.0, 0.0)
        slot = iota((128, tokens), 0) == row % 8
        for table, kept in ((logs, True), (shares, False)):
            got = jnp.where(slot, plain(table, owner, HIGHEST), 0.0)
            got = jnp.sum(got, axis=0, keepdims=True)
            if kept:
                found.append(got)
            else:
                total = total + got
    target = jnp.exp(teacher_ref[...])
    whole = log_sum(found[0], found[1])
    first = cand_ref[...] < panel
    for group in range(2):
        named = first if group == 0 else ~first
        mass = jnp.sum(jnp.where(named, target, 0.0), axis=0, keepdims=True)
        total = total + mass * (whole - found[group])
    loss_ref[...] = total
    first, second = rows_ref[0:1, 0:tokens], rows_ref[0:1, tokens : 2 * tokens]
    for at in range(0, count, 128):
        row = iota((128, tokens), 0) + at
        hot = jnp.where((row == first) | (row == second), 1.0, 0.0)
        table_ref[:, at : at + 128] = hot.T.astype(bf16)


def losses(me, logs, rows, cand, teacher, panel, count):
    tokens = teacher.shape[1]
    return pl.pallas_call(
        functools.partial(loss_kernel, panel),
        in_specs=[pl.BlockSpec(memory_space=pltpu.SMEM), near, near, near, near],
        out_shape=(
            jax.ShapeDtypeStruct((1, tokens), f32),
            jax.ShapeDtypeStruct((tokens, count), bf16),
        ),
        compiler_params=settings(59),
        cost_estimate=pl.CostEstimate(
            flops=12 * 2 * count * tokens * 128, bytes_accessed=4 * count * tokens, transcendentals=0
        ),
        name="losses",
    )(me, logs, rows, cand, teacher)


def combine_kernel(table_ref, parts_ref, out_ref):
    out_ref[...] = plain(table_ref[...], parts_ref[...]).astype(bf16)


def combine(table, parts):
    tokens, count = table.shape
    width = parts.shape[1]
    block = width // 2
    return pl.pallas_call(
        combine_kernel,
        grid=(width // block,),
        in_specs=[
            pl.BlockSpec((tokens, count), lambda s: (0, 0)),
            pl.BlockSpec((count, block), lambda s: (0, s)),
        ],
        out_specs=pl.BlockSpec((tokens, block), lambda s: (0, s)),
        out_shape=jax.ShapeDtypeStruct((tokens, width), bf16),
        compiler_params=settings(59),
        name="combine",
    )(table, parts)


def exchange(values):
    return lax.all_to_all(values, ("tok", "voc"), split_axis=0, concat_axis=0, tiled=True)


def body(hidden, head_weight, tile_owners, cand_pos, teacher_logp):
    panel, width = head_weight.shape
    tiles = tile_owners.shape[0]
    tokens = cand_pos.shape[0]
    per_tile = tokens // tiles
    tok_size, blocks = lax.axis_size("tok"), lax.axis_size("voc")
    owners = tok_size * blocks
    count = owners * 8
    tok = lax.axis_index("tok")
    me = (tok * blocks + lax.axis_index("voc")).astype(i32).reshape(1)
    teacher = teacher_logp.T
    told, home_rows = announce(tile_owners.T, cand_pos.T, teacher, panel, per_tile, owners)
    told = exchange(told)
    sent, told = route(tok.astype(i32).reshape(1), told, hidden.T, per_tile, blocks)
    rows = exchange(sent).reshape(tok_size, width, blocks * 8)
    dense, facts = place(me, told, panel, per_tile)
    part, own, logs = score(head_weight, rows, dense, facts, owners)
    logs = exchange(logs)
    part_rows, dense_rows = turn(part, dense)
    parts, weight, logs = grad_parts(logs, facts, own, part_rows, dense_rows, head_weight, per_tile)
    home_parts = exchange(parts.reshape(owners, 8, width)).reshape(count, width)
    grad_head = grad_of_head(weight, rows)
    loss, table = losses(me, logs, home_rows, cand_pos.T, teacher, panel, count)
    grad_hidden = combine(table, home_parts)
    return (loss.reshape(tokens), grad_hidden, grad_head)


def solution(mesh):
    placed = (
        P("tok", "voc"),
        P(("tok", "voc"), None),
        P(("tok", "voc"), None),
        P(("tok", "voc"), None),
        P(("tok", "voc"), None),
    )
    return jax.shard_map(
        body,
        mesh=mesh,
        in_specs=placed,
        out_specs=(P(("tok", "voc")), P(("tok", "voc"), None), P(("tok", "voc"), None)),
        check_vma=False,
    )
```

```python
import functools

import jax
import jax.numpy as jnp
from jax import lax
from jax.experimental import pallas as pl
from jax.experimental.pallas import tpu as pltpu
from jax.sharding import PartitionSpec as P

loss_weight = 16.0
nothing = -1e30
f32, bf16, i32 = jnp.float32, jnp.bfloat16, jnp.int32
HIGHEST = lax.Precision.HIGHEST


near, far = pl.BlockSpec(memory_space=pltpu.VMEM), pl.BlockSpec(memory_space=pl.ANY)


def settings(mib=32):
    return pltpu.CompilerParams(vmem_limit_bytes=mib * 1024 * 1024)


def by_rows(a, b, precision=None):
    return lax.dot_general(
        a, b, (((1,), (1,)), ((), ())), preferred_element_type=f32, precision=precision
    )


def plain(a, b, precision=None):
    return lax.dot_general(
        a, b, (((1,), (0,)), ((), ())), preferred_element_type=f32, precision=precision
    )


def iota(shape, dim):
    return lax.broadcasted_iota(i32, shape, dim)


def rows_of(codes, per_tile):
    entries = codes.shape[1]
    wide = entries * per_tile
    spread = (iota((entries, wide), 0) == iota((entries, wide), 1) // per_tile).astype(bf16)
    expanded = plain(codes.astype(bf16), spread).astype(i32)
    return expanded * per_tile + iota(expanded.shape, 1) % per_tile


def announce_kernel(panel, per_tile, owner_ref, cand_ref, teacher_ref, out_ref, rows_ref):
    tiles = owner_ref.shape[1]
    entries = 2 * tiles
    tokens = tiles * per_tile
    slots = out_ref.shape[0]
    owner = jnp.concatenate([owner_ref[0:1, :], owner_ref[1:2, :]], axis=1).astype(f32)
    owners = jnp.broadcast_to(owner, (entries, entries))
    earlier = iota((entries, entries), 0) % tiles < iota((entries, entries), 1) % tiles
    same = (owners == owners.T) & earlier
    rank = jnp.sum(jnp.where(same, 1.0, 0.0), axis=0, keepdims=True)
    code = owner * 2.0 + rank
    rows = rows_of(jnp.broadcast_to(code, (8, entries)), per_tile)
    rows_ref[...] = rows
    cand = cand_ref[...]
    first = teacher_ref[...].astype(bf16)
    rest = teacher_ref[...] - first.astype(f32)
    second = rest.astype(bf16)
    third = (rest - second.astype(f32)).astype(bf16)
    sides = []
    for column in (
        jnp.where(cand < panel, cand + 1, 0),
        jnp.where(cand >= panel, cand - panel + 1, 0),
    ):
        high, low = column // 32, column % 32
        sides.append(
            jnp.concatenate(
                [
                    high.astype(f32).astype(bf16),
                    first,
                    low.astype(f32).astype(bf16),
                    second,
                    jnp.zeros_like(first),
                    third,
                ],
                axis=0,
            )
        )
    sides = jnp.concatenate(sides, axis=1)
    width = 2 * cand.shape[0]
    times = jnp.where(iota((slots, width), 1) < cand.shape[0], 32.0, 1.0)
    for which in range(8):
        row = iota((slots, 2 * tokens), 0) * 8 + which
        hot = jnp.where(row == rows[0:1, :], 1.0, 0.0).astype(bf16)
        told = by_rows(hot, sides)
        out_ref[:, 0, which * width : (which + 1) * width] = (
            told[:, 0:width] * times + told[:, width : 2 * width] + told[:, 2 * width :]
        )
    out_ref[:, 0, 8 * width : 8 * width + entries] = jnp.broadcast_to(code, (slots, entries))


def announce(tile_owners, cand, teacher, panel, per_tile, owners):
    entries = 2 * tile_owners.shape[1]
    return pl.pallas_call(
        functools.partial(announce_kernel, panel, per_tile),
        out_shape=(
            jax.ShapeDtypeStruct((owners, 1, 16 * cand.shape[0] + entries), f32),
            jax.ShapeDtypeStruct((8, entries * per_tile), i32),
        ),
        compiler_params=settings(59),
        name="announce",
    )(tile_owners, cand, teacher)


def route_kernel(
    per_tile, tok_ref, codes_ref, hidden_ref, told_ref, out_ref, kept_ref, rows_ref, held_ref, pass_ref, sems
):
    step = pl.program_id(0)
    width = hidden_ref.shape[0]
    owners, lanes, _ = held_ref.shape
    blocks = lanes // 8
    tokens = rows_ref.shape[1] // 2
    pairs = hidden_ref.shape[1] // (2 * tokens)
    steps = blocks // (2 * pairs)

    @pl.when(step == 0)
    def _():
        rows_ref[...] = rows_of(codes_ref[:, 0, :], per_tile)
        pltpu.make_async_copy(told_ref, pass_ref, sems.at[0]).start()

    @pl.when(step < steps)
    def _():
        chunk = 32
        row = iota((chunk * 8, tokens), 0).astype(f32).astype(bf16)
        for pair in range(pairs):
            first = step * (2 * pairs) + 2 * pair
            rows = [rows_ref[pl.ds(first + w, 1), :] for w in range(2)]
            for at in range(0, owners, chunk):
                here = [(r - at * 8).astype(f32).astype(bf16) for r in rows]
                parts = []
                for which in range(2):
                    hot = jnp.where(
                        (row == here[which][:, 0:tokens])
                        | (row == here[which][:, tokens : 2 * tokens]),
                        jnp.ones_like(row),
                        jnp.zeros_like(row),
                    )
                    lane = (2 * pair + which) * tokens
                    part = by_rows(hot, hidden_ref[:, lane : lane + tokens])
                    parts.append(part.reshape(chunk, 8, width))
                held_ref[at : at + chunk, pl.ds(pl.multiple_of(first * 8, 16), 16), :] = (
                    jnp.concatenate(parts, axis=1).astype(bf16)
                )

    @pl.when(step >= steps)
    def _():
        count = out_ref.shape[0]
        for k in range(count):
            out_ref[k] = held_ref[(step - steps) * count + k].T

    @pl.when(step == 1)
    def _():
        pltpu.make_async_copy(told_ref, pass_ref, sems.at[0]).wait()
        pltpu.make_async_copy(pass_ref, kept_ref, sems.at[1]).start()

    @pl.when(step == pl.num_programs(0) - 1)
    def _():
        pltpu.make_async_copy(pass_ref, kept_ref, sems.at[1]).wait()


def route(tok, told, hidden, per_tile, blocks):
    width, total = hidden.shape
    owners = told.shape[0]
    tokens = total // blocks
    entries = 2 * tokens // per_tile
    pairs = 8
    steps = blocks // (2 * pairs)
    turn = 32
    return pl.pallas_call(
        functools.partial(route_kernel, per_tile),
        grid_spec=pltpu.PrefetchScalarGridSpec(
            num_scalar_prefetch=1,
            grid=(steps + owners // turn,),
            in_specs=[
                pl.BlockSpec((blocks, 1, entries), lambda s, t: (t[0], 0, told.shape[2] // entries - 1)),
                pl.BlockSpec(
                    (width, 2 * pairs * tokens), lambda s, t: (0, jnp.minimum(s, steps - 1))
                ),
                far,
            ],
            out_specs=[
                pl.BlockSpec(
                    (turn, width, blocks * 8), lambda s, t: (jnp.maximum(s - steps, 0), 0, 0)
                ),
                far,
            ],
            scratch_shapes=[
                pltpu.VMEM((blocks, 2 * tokens), i32),
                pltpu.VMEM((owners, blocks * 8, width), bf16),
                pltpu.VMEM(told.shape, f32),
                pltpu.SemaphoreType.DMA((2,)),
            ],
        ),
        out_shape=(
            jax.ShapeDtypeStruct((owners, width, blocks * 8), bf16),
            jax.ShapeDtypeStruct(told.shape, f32),
        ),
        compiler_params=settings(59),
        name="route",
    )(tok, told, hidden, told)


def place_kernel(per_tile, owner_ref, told_ref, dense_ref, facts_ref):
    sources = told_ref.shape[0]
    lanes = sources * 8
    width = told_ref.shape[2] // 9
    turned = jnp.stack(
        [told_ref[:, 0, k * width : (k + 1) * width] for k in range(8)], axis=1
    ).reshape(lanes, width).T
    codes = jnp.broadcast_to(
        told_ref[:, :, 8 * width :], (sources, 8, width)
    ).reshape(lanes, width).T
    picks = width // 2
    columns = turned[0:picks].astype(i32) - 1
    teacher = turned[picks:]
    target = jnp.exp(teacher)
    panel = dense_ref.shape[0]
    chunk = 128
    place = iota((chunk, lanes), 0)
    for at in range(0, panel, chunk):
        dense = jnp.zeros((chunk, lanes), f32)
        for k in range(picks):
            dense = jnp.where(place == columns[k : k + 1] - at, target[k : k + 1], dense)
        dense_ref[at : at + chunk, :] = dense
    half = codes.shape[0] // 2
    other = jnp.concatenate([codes[half:], codes[:half]], axis=0)
    slot = (iota((1, lanes), 1) // per_tile) % 2
    mine = (owner_ref[0] * 2 + slot).astype(f32)
    partner = jnp.sum(jnp.where(codes == mine, other + 1.0, 0.0), axis=0, keepdims=True)
    mass = jnp.sum(target, axis=0, keepdims=True)
    entropy = jnp.sum(jnp.where(columns >= 0, target * teacher, 0.0), axis=0, keepdims=True)
    facts_ref[...] = jnp.concatenate(
        [partner, mass, entropy, jnp.zeros((5, lanes), f32)], axis=0
    )


def place(owner, told, panel, per_tile):
    sources, _, width = told.shape
    rows = sources * 8
    block = 16
    return pl.pallas_call(
        functools.partial(place_kernel, per_tile),
        grid_spec=pltpu.PrefetchScalarGridSpec(
            num_scalar_prefetch=1,
            grid=(sources // block,),
            in_specs=[pl.BlockSpec((block, 1, width), lambda s, o: (s, 0, 0))],
            out_specs=[
                pl.BlockSpec((panel, block * 8), lambda s, o: (0, s)),
                pl.BlockSpec((8, block * 8), lambda s, o: (0, s)),
            ],
        ),
        out_shape=(
            jax.ShapeDtypeStruct((panel, rows), f32),
            jax.ShapeDtypeStruct((8, rows), f32),
        ),
        compiler_params=settings(59),
        cost_estimate=pl.CostEstimate(
            flops=2 * 64 * panel * rows, bytes_accessed=8 * panel * rows, transcendentals=64 * rows
        ),
        name="place",
    )(owner, told)


def score_kernel(
    bounds, head_ref, rows_ref, dense_ref, facts_ref, part_ref, own_ref, told_ref,
    total_ref, head_held, rows_held, dense_held, part_held, sems, last_sem, out_sems
):
    groups, _, lanes = rows_ref.shape
    panel, count = total_ref.shape
    copies = []
    for k, (low, high) in enumerate(bounds):
        copies.append(
            (
                pltpu.make_async_copy(
                    head_ref.at[:, low:high], head_held.at[:, low:high], sems.at[0, k]
                ),
                pltpu.make_async_copy(
                    rows_ref.at[:, low:high, :], rows_held.at[:, low:high, :], sems.at[1, k]
                ),
            )
        )
    last = pltpu.make_async_copy(dense_ref, dense_held, last_sem)
    ahead = 4
    for pair in copies[:ahead]:
        pair[0].start()
        pair[1].start()
    for k, (low, high) in enumerate(bounds):
        if k + ahead < len(bounds):
            copies[k + ahead][0].start()
            copies[k + ahead][1].start()
        if k + ahead == len(bounds):
            last.start()
        copies[k][0].wait()
        copies[k][1].wait()
        for t in range(groups):
            here = slice(t * lanes, (t + 1) * lanes)
            product = plain(head_held[:, low:high], rows_held[t, low:high, :])
            total_ref[:, here] = product if k == 0 else total_ref[:, here] + product
    last.wait()
    chunk = 128
    logs, largest, shares, leave = [], [], [], []
    for k, at in enumerate(range(0, count, chunk)):
        here = slice(at, at + chunk)
        dense = dense_held[:, here]
        score = total_ref[:, here]
        named = dense > 0.0
        most = jnp.max(jnp.where(named, score, nothing), axis=0, keepdims=True)
        part = jnp.where(named, jnp.exp(score - most), 0.0)
        part_held[:, here] = part
        leave.append(
            pltpu.make_async_copy(part_held.at[:, here], part_ref.at[:, here], out_sems.at[k])
        )
        leave[-1].start()
        whole = jnp.sum(part, axis=0, keepdims=True)
        log = jnp.where(whole > 0.0, most + jnp.log(jnp.maximum(whole, 1.0)), nothing)
        shares.append(
            facts_ref[2:3, here] - jnp.sum(dense * (score - log), axis=0, keepdims=True)
        )
        logs.append(log)
        largest.append(most)
    logs = jnp.concatenate(logs, axis=1)
    largest = jnp.concatenate(largest, axis=1)
    own_ref[...] = jnp.concatenate([largest, logs, jnp.zeros((6, count), f32)], axis=0)
    owners = told_ref.shape[0]
    told_ref[:, 0, 0:count] = jnp.broadcast_to(logs, (owners, count))
    group = chunk // 8
    home = iota((group, chunk), 1) // 8 == iota((group, chunk), 0)
    which = (iota((chunk, chunk), 0) % 8 == iota((chunk, chunk), 1)).astype(f32)
    spread = [jnp.where(home, jnp.broadcast_to(share, (group, chunk)), 0.0) for share in shares]
    told_ref[:, 0, count : count + chunk] = plain(
        jnp.concatenate(spread, axis=0), which, HIGHEST
    )
    for copy in leave:
        copy.wait()


def score(head, rows, dense, facts, owners):
    panel, width = head.shape
    groups, _, lanes = rows.shape
    count = groups * lanes
    block = 1024
    cuts = [0, 512, 1280, 2560, 3840, 5120]
    bounds = list(zip(cuts[:-1], cuts[1:]))
    return pl.pallas_call(
        functools.partial(score_kernel, bounds),
        in_specs=[far, far, far, near],
        out_specs=[far, near, near],
        out_shape=(
            jax.ShapeDtypeStruct((panel, count), f32),
            jax.ShapeDtypeStruct((8, count), f32),
            jax.ShapeDtypeStruct((owners, 1, count + 128), f32),
        ),
        scratch_shapes=[
            pltpu.VMEM((panel, count), f32),
            pltpu.VMEM((panel, width), bf16),
            pltpu.VMEM((groups, width, lanes), bf16),
            pltpu.VMEM((panel, count), f32),
            pltpu.VMEM((panel, count), f32),
            pltpu.SemaphoreType.DMA((2, len(bounds))),
            pltpu.SemaphoreType.DMA,
            pltpu.SemaphoreType.DMA((count // 128,)),
        ],
        compiler_params=settings(59),
        name="score",
    )(head, rows, dense, facts)


def log_sum(a, b):
    most = jnp.maximum(a, b)
    return most + jnp.log(jnp.exp(a - most) + jnp.exp(b - most))


def turn_kernel(part_ref, dense_ref, part_out, dense_out):
    part_out[...] = part_ref[...].T
    dense_out[...] = (loss_weight * dense_ref[...]).T


def turn(part, dense):
    panel, count = part.shape
    block = 256
    columns = pl.BlockSpec((panel, block), lambda s: (0, s))
    rows = pl.BlockSpec((block, panel), lambda s: (s, 0))
    return pl.pallas_call(
        turn_kernel,
        grid=(count // block,),
        in_specs=[columns, columns],
        out_specs=[rows, rows],
        out_shape=[jax.ShapeDtypeStruct((count, panel), f32)] * 2,
        compiler_params=settings(59),
        cost_estimate=pl.CostEstimate(
            flops=4 * panel * count, bytes_accessed=16 * panel * count, transcendentals=0
        ),
        name="turn",
    )(part, dense)


def part_kernel(
    per_tile, logs_ref, facts_ref, own_ref, part_ref, dense_ref, head_ref, out_ref, weight_ref, kept_ref,
    logs_held, facts_held, own_held, part_held, dense_held, head_held, out_held,
    small_sems, kept_sem, sems, head_sems, out_sems
):
    count, panel = part_ref.shape
    owners = logs_ref.shape[0]
    chunk = 128
    small = [
        pltpu.make_async_copy(facts_ref, facts_held, small_sems.at[0]),
        pltpu.make_async_copy(own_ref, own_held, small_sems.at[1]),
        pltpu.make_async_copy(logs_ref, logs_held, small_sems.at[2]),
    ]
    for copy in small:
        copy.start()
    slots, _, block = out_held.shape
    blocks = out_ref.shape[1] // block
    tables, heads = [], []
    for k in range(count // chunk):
        here = slice(k * chunk, (k + 1) * chunk)
        tables.append(
            (
                pltpu.make_async_copy(part_ref.at[here], part_held.at[here], sems.at[0, k]),
                pltpu.make_async_copy(dense_ref.at[here], dense_held.at[here], sems.at[1, k]),
            )
        )
        tables[-1][0].start()
        tables[-1][1].start(priority=1)
    for k in range(blocks):
        here = slice(k * block, (k + 1) * block)
        heads.append(
            pltpu.make_async_copy(head_ref.at[:, here], head_held.at[:, here], head_sems.at[k])
        )
    for copy in small:
        copy.wait()
    keep = pltpu.make_async_copy(logs_held, kept_ref, kept_sem)
    keep.start(priority=1)
    for k, at in enumerate(range(0, count, chunk)):
        here = slice(at, at + chunk)
        logs = logs_held[:, 0, here]
        partner = facts_held[0:1, here].astype(i32) - 1
        slot = (iota((1, chunk), 1) // per_tile) % 2
        across = jnp.where(
            slot == 0, pltpu.roll(logs, chunk - per_tile, 1), pltpu.roll(logs, per_tile, 1)
        )
        picked = jnp.where(
            iota((owners, chunk), 0) == partner // 2,
            jnp.where(partner % 2 == slot, logs, across),
            0.0,
        )
        other = jnp.sum(picked, axis=0, keepdims=True)
        total = log_sum(own_held[1:2, here], other)
        scale = loss_weight * facts_held[1:2, here] * jnp.exp(own_held[0:1, here] - total)
        scale = jnp.broadcast_to(scale, (chunk, chunk)).T
        tables[k][0].wait()
        tables[k][1].wait()
        if k == 0:
            for copy in heads[:2]:
                copy.start()
        for col in range(0, panel, chunk):
            there = slice(col, col + chunk)
            weight = part_held[here, there] * scale - dense_held[here, there]
            weight_ref[here, there] = weight.astype(bf16)
    leave = []
    for k in range(blocks):
        here = slice(k * block, (k + 1) * block)
        if k >= slots:
            leave[k - slots].wait()
        if k + 2 < blocks:
            heads[k + 2].start()
        heads[k].wait()
        out_held[k % slots] = plain(weight_ref[...], head_held[:, here]).astype(bf16)
        leave.append(
            pltpu.make_async_copy(out_held.at[k % slots], out_ref.at[:, here], out_sems.at[k % slots])
        )
        leave[-1].start(priority=1)
    for copy in leave[blocks - slots :]:
        copy.wait()
    keep.wait()


def grad_parts(logs, facts, own, part, dense, head, per_tile):
    panel, width = head.shape
    count = part.shape[0]
    block = 1024
    return pl.pallas_call(
        functools.partial(part_kernel, per_tile),
        in_specs=[far] * 6,
        out_specs=[far, near, far],
        out_shape=(
            jax.ShapeDtypeStruct((count, width), bf16),
            jax.ShapeDtypeStruct((count, panel), bf16),
            jax.ShapeDtypeStruct(logs.shape, f32),
        ),
        scratch_shapes=[
            pltpu.VMEM(logs.shape, f32),
            pltpu.VMEM(facts.shape, f32),
            pltpu.VMEM(own.shape, f32),
            pltpu.VMEM((count, panel), f32),
            pltpu.VMEM((count, panel), f32),
            pltpu.VMEM((panel, width), bf16),
            pltpu.VMEM((2, count, block), bf16),
            pltpu.SemaphoreType.DMA((3,)),
            pltpu.SemaphoreType.DMA,
            pltpu.SemaphoreType.DMA((2, count // 128)),
            pltpu.SemaphoreType.DMA((width // block,)),
            pltpu.SemaphoreType.DMA((2,)),
        ],
        compiler_params=settings(59),
        name="grad_parts",
    )(logs, facts, own, part, dense, head)


def head_kernel(weight_ref, rows_ref, out_ref, turned_ref):
    groups, _, lanes = rows_ref.shape

    @pl.when(pl.program_id(0) == 0)
    def _():
        for at in range(0, weight_ref.shape[0], 128):
            turned_ref[:, at : at + 128] = weight_ref[at : at + 128, :].T

    total = by_rows(turned_ref[:, 0:lanes], rows_ref[0])
    for t in range(1, groups):
        total = total + by_rows(turned_ref[:, t * lanes : (t + 1) * lanes], rows_ref[t])
    out_ref[...] = total.astype(bf16)


def grad_of_head(weight, rows):
    count, panel = weight.shape
    groups, width, lanes = rows.shape
    block = 512
    return pl.pallas_call(
        head_kernel,
        grid=(width // block,),
        in_specs=[
            pl.BlockSpec((count, panel), lambda s: (0, 0)),
            pl.BlockSpec((groups, block, lanes), lambda s: (0, s, 0)),
        ],
        out_specs=pl.BlockSpec((panel, block), lambda s: (0, s)),
        out_shape=jax.ShapeDtypeStruct((panel, width), bf16),
        scratch_shapes=[pltpu.VMEM((panel, count), bf16)],
        compiler_params=settings(),
        cost_estimate=pl.CostEstimate(
            flops=2 * panel * count * width,
            bytes_accessed=2 * (panel + count) * width,
            transcendentals=0,
        ),
        name="grad_of_head",
    )(weight, rows)


def loss_kernel(panel, me_ref, logs_ref, rows_ref, cand_ref, teacher_ref, loss_ref, table_ref):
    owners = logs_ref.shape[0]
    tokens = teacher_ref.shape[1]
    count = table_ref.shape[1]
    mine = iota((count, 128), 0) == me_ref[0] * 8 + iota((count, 128), 1)
    mine = jnp.where(mine & (iota((count, 128), 1) < 8), 1.0, 0.0)
    logs = plain(logs_ref[:, 0, 0:count], mine, HIGHEST).T
    shares = logs_ref[:, 0, count : count + 128].T
    found = []
    total = jnp.zeros((1, tokens), f32)
    for group in range(2):
        row = rows_ref[0:1, group * tokens : (group + 1) * tokens]
        owner = jnp.where(iota((owners, tokens), 0) == row // 8, 1.0, 0.0)
        slot = iota((128, tokens), 0) == row % 8
        for table, kept in ((logs, True), (shares, False)):
            got = jnp.where(slot, plain(table, owner, HIGHEST), 0.0)
            got = jnp.sum(got, axis=0, keepdims=True)
            if kept:
                found.append(got)
            else:
                total = total + got
    target = jnp.exp(teacher_ref[...])
    whole = log_sum(found[0], found[1])
    first = cand_ref[...] < panel
    for group in range(2):
        named = first if group == 0 else ~first
        mass = jnp.sum(jnp.where(named, target, 0.0), axis=0, keepdims=True)
        total = total + mass * (whole - found[group])
    loss_ref[...] = total
    first, second = rows_ref[0:1, 0:tokens], rows_ref[0:1, tokens : 2 * tokens]
    for at in range(0, count, 128):
        row = iota((128, tokens), 0) + at
        hot = jnp.where((row == first) | (row == second), 1.0, 0.0)
        table_ref[:, at : at + 128] = hot.T.astype(bf16)


def losses(me, logs, rows, cand, teacher, panel, count):
    tokens = teacher.shape[1]
    return pl.pallas_call(
        functools.partial(loss_kernel, panel),
        in_specs=[pl.BlockSpec(memory_space=pltpu.SMEM), near, near, near, near],
        out_shape=(
            jax.ShapeDtypeStruct((1, tokens), f32),
            jax.ShapeDtypeStruct((tokens, count), bf16),
        ),
        compiler_params=settings(59),
        cost_estimate=pl.CostEstimate(
            flops=12 * 2 * count * tokens * 128, bytes_accessed=4 * count * tokens, transcendentals=0
        ),
        name="losses",
    )(me, logs, rows, cand, teacher)


def combine_kernel(table_ref, parts_ref, out_ref):
    out_ref[...] = plain(table_ref[...], parts_ref[...]).astype(bf16)


def combine(table, parts):
    tokens, count = table.shape
    width = parts.shape[1]
    block = width // 2
    return pl.pallas_call(
        combine_kernel,
        grid=(width // block,),
        in_specs=[
            pl.BlockSpec((tokens, count), lambda s: (0, 0)),
            pl.BlockSpec((count, block), lambda s: (0, s)),
        ],
        out_specs=pl.BlockSpec((tokens, block), lambda s: (0, s)),
        out_shape=jax.ShapeDtypeStruct((tokens, width), bf16),
        compiler_params=settings(59),
        name="combine",
    )(table, parts)


def exchange(values):
    return lax.all_to_all(values, ("tok", "voc"), split_axis=0, concat_axis=0, tiled=True)


def body(hidden, head_weight, tile_owners, cand_pos, teacher_logp):
    panel, width = head_weight.shape
    tiles = tile_owners.shape[0]
    tokens = cand_pos.shape[0]
    per_tile = tokens // tiles
    tok_size, blocks = lax.axis_size("tok"), lax.axis_size("voc")
    owners = tok_size * blocks
    count = owners * 8
    tok = lax.axis_index("tok")
    me = (tok * blocks + lax.axis_index("voc")).astype(i32).reshape(1)
    teacher = teacher_logp.T
    told, home_rows = announce(tile_owners.T, cand_pos.T, teacher, panel, per_tile, owners)
    told = exchange(told)
    sent, told = route(tok.astype(i32).reshape(1), told, hidden.T, per_tile, blocks)
    rows = exchange(sent).reshape(tok_size, width, blocks * 8)
    dense, facts = place(me, told, panel, per_tile)
    part, own, logs = score(head_weight, rows, dense, facts, owners)
    logs = exchange(logs)
    part_rows, dense_rows = turn(part, dense)
    parts, weight, logs = grad_parts(logs, facts, own, part_rows, dense_rows, head_weight, per_tile)
    home_parts = exchange(parts.reshape(owners, 8, width)).reshape(count, width)
    grad_head = grad_of_head(weight, rows)
    loss, table = losses(me, logs, home_rows, cand_pos.T, teacher, panel, count)
    grad_hidden = combine(table, home_parts)
    return (loss.reshape(tokens), grad_hidden, grad_head)


def solution(mesh):
    placed = (
        P("tok", "voc"),
        P(("tok", "voc"), None),
        P(("tok", "voc"), None),
        P(("tok", "voc"), None),
        P(("tok", "voc"), None),
    )
    return jax.shard_map(
        body,
        mesh=mesh,
        in_specs=placed,
        out_specs=(P(("tok", "voc")), P(("tok", "voc"), None), P(("tok", "voc"), None)),
        check_vma=False,
    )
```
